32 devices in a mesh: head: 2 (over core), tok: 16 (over z, y, x).
Axes of the slice: x: 2, y: 2, z: 4, core: 2. Of those that a mesh axis runs over, the one named last changes fastest.
Arguments:
- patches: bfloat16 [2, 16, 512, 128], P(None, 'tok', 'head'), may hold values from -6 to 6
- patch_sizes: int32 [2, 16, 512], P(None, 'tok', 'head'), may hold values from 0 to 4
- sample_lengths: int32 [2, 16, 8], P(None, 'tok'), may hold values from 1 to 320, 512 in all within a row
- variate_ids: int32 [2, 16, 512], P(None, 'tok'), may hold values from 0 to 7
- time_ids: int32 [2, 16, 512], P(None, 'tok', 'head'), may hold values from 0 to 511
- predict_mask: int32 [2, 16, 512], P(None, 'tok', 'head'), may hold values from 0 to 1
- block_owner_slot: int32 [159], replicated, may hold values from 0 to 159, as said below
- master_blocks: float32 [160, 128, 128], P(('head', 'tok'))
- left_stats: float32 [160, 128, 128], P(('head', 'tok')), as said below
- right_stats: float32 [160, 128, 128], P(('head', 'tok')), as said below
- left_roots: float32 [160, 128, 128], P(('head', 'tok')), as said below
- right_roots: float32 [160, 128, 128], P(('head', 'tok')), as said below
- vectors: float32 [4, 384], replicated, may hold values from 0.1 to 1.9
- vector_first: float32 [4, 384], replicated
- vector_second: float32 [4, 384], replicated, as said below
- var_bias: float32 [1, 12], replicated, may hold values from -4 to 4
- bias_first: float32 [1, 12], replicated
- bias_second: float32 [1, 12], replicated, as said below
Outputs:
- loss_sum: float32 [], replicated
- value_count: float32 [], replicated
- grad_norm: float32 [], replicated
- clipped_block_gradient: float32 [160, 128, 128], P(('head', 'tok'))
- left_new: float32 [160, 128, 128], P(('head', 'tok'))
- right_new: float32 [160, 128, 128], P(('head', 'tok'))
- master_new: float32 [160, 128, 128], P(('head', 'tok'))
- vector_grads: float32 [4, 384], replicated
- vector_second_new: float32 [4, 384], replicated
- vector_new: float32 [4, 384], replicated
- bias_grads: float32 [1, 12], replicated
- bias_second_new: float32 [1, 12], replicated
- bias_new: float32 [1, 12], replicated
The draws below stay inside these ranges and needn't reach their ends.
Inputs may be any that keep to these rules, and one draw needn't show every extreme that they name: `block_owner_slot`: distinct slot numbers, one for each of the 159 blocks. `left_stats`: symmetric positive definite. `right_stats`: symmetric positive definite. `left_roots`: symmetric. `right_roots`: symmetric. `vector_second`: positive. `bias_second`: positive.
All inputs are finite; a program needn't handle non-finite values.
Results may differ from the reference program's by a relative error of at most 0.012.
The reference program's roundings to bfloat16 on the way count: a program that leaves them out, or rounds other values in their place, can miss the bound.
Values may be sent and summed in bfloat16 or wider, within the bound.
A program may use at most 128 MiB of HBM per device.

```python
import math
import jax
import jax.numpy as jnp
import numpy as np
from jax import lax

D = 384
FF = 1024
HEADS = 6
HEAD_DIM = 64
PSIZES = 5
PMAX = 128
COMPS = 4
SEQ = 512
LAYERS = 1
MICRO = 2
SAMPLES = 8
LONGEST = 320
VARS = 8
BLOCK_SIDE = 128
STEP = 10
ROWS = 16
WEIGHT_BLOCKS = 159
SLOT_TOTAL = 160


clip_limit = 0.02


def block_slots(key):
    first_moment, second_moment = jax.random.split(key)
    spare_slot = jax.random.permutation(first_moment, SLOT_TOTAL - 1)[:WEIGHT_BLOCKS - 1].astype(jnp.int32)
    place_position = jax.random.randint(second_moment, (), 0, WEIGHT_BLOCKS)
    block_index = jnp.arange(WEIGHT_BLOCKS)
    before_update = jnp.concatenate([spare_slot, spare_slot[:1]])
    after_update = jnp.concatenate([spare_slot[:1], spare_slot])
    return jnp.where(block_index < place_position, before_update, jnp.where(block_index == place_position, SLOT_TOTAL - 1, after_update)).astype(jnp.int32)


def grad_unit():
    total = WEIGHT_BLOCKS * BLOCK_SIDE * BLOCK_SIDE + (2 * LAYERS + 2) * D + 2 * LAYERS * HEADS
    return clip_limit / math.sqrt(total)


def fan_table():
    fan_ins = [PMAX] * (PSIZES * (PMAX // BLOCK_SIDE) * (D // BLOCK_SIDE)) + [D] * (D // BLOCK_SIDE * (3 * COMPS * PMAX // BLOCK_SIDE))
    for block_index in range(LAYERS):
        fan_ins = fan_ins + [D] * (D // BLOCK_SIDE * (3 * D // BLOCK_SIDE)) + [max(D // 8, 1)] * (D // BLOCK_SIDE * (D // BLOCK_SIDE))
        fan_ins = fan_ins + [D] * (D // BLOCK_SIDE * (2 * FF // BLOCK_SIDE)) + [FF] * (FF // BLOCK_SIDE * (D // BLOCK_SIDE))
    return np.array(fan_ins + [D], dtype=np.float32)


def dominant(key, scale_factor):
    first_moment, second_moment = jax.random.split(key)
    diagonal_part = scale_factor * (1.0 + 3.0 * jax.random.uniform(first_moment, (SLOT_TOTAL, BLOCK_SIDE), jnp.float32))
    noise_sample = scale_factor * 0.7 / max(BLOCK_SIDE - 1, 1) * jax.random.uniform(second_moment, (SLOT_TOTAL, BLOCK_SIDE, BLOCK_SIDE), jnp.float32, -1.0, 1.0)
    return 0.5 * (noise_sample + noise_sample.transpose(0, 2, 1)) + diagonal_part[:, :, None] * jnp.eye(BLOCK_SIDE, dtype=jnp.float32)


def stat_scale():
    return (1.0 / 0.99 - 1.0) * BLOCK_SIDE * grad_unit() ** 2


def draw_predict_mask(key, part):
    key = jax.random.fold_in(key, 5)
    row_index = jnp.arange(ROWS)
    limit = 200 + 400 * row_index // max(ROWS - 1, 1)
    values = jax.random.randint(key, (MICRO, ROWS, SEQ), 0, 1000)
    return (values < limit[None, :, None]).astype(jnp.int32)


def draw_block_owner_slot(key, part):
    return block_slots(key)


def draw_master_blocks(key, part):
    slot_entries = block_slots(key)
    key = jax.random.fold_in(key, 11)
    holder_slot = jnp.full((SLOT_TOTAL,), WEIGHT_BLOCKS, jnp.int32).at[slot_entries].set(jnp.arange(WEIGHT_BLOCKS, dtype=jnp.int32))
    scale_factors = jnp.asarray(fan_table()) ** (-0.5)
    return jax.random.normal(key, (SLOT_TOTAL, BLOCK_SIDE, BLOCK_SIDE), jnp.float32) * scale_factors[holder_slot][:, None, None]


def draw_left_stats(key, part):
    key = jax.random.fold_in(key, 21)
    return dominant(key, stat_scale())


def draw_right_stats(key, part):
    key = jax.random.fold_in(key, 22)
    return dominant(key, stat_scale())


def draw_left_roots(key, part):
    key = jax.random.fold_in(key, 23)
    return dominant(key, stat_scale() ** (-0.25))


def draw_right_roots(key, part):
    key = jax.random.fold_in(key, 24)
    return dominant(key, stat_scale() ** (-0.25))


def draw_vector_first(key, part):
    key = jax.random.fold_in(key, 31)
    return (1.0 / 0.9 - 1.0) * 5.0 * grad_unit() * jax.random.normal(key, (2 * LAYERS + 2, D), jnp.float32)


def draw_vector_second(key, part):
    key = jax.random.fold_in(key, 32)
    return (1.0 / 0.95 - 1.0) * (5.0 * grad_unit()) ** 2 * jax.random.uniform(key, (2 * LAYERS + 2, D), jnp.float32, 1.0, 4.0)


def draw_bias_first(key, part):
    key = jax.random.fold_in(key, 33)
    return (1.0 / 0.9 - 1.0) * 0.5 * grad_unit() * jax.random.normal(key, (LAYERS, 2 * HEADS), jnp.float32)


def draw_bias_second(key, part):
    key = jax.random.fold_in(key, 34)
    return (1.0 / 0.95 - 1.0) * (0.5 * grad_unit()) ** 2 * jax.random.uniform(key, (LAYERS, 2 * HEADS), jnp.float32, 1.0, 4.0)


def with_ends(drawn, own_key, low, top_value):
    place = [jax.random.randint(jax.random.fold_in(own_key, axis), (), 0, length) for axis, length in enumerate(drawn.shape)]
    longest = drawn.shape.index(max(drawn.shape))
    next_to = place[:longest] + [(place[longest] + 1) % drawn.shape[longest]] + place[longest + 1:]
    return drawn.at[tuple(place)].set(low).at[tuple(next_to)].set(top_value)


def block_scale(key, dims, shards, least, largest):
    factor_of = 1.0
    for position, blocks in shards:
        draws = jax.random.uniform(jax.random.fold_in(jax.random.fold_in(key, 6), position), (blocks,), jnp.float32, least / len(shards), largest / len(shards))
        factor_of = factor_of * jnp.repeat(jnp.exp(draws), dims[position] // blocks).reshape((-1,) + (1,) * (len(dims) - 1 - position))
    return factor_of


def profile(number_of, total, bound, slope):
    loads = [(1 << 20) // math.isqrt(standing ** slope) + 1 for standing in range(2, number_of + 1)]
    rest, holding = total - bound - (number_of - 1), [1] * (number_of - 1)
    while rest > 0:
        movable = [i for i in range(number_of - 1) if holding[i] < bound]
        mass, left = sum([loads[i] for i in movable]), rest
        for i in movable:
            addition = min(bound - holding[i], max(1, left * loads[i] // mass), rest)
            holding[i] = holding[i] + addition
            rest = rest - addition
    return np.array([bound] + holding)


def ragged(rng, amount, total, most, lean):
    if amount == 2:
        one = jax.random.randint(rng, (), max(1, total - most), min(most, total - 1) + 1)
        return jnp.stack([one, total - one])
    sizes = jnp.asarray(profile(amount, total, most, lean), jnp.int32)
    pairs = (amount - 1) // 2
    source_of, taker = sizes[1:1 + 2 * pairs:2], sizes[2:2 + 2 * pairs:2]
    room = jnp.minimum(source_of - 1, most - taker)
    shifted = jax.random.randint(jax.random.fold_in(rng, 1), (pairs,), 0, 1 << 20) % (room + 1)
    sizes = sizes.at[1:1 + 2 * pairs:2].set(source_of - shifted).at[2:2 + 2 * pairs:2].set(taker + shifted)
    return sizes[jax.random.permutation(jax.random.fold_in(rng, 2), amount)]


def noise(stream_key, shape, width, bound, shards=(), held_as=jnp.bfloat16):
    factor_of = block_scale(stream_key, shape, shards, -0.22, 0.18) if shards else 1.0
    entries = jax.random.normal(stream_key, shape, jnp.float32) * width * factor_of
    return jnp.minimum(jnp.maximum(entries, -bound), bound).astype(held_as)


def setup_inputs(seed: int = 0) -> dict:
    key_of = jax.random.split(jax.random.key(seed), 19)
    patches = noise(key_of[0], (MICRO, ROWS, SEQ, PMAX), 1.0, 6.0, ((1, 16), (2, 2)))
    patch_sizes = with_ends(jax.random.randint(key_of[1], (MICRO, ROWS, SEQ), 0, PSIZES), jax.random.fold_in(key_of[1], 1), 0, PSIZES - 1).astype(jnp.int32)
    sample_lengths = jax.vmap(lambda own: ragged(own, SAMPLES, SEQ, LONGEST, 2))(jax.random.split(key_of[2], MICRO * ROWS)).reshape((MICRO, ROWS, SAMPLES)).astype(jnp.int32)
    variate_ids = with_ends(jax.random.randint(key_of[3], (MICRO, ROWS, SEQ), 0, VARS), jax.random.fold_in(key_of[3], 1), 0, VARS - 1).astype(jnp.int32)
    time_ids = with_ends(jax.random.randint(key_of[4], (MICRO, ROWS, SEQ), 0, SEQ), jax.random.fold_in(key_of[4], 1), 0, SEQ - 1).astype(jnp.int32)
    predict_mask = draw_predict_mask(jax.random.fold_in(key_of[18], 71), 0)
    block_owner_slot = draw_block_owner_slot(jax.random.fold_in(key_of[18], 71), 0)
    master_blocks = draw_master_blocks(jax.random.fold_in(key_of[18], 71), 0)
    left_stats = draw_left_stats(jax.random.fold_in(key_of[18], 71), 0)
    right_stats = draw_right_stats(jax.random.fold_in(key_of[18], 71), 0)
    left_roots = draw_left_roots(jax.random.fold_in(key_of[18], 71), 0)
    right_roots = draw_right_roots(jax.random.fold_in(key_of[18], 71), 0)
    vectors = jnp.clip(1.0 + 0.18 * jax.random.normal(key_of[12], (2 * LAYERS + 2, D), jnp.float32), 0.1, 1.9)
    vector_first = draw_vector_first(jax.random.fold_in(key_of[18], 71), 0)
    vector_second = draw_vector_second(jax.random.fold_in(key_of[18], 71), 0)
    var_bias = noise(key_of[15], (LAYERS, 2 * HEADS), 1.0, 4.0, (), jnp.float32)
    bias_first = draw_bias_first(jax.random.fold_in(key_of[18], 71), 0)
    bias_second = draw_bias_second(jax.random.fold_in(key_of[18], 71), 0)
    return {"patches": patches, "patch_sizes": patch_sizes, "sample_lengths": sample_lengths, "variate_ids": variate_ids, "time_ids": time_ids, "predict_mask": predict_mask, "block_owner_slot": block_owner_slot, "master_blocks": master_blocks, "left_stats": left_stats, "right_stats": right_stats, "left_roots": left_roots, "right_roots": right_roots, "vectors": vectors, "vector_first": vector_first, "vector_second": vector_second, "var_bias": var_bias, "bias_first": bias_first, "bias_second": bias_second}


norm_eps = 1e-06
scale_floor = 0.05
half_log_tau = 0.9189385332046727
clip_limit = 0.02
mat_rate = 0.01
vec_rate = 0.3
decay_rate = 0.01
beta_one = 0.9
beta_two = 0.95
stat_beta = 0.99
root_eps = 1e-06
adam_eps = 1e-08
highest = lax.Precision.HIGHEST

@jax.custom_vjp
def low(v):
    return lax.optimization_barrier(v.astype(jnp.bfloat16)).astype(jnp.float32)

@jax.custom_vjp
def low_back(v):
    return v

def low_keep(v):
    return (low(v), None)

def low_pass(kept, grad):
    return (grad,)

def back_keep(v):
    return (v, None)

def back_low(kept, grad):
    return (low(grad),)
low.defvjp(low_keep, low_pass)
low_back.defvjp(back_keep, back_low)

def patch_length(codes):
    return PMAX * jnp.left_shift(1, codes) // 2 ** (PSIZES - 1)

def sample_ids(lengths):
    ends = jnp.cumsum(lengths, axis=-1)
    places = jnp.arange(SEQ)
    return lax.optimization_barrier(jnp.sum((places[:, None] >= ends[..., None, :]).astype(jnp.int32), axis=-1))

def rotate(values, positions):
    half_dim = HEAD_DIM // 2
    frequency = 10000.0 ** (-jnp.arange(half_dim, dtype=jnp.float32) / half_dim)
    angle = positions[..., None] * frequency
    cosine = jnp.cos(angle)[..., None, :]
    sine = jnp.sin(angle)[..., None, :]
    first_moment = values[..., :half_dim]
    second_moment = values[..., half_dim:]
    return jnp.concatenate([first_moment * cosine - second_moment * sine, first_moment * sine + second_moment * cosine], axis=-1)

def shapes_list():
    shapes = [(PMAX, D)] * PSIZES + [(D, 3 * COMPS * PMAX)]
    for block_index in range(LAYERS):
        shapes = shapes + [(D, 3 * D), (D, D), (D, 2 * FF), (FF, D)]
    return shapes

def unpack(blocks):
    result = []
    offset = 0
    for row_count, col_count in shapes_list():
        number = row_count // BLOCK_SIDE * (col_count // BLOCK_SIDE)
        piece = blocks[offset:offset + number].reshape(row_count // BLOCK_SIDE, col_count // BLOCK_SIDE, BLOCK_SIDE, BLOCK_SIDE)
        result.append(piece.transpose(0, 2, 1, 3).reshape(row_count, col_count))
        offset = offset + number
    return result

def nll_sum(params, targets, weight):
    log_mix = jax.nn.log_softmax(params[:, :, 0], axis=-1)
    widths = jax.nn.softplus(params[:, :, 2]) + scale_floor
    normal_z = (targets[:, :, None] - params[:, :, 1]) / widths
    terms = log_mix - 0.5 * normal_z * normal_z - jnp.log(widths) - half_log_tau
    return jnp.sum(weight * -jax.nn.logsumexp(terms, axis=-1))

def shampoo(gradients, left, right, left_root, right_root, master):
    left_next = stat_beta * left + (1.0 - stat_beta) * jnp.einsum('sij,skj->sik', gradients, gradients, precision=highest)
    right_next = stat_beta * right + (1.0 - stat_beta) * jnp.einsum('sji,sjk->sik', gradients, gradients, precision=highest)
    shaped = jnp.einsum('sij,sjk->sik', left_root, gradients, precision=highest)
    shaped = jnp.einsum('sij,sjk->sik', shaped, right_root, precision=highest)
    unit = shaped * lax.rsqrt(lax.optimization_barrier(jnp.mean(shaped * shaped, axis=(1, 2), keepdims=True)) + root_eps)
    return (left_next, right_next, master - mat_rate * (unit + decay_rate * master))

def adamw(gradients, first_moment, second_moment, values):
    first_next = beta_one * first_moment + (1.0 - beta_one) * gradients
    second_next = beta_two * second_moment + (1.0 - beta_two) * gradients * gradients
    ratio = first_next / (1.0 - beta_one ** STEP) / (jnp.sqrt(second_next / (1.0 - beta_two ** STEP)) + adam_eps)
    return (second_next, values - vec_rate * (ratio + decay_rate * values))

def rms_norm(stream, gain):
    return stream * lax.rsqrt(lax.optimization_barrier(jnp.mean(stream * stream, axis=-1, keepdims=True)) + norm_eps) * gain

def product(left, right):
    return jnp.dot(left, right, precision=highest)

def row_loss(matrices, vectors, var_bias, patch, codes, lengths, variates, times, predict):
    targets = patch.astype(jnp.float32)
    valid = jnp.arange(PMAX)[None, :] < patch_length(codes)[:, None]
    inputs = jnp.where(valid, targets, 0.0)
    embedded = jnp.zeros((SEQ, D), jnp.float32)
    for block_index in range(PSIZES):
        chosen = (codes == block_index)[:, None]
        embedded = embedded + jnp.where(chosen, low_back(product(inputs, low(matrices[block_index]))), 0.0)
    flag = (predict == 1)[:, None]
    stream = jnp.where(flag, vectors[2 * LAYERS + 1][None, :], embedded)
    ids = sample_ids(lengths)
    same_sample = (ids[:, None] == ids[None, :])[None]
    same_var = (variates[:, None] == variates[None, :])[None]
    positions = times.astype(jnp.float32)
    for block_index in range(LAYERS):
        w_qkv, w_out, w_gate_up, w_down = matrices[PSIZES + 1 + 4 * block_index:PSIZES + 5 + 4 * block_index]
        normed = low(rms_norm(stream, vectors[2 * block_index]))
        mixed = low_back(product(normed, low(w_qkv))).reshape(SEQ, 3, HEADS, HEAD_DIM)
        packed = low(low_back(jnp.stack([rotate(mixed[:, 0], positions), rotate(mixed[:, 1], positions), mixed[:, 2]], axis=1)))
        scores = low_back(jnp.einsum('qhd,khd->hqk', packed[:, 0], packed[:, 1], precision=highest)) * HEAD_DIM ** (-0.5)
        pair = var_bias[block_index].reshape(2, HEADS)
        bias = jnp.where(same_var, pair[0][:, None, None], pair[1][:, None, None])
        weights_p = low(jax.nn.softmax(jnp.where(same_sample, scores + bias, -1e+30), axis=-1))
        attended = low(low_back(jnp.einsum('hqk,khd->qhd', weights_p, packed[:, 2], precision=highest)))
        middle = stream + low_back(product(attended.reshape(SEQ, D), low(w_out)))
        normed = low(rms_norm(middle, vectors[2 * block_index + 1]))
        gate_up = low_back(product(normed, low(w_gate_up)))
        hidden = low(jax.nn.silu(gate_up[:, :FF]) * gate_up[:, FF:])
        stream = middle + low_back(product(hidden, low(w_down)))
    normed = low(rms_norm(stream, vectors[2 * LAYERS]))
    params = low_back(product(normed, low(matrices[PSIZES]))).reshape(SEQ, PMAX, 3, COMPS)
    weight = (valid & flag).astype(jnp.float32)
    return nll_sum(params, targets, weight)

def reference(patches, patch_sizes, sample_lengths, variate_ids, time_ids, predict_mask, block_owner_slot, master_blocks, left_stats, right_stats, left_roots, right_roots, vectors, vector_first, vector_second, var_bias, bias_first, bias_second):
    blocks = master_blocks[block_owner_slot]

    def flatten(array):
        return array.reshape((MICRO * ROWS,) + array.shape[2:])
    data = tuple((flatten(a) for a in (patches, patch_sizes, sample_lengths, variate_ids, time_ids, predict_mask)))
    value_count = jnp.sum(patch_length(patch_sizes) * predict_mask).astype(jnp.float32)
    saved_row = jax.checkpoint(row_loss)

    def objective(blocks, vectors, var_bias):
        matrices = unpack(blocks)

        def advance(carry, row):
            return (carry + saved_row(matrices, vectors, var_bias, *row), None)
        total, unused = lax.scan(advance, jnp.zeros((), jnp.float32), data)
        return (total / value_count, total)
    value, pullback, loss_sum = jax.vjp(objective, blocks, vectors, var_bias, has_aux=True)
    gradient_block_list, grad_vectors, grad_bias = pullback(jnp.ones((), jnp.float32))
    grad_norm = jnp.sqrt(jnp.sum(gradient_block_list * gradient_block_list) + jnp.sum(grad_vectors * grad_vectors) + jnp.sum(grad_bias * grad_bias))
    factor_value = jnp.minimum(1.0, clip_limit / grad_norm)
    clipped_block_gradient = jnp.zeros((SLOT_TOTAL, BLOCK_SIDE, BLOCK_SIDE), jnp.float32).at[block_owner_slot].set(gradient_block_list * factor_value)
    left_new, right_new, master_new = shampoo(clipped_block_gradient, left_stats, right_stats, left_roots, right_roots, master_blocks)
    vector_grads = grad_vectors * factor_value
    vector_second_new, vector_new = adamw(vector_grads, vector_first, vector_second, vectors)
    bias_grads = grad_bias * factor_value
    bias_second_new, bias_new = adamw(bias_grads, bias_first, bias_second, var_bias)
    return (loss_sum, value_count, grad_norm, clipped_block_gradient, left_new, right_new, master_new, vector_grads, vector_second_new, vector_new, bias_grads, bias_second_new, bias_new)
```

```python
import functools

import jax
import jax.numpy as jnp
import numpy as np
from jax import lax
from jax.experimental import pallas as pl
from jax.experimental.pallas import tpu as pltpu
from jax.sharding import PartitionSpec as P

D = 384
FF = 1024
HEADS = 6
HEAD_DIM = 64
PSIZES = 5
PMAX = 128
COMPS = 4
SEQ = 512
SIDE = 128
STEP = 10
HEADCOLS = 3 * COMPS * PMAX
BLOCKS = 159

norm_eps = 1e-06
scale_floor = 0.05
half_log_tau = 0.9189385332046727
clip_limit = 0.02
mat_rate = 0.01
vec_rate = 0.3
decay_rate = 0.01
beta_one = 0.9
beta_two = 0.95
stat_beta = 0.99
root_eps = 1e-06
adam_eps = 1e-08
highest = lax.Precision.HIGHEST
f32 = jnp.float32
bf16 = jnp.bfloat16

GRIDS = ((5, 3), (3, 12), (3, 9), (3, 3), (3, 16), (8, 3))
FIRSTS = (0, 15, 51, 78, 87, 135)
M_IN, M_HEAD, M_QKV, M_OUT, M_GU, M_DOWN = range(6)


def mm(a, b):
    return jnp.dot(a, b, preferred_element_type=f32)


def mm_nt(a, b):
    return lax.dot_general(a, b, (((1,), (1,)), ((), ())), preferred_element_type=f32)


def mm_tn(a, b):
    return lax.dot_general(a, b, (((0,), (0,)), ((), ())), preferred_element_type=f32)


def column_order():
    order = np.zeros((HEADCOLS, HEADCOLS), np.float32)
    for col in range(HEADCOLS):
        order[col, (col % (3 * COMPS)) * PMAX + col // (3 * COMPS)] = 1.0
    return order


SCRATCH = dict(
    w_in=((640, D), bf16), w_head=((D, HEADCOLS), bf16), w_qkv=((D, 3 * D), bf16), w_out=((D, D), bf16),
    w_gu=((D, 2 * FF), bf16), w_down=((FF, D), bf16), w_order=((HEADCOLS, HEADCOLS), bf16),
    w_headp=((D, HEADCOLS), bf16),
    g_in=((640, D), bf16), g_head=((D, HEADCOLS), bf16), g_qkv=((D, 3 * D), bf16), g_out=((D, D), bf16),
    g_gu=((D, 2 * FF), bf16), g_down=((FF, D), bf16), zero_block=((SIDE, SIDE), bf16),
    x5=((SEQ, 640), bf16), weight=((SEQ, PMAX), f32), cos_t=((SEQ, 128), f32), sin_t=((SEQ, 128), f32),
    code_t=((SEQ, SEQ), f32), probs=((HEADS, SEQ, SEQ), f32),
    stream=((SEQ, D), f32), middle=((SEQ, D), f32), last=((SEQ, D), f32), grad=((SEQ, D), f32), inner=((SEQ, D), f32),
    inv_a=((SEQ, 128), f32), inv_b=((SEQ, 128), f32), inv_f=((SEQ, 128), f32),
    normed_a=((SEQ, D), bf16), normed_b=((SEQ, D), bf16), normed_f=((SEQ, D), bf16),
    qs=((SEQ, D), bf16), ks=((SEQ, D), bf16), vs=((SEQ, D), bf16), merged=((SEQ, D), bf16),
    gate=((SEQ, FF), f32), upper=((SEQ, FF), f32), hidden=((SEQ, FF), bf16),
    params=((SEQ, HEADCOLS), f32), gparams=((SEQ, HEADCOLS), bf16), ggu=((SEQ, 2 * FF), bf16),
    rounded=((SEQ, D), bf16), dattn=((SEQ, D), bf16), dqkv=((SEQ, 3 * D), bf16), dscore=((SEQ, SEQ), bf16),
    loss_acc=((32, 128), f32), bias_acc=((16, 128), f32), vec_acc=((8, D), f32),
)


def tile(i, size):
    return pl.ds(pl.multiple_of(i * size, size), size)


def row_kernel(
    slots, lengths, bias, inv_count, patches, meta, vectors, freq, order, gathered, gout, vec_out, bias_out, *scratch
):
    s = type("S", (), dict(zip(SCRATCH, scratch)))
    marks, w_sem, o_sem, g_sem = scratch[len(SCRATCH) :]
    weights = (s.w_in, s.w_head, s.w_qkv, s.w_out, s.w_gu, s.w_down)
    grads = (s.g_in, s.g_head, s.g_qkv, s.g_out, s.g_gu, s.g_down)
    slot_count = gathered.shape[0]

    def load(m):
        rows, cols = GRIDS[m]

        @pl.loop(0, rows * cols)
        def _(i):
            pltpu.make_async_copy(
                gathered.at[slots[FIRSTS[m] + i]],
                weights[m].at[tile(i // cols, SIDE), tile(i % cols, SIDE)],
                w_sem.at[m],
            ).start()

    def loaded(m):
        pltpu.make_async_copy(weights[m], weights[m], w_sem.at[m]).wait()

    def send(m):
        rows, cols = GRIDS[m]

        @pl.loop(0, rows * cols)
        def _(i):
            pltpu.make_async_copy(
                grads[m].at[tile(i // cols, SIDE), tile(i % cols, SIDE)],
                gout.at[slots[FIRSTS[m] + i]],
                g_sem.at[m],
            ).start()

    for m in (M_IN, M_QKV, M_OUT, M_GU, M_DOWN, M_HEAD):
        load(m)
    order_copy = pltpu.make_async_copy(order, s.w_order, o_sem)
    order_copy.start()

    s.zero_block[...] = jnp.zeros_like(s.zero_block)

    @pl.loop(0, slot_count)
    def _(i):
        marks[i] = 0

    @pl.loop(0, BLOCKS)
    def _(b):
        marks[slots[b]] = 1

    @pl.loop(0, slot_count)
    def _(i):
        @pl.when(marks[i] == 0)
        def _():
            pltpu.make_async_copy(s.zero_block, gout.at[i], g_sem.at[6]).start()

    metaf = meta[...].astype(f32)
    columns = jnp.transpose(metaf)
    codes, times, flag = columns[:, 0:1], columns[:, 1:2], columns[:, 2:3] == 1.0
    position = lax.broadcasted_iota(jnp.int32, (1, SEQ), 1)
    ids = jnp.zeros((1, SEQ), f32)
    end = jnp.int32(0)
    for j in range(lengths.shape[0]):
        end = end + lengths[j]
        ids = ids + jnp.where(position >= end, 1.0, 0.0)
    variates = metaf[3:4]
    id_columns = jnp.transpose(jnp.concatenate([ids] * 8, axis=0))[:, 0:1]
    var_columns = columns[:, 3:4]
    for c in range(4):
        cs = slice(c * 128, (c + 1) * 128)
        same_sample = id_columns == ids[:, cs]
        same_var = var_columns == variates[:, cs]
        s.code_t[:, cs] = jnp.where(same_sample, jnp.where(same_var, 2.0, 1.0), 0.0)
    lane = lax.broadcasted_iota(jnp.int32, (1, 128), 1)
    first_half = lane % HEAD_DIM < HEAD_DIM // 2
    low_head = lane < HEAD_DIM
    angle = times * freq[0:1, :]
    s.cos_t[...] = jnp.cos(angle)
    s.sin_t[...] = jnp.where(first_half, -1.0, 1.0) * jnp.sin(angle)

    def turn(v, sine):
        swapped = jnp.where(first_half, pltpu.roll(v, 96, 1), pltpu.roll(v, 32, 1))
        return v * s.cos_t[...] + swapped * sine

    wide = patches[...].astype(f32)
    weight = jnp.zeros((SEQ, PMAX), f32)
    for c in range(PSIZES):
        keep = (codes == float(c)) & (lane < PMAX * 2**c // 2 ** (PSIZES - 1))
        s.x5[:, c * 128 : (c + 1) * 128] = jnp.where(keep, wide, 0.0).astype(bf16)
        weight = jnp.where(keep, 1.0, weight)
    s.weight[...] = jnp.where(flag, weight, 0.0)
    loaded(M_IN)
    s.stream[...] = jnp.where(flag, vectors[3:4, :], mm(s.x5[...], s.w_in[...]))

    def norm(src, inv_ref, gain, dst):
        @pl.loop(0, SEQ // 128)
        def _(i):
            rs = tile(i, 128)
            v = src[rs, :]
            inverse = lax.rsqrt(jnp.sum(v * v, axis=-1, keepdims=True) / D + norm_eps)
            inv_ref[rs, :] = jnp.broadcast_to(inverse, (128, 128))
            dst[rs, :] = (v * inverse * gain).astype(bf16)

    def norm_back(src, inv_ref, row, extra):
        gain = vectors[row : row + 1, :]

        @pl.loop(0, SEQ // 128)
        def _(i):
            rs = tile(i, 128)
            up = s.inner[rs, :]
            inverse = inv_ref[rs, 0:1]
            scaled = src[rs, :] * inverse
            inner = up * gain
            mean = jnp.sum(inner * scaled, axis=-1, keepdims=True) / D
            result = inverse * (inner - scaled * mean)
            s.grad[rs, :] = result if extra is None else result + extra[rs, :]
            s.vec_acc[row : row + 1, :] += jnp.sum(up * scaled, axis=0, keepdims=True)

    s.vec_acc[...] = jnp.zeros_like(s.vec_acc)
    norm(s.stream, s.inv_a, vectors[0:1, :], s.normed_a)
    loaded(M_QKV)
    for part, dst in ((0, s.qs), (1, s.ks), (2, s.vs)):
        mixed = mm(s.normed_a[...], s.w_qkv[:, part * D : (part + 1) * D])
        for c in range(3):
            piece = mixed[:, c * 128 : (c + 1) * 128]
            if part < 2:
                piece = turn(piece, s.sin_t[...])
            dst[:, c * 128 : (c + 1) * 128] = piece.astype(bf16)

    @pl.loop(0, HEADS // 2)
    def _(p):
        ps = tile(p, 128)
        qp, kp = s.qs[:, ps], s.ks[:, ps]
        vt = jnp.transpose(s.vs[:, ps])
        outs = []
        for hh in range(2):
            mine = low_head if hh == 0 else jnp.logical_not(low_head)
            qm = jnp.where(mine, qp.astype(f32) * HEAD_DIM**-0.5, 0.0).astype(bf16)
            b0 = bias[2 * p + hh]
            b1 = bias[HEADS + 2 * p + hh]
            parts = []
            for c in range(4):
                cs = slice(c * 128, (c + 1) * 128)
                code = s.code_t[:, cs]
                score = mm_nt(kp, qm[cs, :])
                score = jnp.where(code > 0.5, score + jnp.where(code > 1.5, b0, b1), -1e30)
                raised = jnp.exp(score - jnp.max(score, axis=0, keepdims=True))
                prob = raised * (1.0 / jnp.sum(raised, axis=0, keepdims=True))
                s.probs[2 * p + hh, :, cs] = prob
                parts.append(mm(vt[hh * 64 : (hh + 1) * 64, :], prob.astype(bf16)))
            outs.append(jnp.concatenate(parts, axis=1))
        s.merged[:, ps] = jnp.transpose(jnp.concatenate(outs, axis=0)).astype(bf16)

    loaded(M_OUT)
    s.middle[...] = s.stream[...] + mm(s.merged[...], s.w_out[...])
    norm(s.middle, s.inv_b, vectors[1:2, :], s.normed_b)
    loaded(M_GU)

    @pl.loop(0, FF // 256)
    def _(j):
        js = tile(j, 256)
        opening = mm(s.normed_b[...], s.w_gu[:, js])
        up = mm(s.normed_b[...], s.w_gu[:, tile(j + FF // 256, 256)])
        s.gate[:, js] = opening
        s.upper[:, js] = up
        s.hidden[:, js] = (opening * (1.0 / (1.0 + jnp.exp(-opening))) * up).astype(bf16)

    loaded(M_DOWN)
    s.last[...] = s.middle[...] + mm(s.hidden[...], s.w_down[...])
    norm(s.last, s.inv_f, vectors[2:3, :], s.normed_f)

    order_copy.wait()
    loaded(M_HEAD)

    @pl.loop(0, HEADCOLS // 256)
    def _(j):
        js = tile(j, 256)
        s.w_headp[:, js] = mm(s.w_head[...], s.w_order[:, js]).astype(bf16)
        s.params[:, js] = mm(s.normed_f[...], s.w_headp[:, js])

    inv_n = inv_count[0]
    s.loss_acc[...] = jnp.zeros_like(s.loss_acc)

    @pl.loop(0, SEQ // 32)
    def _(i):
        rs = tile(i, 32)
        y = patches[rs, :].astype(f32)
        weight = s.weight[rs, :]
        logits, means, raws = [
            [s.params[rs, (4 * kind + k) * 128 : (4 * kind + k + 1) * 128] for k in range(COMPS)] for kind in range(3)
        ]
        top = jnp.maximum(jnp.maximum(logits[0], logits[1]), jnp.maximum(logits[2], logits[3]))
        shifted = [v - top for v in logits]
        raised = [jnp.exp(v) for v in shifted]
        total = raised[0] + raised[1] + raised[2] + raised[3]
        log_total = jnp.log(total)
        inv_total = 1.0 / total
        terms, zs, inv_widths = [], [], []
        for k in range(COMPS):
            width = jnp.maximum(raws[k], 0.0) + jnp.log1p(jnp.exp(-jnp.abs(raws[k]))) + scale_floor
            inv_width = 1.0 / width
            z = (y - means[k]) * inv_width
            terms.append((shifted[k] - log_total) - 0.5 * z * z - jnp.log(width) - half_log_tau)
            zs.append(z)
            inv_widths.append(inv_width)
        best = jnp.maximum(jnp.maximum(terms[0], terms[1]), jnp.maximum(terms[2], terms[3]))
        lifted = [jnp.exp(t - best) for t in terms]
        lift_total = lifted[0] + lifted[1] + lifted[2] + lifted[3]
        inv_lift = 1.0 / lift_total
        s.loss_acc[...] += jnp.where(weight > 0.0, -(best + jnp.log(lift_total)), 0.0)
        scale = -(weight * inv_n)
        for k in range(COMPS):
            share = lifted[k] * inv_lift
            d_term = scale * share
            ratio = zs[k] * inv_widths[k]
            d_logit = scale * (share - raised[k] * inv_total)
            d_width = d_term * (zs[k] * ratio - inv_widths[k])
            sigma = 1.0 / (1.0 + jnp.exp(-raws[k]))
            for kind, value in ((0, d_logit), (1, d_term * ratio), (2, d_width * sigma)):
                at = (4 * kind + k) * 128
                s.gparams[rs, at : at + 128] = value.astype(bf16)

    @pl.loop(0, HEADCOLS // 256)
    def _(j):
        js = tile(j, 256)
        s.w_head[:, js] = mm_tn(s.normed_f[...], s.gparams[:, js]).astype(bf16)

    @pl.loop(0, HEADCOLS // 256)
    def _(j):
        js = tile(j, 256)
        s.g_head[:, js] = mm_nt(s.w_head[...], s.w_order[js, :]).astype(bf16)

    send(M_HEAD)
    s.inner[...] = mm_nt(s.gparams[...], s.w_headp[...])
    norm_back(s.last, s.inv_f, 2, None)

    s.rounded[...] = s.grad[...].astype(bf16)

    @pl.loop(0, FF // 256)
    def _(j):
        js = tile(j, 256)
        s.g_down[js, :] = mm_tn(s.hidden[:, js], s.rounded[...]).astype(bf16)
        up_grad = mm_nt(s.rounded[...], s.w_down[js, :])
        opening = s.gate[:, js]
        sigma = 1.0 / (1.0 + jnp.exp(-opening))
        s.ggu[:, js] = (up_grad * s.upper[:, js] * sigma * (1.0 + opening * (1.0 - sigma))).astype(bf16)
        s.ggu[:, tile(j + FF // 256, 256)] = (up_grad * opening * sigma).astype(bf16)

    send(M_DOWN)

    @pl.loop(0, 2 * FF // 256)
    def _(j):
        js = tile(j, 256)
        s.g_gu[:, js] = mm_tn(s.normed_b[...], s.ggu[:, js]).astype(bf16)

    send(M_GU)
    s.inner[...] = mm_nt(s.ggu[...], s.w_gu[...])
    norm_back(s.middle, s.inv_b, 1, s.grad)

    s.rounded[...] = s.grad[...].astype(bf16)
    s.g_out[...] = mm_tn(s.merged[...], s.rounded[...]).astype(bf16)
    send(M_OUT)
    s.dattn[...] = mm_nt(s.rounded[...], s.w_out[...]).astype(bf16)
    s.bias_acc[...] = jnp.zeros_like(s.bias_acc)

    @pl.loop(0, HEADS // 2)
    def _(p):
        ps = tile(p, 128)
        qp, kp, vp, dop = s.qs[:, ps], s.ks[:, ps], s.vs[:, ps], s.dattn[:, ps]
        kt = jnp.transpose(kp)
        dq, dk, dv = [], [], []
        for hh in range(2):
            mine = low_head if hh == 0 else jnp.logical_not(low_head)
            dom = jnp.where(mine, dop.astype(f32), 0.0).astype(bf16)
            same_sum = jnp.zeros((1, 128), f32)
            all_sum = jnp.zeros((1, 128), f32)
            for c in range(4):
                cs = slice(c * 128, (c + 1) * 128)
                prob = s.probs[2 * p + hh, :, cs]
                d_prob = mm_nt(vp, dom[cs, :])
                d_score = prob * (d_prob - jnp.sum(prob * d_prob, axis=0, keepdims=True))
                same_sum += jnp.sum(jnp.where(s.code_t[:, cs] > 1.5, d_score, 0.0), axis=0, keepdims=True)
                all_sum += jnp.sum(d_score, axis=0, keepdims=True)
                s.dscore[:, cs] = (d_score * HEAD_DIM**-0.5).astype(bf16)
            s.bias_acc[pl.ds(2 * p + hh, 1), :] = same_sum
            s.bias_acc[pl.ds(8 + 2 * p + hh, 1), :] = all_sum
            dv.append(mm(s.probs[2 * p + hh].astype(bf16), dop))
            dk.append(mm(s.dscore[...], qp))
            dq.append(mm(kt[hh * 64 : (hh + 1) * 64, :], s.dscore[...]))
        dqs = jnp.transpose(jnp.concatenate(dq, axis=0)).astype(bf16).astype(f32)
        dks = jnp.where(low_head, dk[0], dk[1]).astype(bf16).astype(f32)
        s.dqkv[:, ps] = turn(dqs, -s.sin_t[...]).astype(bf16)
        s.dqkv[:, tile(p + 3, 128)] = turn(dks, -s.sin_t[...]).astype(bf16)
        s.dqkv[:, tile(p + 6, 128)] = jnp.where(low_head, dv[0], dv[1]).astype(bf16)

    for j in range(3):
        js = slice(j * D, (j + 1) * D)
        s.g_qkv[:, js] = mm_tn(s.normed_a[...], s.dqkv[:, js]).astype(bf16)
    send(M_QKV)
    s.inner[...] = mm_nt(s.dqkv[...], s.w_qkv[...])
    norm_back(s.stream, s.inv_a, 0, s.grad)
    s.vec_acc[3:4, :] = jnp.sum(jnp.where(flag, s.grad[...], 0.0), axis=0, keepdims=True)
    s.rounded[...] = jnp.where(flag, 0.0, s.grad[...]).astype(bf16)
    s.g_in[...] = mm_tn(s.x5[...], s.rounded[...]).astype(bf16)
    send(M_IN)

    row = lax.broadcasted_iota(jnp.int32, (8, D), 0)
    vec_out[...] = jnp.where(row == 4, jnp.sum(s.loss_acc[...]), s.vec_acc[...])
    sums = jnp.sum(s.bias_acc[...], axis=1, keepdims=True)
    bias_out[0:8, :] = jnp.broadcast_to(sums[0:8], (8, 128))
    bias_out[8:16, :] = jnp.broadcast_to(sums[8:16] - sums[0:8], (8, 128))

    for m in range(6):
        pltpu.make_async_copy(grads[m], grads[m], g_sem.at[m]).wait()

    @pl.loop(0, slot_count)
    def _(i):
        @pl.when(marks[i] == 0)
        def _():
            pltpu.make_async_copy(s.zero_block, gout.at[i], g_sem.at[6]).wait()


def row_step(slots, lengths, bias, inv_count, patches, meta, vectors, gathered):
    freq = 10000.0 ** (-jnp.arange(HEAD_DIM // 2, dtype=f32) / (HEAD_DIM // 2))
    freq = jnp.tile(freq[None], (8, 4))
    smem = pl.BlockSpec(memory_space=pltpu.SMEM)
    vmem = pl.BlockSpec(memory_space=pltpu.VMEM)
    hbm = pl.BlockSpec(memory_space=pl.ANY)
    return pl.pallas_call(
        row_kernel,
        out_shape=(
            jax.ShapeDtypeStruct(gathered.shape, bf16),
            jax.ShapeDtypeStruct((8, D), f32),
            jax.ShapeDtypeStruct((16, 128), f32),
        ),
        in_specs=[smem] * 4 + [vmem] * 4 + [hbm] * 2,
        out_specs=(hbm, vmem, vmem),
        scratch_shapes=[pltpu.VMEM(shape, dtype) for shape, dtype in SCRATCH.values()]
        + [
            pltpu.SMEM((gathered.shape[0],), jnp.int32),
            pltpu.SemaphoreType.DMA((6,)),
            pltpu.SemaphoreType.DMA,
            pltpu.SemaphoreType.DMA((7,)),
        ],
        compiler_params=pltpu.CompilerParams(vmem_limit_bytes=62 * 2**20),
        name="row",
    )(slots, lengths, bias, inv_count, patches, meta, vectors, freq, jnp.asarray(column_order(), bf16), gathered)


def shampoo(gradients, left, right, left_root, right_root, master):
    left_next = stat_beta * left + (1.0 - stat_beta) * jnp.einsum(
        "sij,skj->sik", gradients, gradients, precision=highest
    )
    right_next = stat_beta * right + (1.0 - stat_beta) * jnp.einsum(
        "sji,sjk->sik", gradients, gradients, precision=highest
    )
    shaped = jnp.einsum("sij,sjk->sik", left_root, gradients, precision=highest)
    shaped = jnp.einsum("sij,sjk->sik", shaped, right_root, precision=highest)
    unit = shaped * lax.rsqrt(jnp.mean(shaped * shaped, axis=(1, 2), keepdims=True) + root_eps)
    return (left_next, right_next, master - mat_rate * (unit + decay_rate * master))


def adamw(gradients, first_moment, second_moment, values):
    first_next = beta_one * first_moment + (1.0 - beta_one) * gradients
    second_next = beta_two * second_moment + (1.0 - beta_two) * gradients * gradients
    ratio = (
        first_next
        / (1.0 - beta_one**STEP)
        / (jnp.sqrt(second_next / (1.0 - beta_two**STEP)) + adam_eps)
    )
    return (second_next, values - vec_rate * (ratio + decay_rate * values))


def shards(
    patches, patch_sizes, sample_lengths, variate_ids, time_ids, predict_mask, block_owner_slot,
    master_blocks, left_stats, right_stats, left_roots, right_roots,
    vectors, vector_first, vector_second, var_bias, bias_first, bias_second,
):
    both = ("head", "tok")
    head = lax.axis_index("head")
    local_count = jnp.sum(PMAX * jnp.left_shift(1, patch_sizes) // 2 ** (PSIZES - 1) * predict_mask).astype(f32)
    count = lax.psum(local_count, both)
    gathered = lax.all_gather(master_blocks.astype(bf16), both, axis=0, tiled=True)
    row_patches = lax.all_to_all(patches, "head", split_axis=0, concat_axis=2, tiled=True).reshape(SEQ, PMAX)
    ints = jnp.stack([patch_sizes, time_ids, predict_mask], axis=1)
    ints = lax.all_to_all(ints, "head", split_axis=0, concat_axis=3, tiled=True).reshape(3, SEQ)
    variates = lax.dynamic_index_in_dim(variate_ids, head, 0, False)
    meta = jnp.concatenate([ints, variates, jnp.zeros((4, SEQ), jnp.int32)], axis=0)
    lengths = lax.dynamic_index_in_dim(sample_lengths, head, 0, False)[0]
    grad_slots, vec, bias_rows = row_step(
        block_owner_slot, lengths, var_bias[0], (1.0 / count)[None], row_patches, meta, vectors, gathered
    )
    owned = lax.psum_scatter(grad_slots.astype(f32), both, scatter_dimension=0, tiled=True)
    bias_local = jnp.concatenate([bias_rows[0:HEADS, 0], bias_rows[8 : 8 + HEADS, 0]])[None]
    vector_total, bias_total, loss_sum = lax.psum((vec[0:4], bias_local, vec[4, 0]), both)
    block_square = lax.psum(jnp.sum(owned * owned), both)
    grad_norm = jnp.sqrt(
        block_square + jnp.sum(vector_total * vector_total) + jnp.sum(bias_total * bias_total)
    )
    factor_value = jnp.minimum(1.0, clip_limit / grad_norm)
    clipped_block_gradient = owned * factor_value
    left_new, right_new, master_new = shampoo(
        clipped_block_gradient, left_stats, right_stats, left_roots, right_roots, master_blocks
    )
    vector_grads = vector_total * factor_value
    vector_second_new, vector_new = adamw(vector_grads, vector_first, vector_second, vectors)
    bias_grads = bias_total * factor_value
    bias_second_new, bias_new = adamw(bias_grads, bias_first, bias_second, var_bias)
    return (
        loss_sum, count, grad_norm, clipped_block_gradient, left_new, right_new, master_new,
        vector_grads, vector_second_new, vector_new, bias_grads, bias_second_new, bias_new,
    )


def solution(mesh):
    rep = P()
    slot = P(("head", "tok"), None, None)
    return jax.shard_map(
        shards,
        mesh=mesh,
        in_specs=(
            P(None, "tok", "head", None), P(None, "tok", "head"), P(None, "tok", None), P(None, "tok", None),
            P(None, "tok", "head"), P(None, "tok", "head"), rep, slot, slot, slot, slot, slot,
            rep, rep, rep, rep, rep, rep,
        ),
        out_specs=(rep, rep, rep, slot, slot, slot, slot, rep, rep, rep, rep, rep, rep),
        check_vma=False,
    )
```

```python
import functools

import jax
import jax.numpy as jnp
import numpy as np
from jax import lax
from jax.experimental import pallas as pl
from jax.experimental.pallas import tpu as pltpu
from jax.sharding import PartitionSpec as P

D = 384
FF = 1024
HEADS = 6
HEAD_DIM = 64
PSIZES = 5
PMAX = 128
COMPS = 4
SEQ = 512
SIDE = 128
STEP = 10
HEADCOLS = 3 * COMPS * PMAX
BLOCKS = 159

norm_eps = 1e-06
scale_floor = 0.05
half_log_tau = 0.9189385332046727
clip_limit = 0.02
mat_rate = 0.01
vec_rate = 0.3
decay_rate = 0.01
beta_one = 0.9
beta_two = 0.95
stat_beta = 0.99
root_eps = 1e-06
adam_eps = 1e-08
highest = lax.Precision.HIGHEST
f32 = jnp.float32
bf16 = jnp.bfloat16

GRIDS = ((5, 3), (3, 12), (3, 9), (3, 3), (3, 16), (8, 3))
FIRSTS = (0, 15, 51, 78, 87, 135)
M_IN, M_HEAD, M_QKV, M_OUT, M_GU, M_DOWN = range(6)


def mm(a, b):
    return jnp.dot(a, b, preferred_element_type=f32)


def mm_nt(a, b):
    return lax.dot_general(a, b, (((1,), (1,)), ((), ())), preferred_element_type=f32)


def mm_tn(a, b):
    return lax.dot_general(a, b, (((0,), (0,)), ((), ())), preferred_element_type=f32)


def column_order():
    order = np.zeros((HEADCOLS, HEADCOLS), np.float32)
    for col in range(HEADCOLS):
        order[col, (col % (3 * COMPS)) * PMAX + col // (3 * COMPS)] = 1.0
    return order


SCRATCH = dict(
    w_in=((640, D), bf16), w_head=((D, HEADCOLS), bf16), w_qkv=((D, 3 * D), bf16), w_out=((D, D), bf16),
    w_gu=((D, 2 * FF), bf16), w_down=((FF, D), bf16), w_order=((HEADCOLS, HEADCOLS), bf16),
    w_headp=((D, HEADCOLS), bf16),
    g_in=((640, D), bf16), g_head=((D, HEADCOLS), bf16), g_qkv=((D, 3 * D), bf16), g_out=((D, D), bf16),
    g_gu=((D, 2 * FF), bf16), g_down=((FF, D), bf16), zero_block=((SIDE, SIDE), bf16),
    x5=((SEQ, 640), bf16), weight=((SEQ, PMAX), f32), cos_t=((SEQ, 128), f32), sin_t=((SEQ, 128), f32),
    code_t=((SEQ, SEQ), f32), probs=((HEADS, SEQ, SEQ), f32),
    stream=((SEQ, D), f32), middle=((SEQ, D), f32), last=((SEQ, D), f32), grad=((SEQ, D), f32), inner=((SEQ, D), f32),
    inv_a=((SEQ, 128), f32), inv_b=((SEQ, 128), f32), inv_f=((SEQ, 128), f32),
    normed_a=((SEQ, D), bf16), normed_b=((SEQ, D), bf16), normed_f=((SEQ, D), bf16),
    qs=((SEQ, D), bf16), ks=((SEQ, D), bf16), vs=((SEQ, D), bf16), merged=((SEQ, D), bf16),
    gate=((SEQ, FF), f32), upper=((SEQ, FF), f32), hidden=((SEQ, FF), bf16),
    params=((SEQ, HEADCOLS), f32), gparams=((SEQ, HEADCOLS), bf16), ggu=((SEQ, 2 * FF), bf16),
    rounded=((SEQ, D), bf16), dattn=((SEQ, D), bf16), dqkv=((SEQ, 3 * D), bf16), dscore=((SEQ, SEQ), bf16),
    loss_acc=((32, 128), f32), bias_acc=((16, 128), f32), vec_acc=((8, D), f32),
)


def tile(i, size):
    return pl.ds(pl.multiple_of(i * size, size), size)


def row_kernel(
    slots, lengths, bias, inv_count, patches, meta, vectors, freq, order, gathered, gout, small, *scratch
):
    s = type("S", (), dict(zip(SCRATCH, scratch)))
    marks, w_sem, o_sem, g_sem = scratch[len(SCRATCH) :]
    weights = (s.w_in, s.w_head, s.w_qkv, s.w_out, s.w_gu, s.w_down)
    grads = (s.g_in, s.g_head, s.g_qkv, s.g_out, s.g_gu, s.g_down)
    slot_count = gathered.shape[0]

    def load(m):
        rows, cols = GRIDS[m]

        @pl.loop(0, rows * cols)
        def _(i):
            pltpu.make_async_copy(
                gathered.at[slots[FIRSTS[m] + i]],
                weights[m].at[tile(i // cols, SIDE), tile(i % cols, SIDE)],
                w_sem.at[m],
            ).start()

    def loaded(m):
        pltpu.make_async_copy(weights[m], weights[m], w_sem.at[m]).wait()

    def send(m):
        rows, cols = GRIDS[m]

        @pl.loop(0, rows * cols)
        def _(i):
            pltpu.make_async_copy(
                grads[m].at[tile(i // cols, SIDE), tile(i % cols, SIDE)],
                gout.at[slots[FIRSTS[m] + i]],
                g_sem.at[m],
            ).start()

    for m in (M_IN, M_QKV, M_OUT, M_GU, M_DOWN, M_HEAD):
        load(m)
    order_copy = pltpu.make_async_copy(order, s.w_order, o_sem)
    order_copy.start()

    s.zero_block[...] = jnp.zeros_like(s.zero_block)

    @pl.loop(0, slot_count)
    def _(i):
        marks[i] = 0

    @pl.loop(0, BLOCKS)
    def _(b):
        marks[slots[b]] = 1

    @pl.loop(0, slot_count)
    def _(i):
        @pl.when(marks[i] == 0)
        def _():
            pltpu.make_async_copy(s.zero_block, gout.at[i], g_sem.at[6]).start()

    metaf = meta[...].astype(f32)
    columns = jnp.transpose(metaf)
    codes, times, flag = columns[:, 0:1], columns[:, 1:2], columns[:, 2:3] == 1.0
    position = lax.broadcasted_iota(jnp.int32, (1, SEQ), 1)
    ids = jnp.zeros((1, SEQ), f32)
    end = jnp.int32(0)
    for j in range(lengths.shape[0]):
        end = end + lengths[j]
        ids = ids + jnp.where(position >= end, 1.0, 0.0)
    variates = metaf[3:4]
    id_columns = jnp.transpose(jnp.concatenate([ids] * 8, axis=0))[:, 0:1]
    var_columns = columns[:, 3:4]
    for c in range(4):
        cs = slice(c * 128, (c + 1) * 128)
        same_sample = id_columns == ids[:, cs]
        same_var = var_columns == variates[:, cs]
        s.code_t[:, cs] = jnp.where(same_sample, jnp.where(same_var, 2.0, 1.0), 0.0)
    lane = lax.broadcasted_iota(jnp.int32, (1, 128), 1)
    first_half = lane % HEAD_DIM < HEAD_DIM // 2
    low_head = lane < HEAD_DIM
    angle = times * freq[0:1, :]
    s.cos_t[...] = jnp.cos(angle)
    s.sin_t[...] = jnp.where(first_half, -1.0, 1.0) * jnp.sin(angle)

    def turn(v, sine):
        swapped = jnp.where(first_half, pltpu.roll(v, 96, 1), pltpu.roll(v, 32, 1))
        return v * s.cos_t[...] + swapped * sine

    wide = patches[...].astype(f32)
    weight = jnp.zeros((SEQ, PMAX), f32)
    for c in range(PSIZES):
        keep = (codes == float(c)) & (lane < PMAX * 2**c // 2 ** (PSIZES - 1))
        s.x5[:, c * 128 : (c + 1) * 128] = jnp.where(keep, wide, 0.0).astype(bf16)
        weight = jnp.where(keep, 1.0, weight)
    s.weight[...] = jnp.where(flag, weight, 0.0)
    loaded(M_IN)
    s.stream[...] = jnp.where(flag, vectors[3:4, :], mm(s.x5[...], s.w_in[...]))

    def norm(src, inv_ref, gain, dst):
        @pl.loop(0, SEQ // 128)
        def _(i):
            rs = tile(i, 128)
            v = src[rs, :]
            inverse = lax.rsqrt(jnp.sum(v * v, axis=-1, keepdims=True) / D + norm_eps)
            inv_ref[rs, :] = jnp.broadcast_to(inverse, (128, 128))
            dst[rs, :] = (v * inverse * gain).astype(bf16)

    def norm_back(src, inv_ref, row, extra):
        gain = vectors[row : row + 1, :]

        @pl.loop(0, SEQ // 128)
        def _(i):
            rs = tile(i, 128)
            up = s.inner[rs, :]
            inverse = inv_ref[rs, 0:1]
            scaled = src[rs, :] * inverse
            inner = up * gain
            mean = jnp.sum(inner * scaled, axis=-1, keepdims=True) / D
            result = inverse * (inner - scaled * mean)
            s.grad[rs, :] = result if extra is None else result + extra[rs, :]
            s.vec_acc[row : row + 1, :] += jnp.sum(up * scaled, axis=0, keepdims=True)

    s.vec_acc[...] = jnp.zeros_like(s.vec_acc)
    norm(s.stream, s.inv_a, vectors[0:1, :], s.normed_a)
    loaded(M_QKV)
    for part, dst in ((0, s.qs), (1, s.ks), (2, s.vs)):
        mixed = mm(s.normed_a[...], s.w_qkv[:, part * D : (part + 1) * D])
        for c in range(3):
            piece = mixed[:, c * 128 : (c + 1) * 128]
            if part < 2:
                piece = turn(piece, s.sin_t[...])
            dst[:, c * 128 : (c + 1) * 128] = piece.astype(bf16)

    @pl.loop(0, HEADS // 2)
    def _(p):
        ps = tile(p, 128)
        qp, kp = s.qs[:, ps], s.ks[:, ps]
        vt = jnp.transpose(s.vs[:, ps])
        outs = []
        for hh in range(2):
            mine = low_head if hh == 0 else jnp.logical_not(low_head)
            qm = jnp.where(mine, qp.astype(f32) * HEAD_DIM**-0.5, 0.0).astype(bf16)
            b0 = bias[2 * p + hh]
            b1 = bias[HEADS + 2 * p + hh]
            parts = []
            for c in range(4):
                cs = slice(c * 128, (c + 1) * 128)
                code = s.code_t[:, cs]
                score = mm_nt(kp, qm[cs, :])
                score = jnp.where(code > 0.5, score + jnp.where(code > 1.5, b0, b1), -1e30)
                raised = jnp.exp(score - jnp.max(score, axis=0, keepdims=True))
                prob = raised * (1.0 / jnp.sum(raised, axis=0, keepdims=True))
                s.probs[2 * p + hh, :, cs] = prob
                parts.append(mm(vt[hh * 64 : (hh + 1) * 64, :], prob.astype(bf16)))
            outs.append(jnp.concatenate(parts, axis=1))
        s.merged[:, ps] = jnp.transpose(jnp.concatenate(outs, axis=0)).astype(bf16)

    loaded(M_OUT)
    s.middle[...] = s.stream[...] + mm(s.merged[...], s.w_out[...])
    norm(s.middle, s.inv_b, vectors[1:2, :], s.normed_b)
    loaded(M_GU)

    @pl.loop(0, FF // 256)
    def _(j):
        js = tile(j, 256)
        opening = mm(s.normed_b[...], s.w_gu[:, js])
        up = mm(s.normed_b[...], s.w_gu[:, tile(j + FF // 256, 256)])
        s.gate[:, js] = opening
        s.upper[:, js] = up
        s.hidden[:, js] = (opening * (1.0 / (1.0 + jnp.exp(-opening))) * up).astype(bf16)

    loaded(M_DOWN)
    s.last[...] = s.middle[...] + mm(s.hidden[...], s.w_down[...])
    norm(s.last, s.inv_f, vectors[2:3, :], s.normed_f)

    order_copy.wait()
    loaded(M_HEAD)

    @pl.loop(0, HEADCOLS // 256)
    def _(j):
        js = tile(j, 256)
        s.w_headp[:, js] = mm(s.w_head[...], s.w_order[:, js]).astype(bf16)
        s.params[:, js] = mm(s.normed_f[...], s.w_headp[:, js])

    inv_n = inv_count[0]
    s.loss_acc[...] = jnp.zeros_like(s.loss_acc)

    @pl.loop(0, SEQ // 32)
    def _(i):
        rs = tile(i, 32)
        y = patches[rs, :].astype(f32)
        weight = s.weight[rs, :]
        logits, means, raws = [
            [s.params[rs, (4 * kind + k) * 128 : (4 * kind + k + 1) * 128] for k in range(COMPS)] for kind in range(3)
        ]
        top = jnp.maximum(jnp.maximum(logits[0], logits[1]), jnp.maximum(logits[2], logits[3]))
        shifted = [v - top for v in logits]
        raised = [jnp.exp(v) for v in shifted]
        total = raised[0] + raised[1] + raised[2] + raised[3]
        log_total = jnp.log(total)
        inv_total = 1.0 / total
        terms, zs, inv_widths = [], [], []
        for k in range(COMPS):
            width = jnp.maximum(raws[k], 0.0) + jnp.log1p(jnp.exp(-jnp.abs(raws[k]))) + scale_floor
            inv_width = 1.0 / width
            z = (y - means[k]) * inv_width
            terms.append((shifted[k] - log_total) - 0.5 * z * z - jnp.log(width) - half_log_tau)
            zs.append(z)
            inv_widths.append(inv_width)
        best = jnp.maximum(jnp.maximum(terms[0], terms[1]), jnp.maximum(terms[2], terms[3]))
        lifted = [jnp.exp(t - best) for t in terms]
        lift_total = lifted[0] + lifted[1] + lifted[2] + lifted[3]
        inv_lift = 1.0 / lift_total
        s.loss_acc[...] += jnp.where(weight > 0.0, -(best + jnp.log(lift_total)), 0.0)
        scale = -(weight * inv_n)
        for k in range(COMPS):
            share = lifted[k] * inv_lift
            d_term = scale * share
            ratio = zs[k] * inv_widths[k]
            d_logit = scale * (share - raised[k] * inv_total)
            d_width = d_term * (zs[k] * ratio - inv_widths[k])
            sigma = 1.0 / (1.0 + jnp.exp(-raws[k]))
            for kind, value in ((0, d_logit), (1, d_term * ratio), (2, d_width * sigma)):
                at = (4 * kind + k) * 128
                s.gparams[rs, at : at + 128] = value.astype(bf16)

    @pl.loop(0, HEADCOLS // 256)
    def _(j):
        js = tile(j, 256)
        s.w_head[:, js] = mm_tn(s.normed_f[...], s.gparams[:, js]).astype(bf16)

    @pl.loop(0, HEADCOLS // 256)
    def _(j):
        js = tile(j, 256)
        s.g_head[:, js] = mm_nt(s.w_head[...], s.w_order[js, :]).astype(bf16)

    send(M_HEAD)
    s.inner[...] = mm_nt(s.gparams[...], s.w_headp[...])
    norm_back(s.last, s.inv_f, 2, None)

    s.rounded[...] = s.grad[...].astype(bf16)

    @pl.loop(0, FF // 256)
    def _(j):
        js = tile(j, 256)
        s.g_down[js, :] = mm_tn(s.hidden[:, js], s.rounded[...]).astype(bf16)
        up_grad = mm_nt(s.rounded[...], s.w_down[js, :])
        opening = s.gate[:, js]
        sigma = 1.0 / (1.0 + jnp.exp(-opening))
        s.ggu[:, js] = (up_grad * s.upper[:, js] * sigma * (1.0 + opening * (1.0 - sigma))).astype(bf16)
        s.ggu[:, tile(j + FF // 256, 256)] = (up_grad * opening * sigma).astype(bf16)

    send(M_DOWN)

    @pl.loop(0, 2 * FF // 256)
    def _(j):
        js = tile(j, 256)
        s.g_gu[:, js] = mm_tn(s.normed_b[...], s.ggu[:, js]).astype(bf16)

    send(M_GU)
    s.inner[...] = mm_nt(s.ggu[...], s.w_gu[...])
    norm_back(s.middle, s.inv_b, 1, s.grad)

    s.rounded[...] = s.grad[...].astype(bf16)
    s.g_out[...] = mm_tn(s.merged[...], s.rounded[...]).astype(bf16)
    send(M_OUT)
    s.dattn[...] = mm_nt(s.rounded[...], s.w_out[...]).astype(bf16)
    s.bias_acc[...] = jnp.zeros_like(s.bias_acc)

    @pl.loop(0, HEADS // 2)
    def _(p):
        ps = tile(p, 128)
        qp, kp, vp, dop = s.qs[:, ps], s.ks[:, ps], s.vs[:, ps], s.dattn[:, ps]
        kt = jnp.transpose(kp)
        dq, dk, dv = [], [], []
        for hh in range(2):
            mine = low_head if hh == 0 else jnp.logical_not(low_head)
            dom = jnp.where(mine, dop.astype(f32), 0.0).astype(bf16)
            same_sum = jnp.zeros((1, 128), f32)
            all_sum = jnp.zeros((1, 128), f32)
            for c in range(4):
                cs = slice(c * 128, (c + 1) * 128)
                prob = s.probs[2 * p + hh, :, cs]
                d_prob = mm_nt(vp, dom[cs, :])
                d_score = prob * (d_prob - jnp.sum(prob * d_prob, axis=0, keepdims=True))
                same_sum += jnp.sum(jnp.where(s.code_t[:, cs] > 1.5, d_score, 0.0), axis=0, keepdims=True)
                all_sum += jnp.sum(d_score, axis=0, keepdims=True)
                s.dscore[:, cs] = (d_score * HEAD_DIM**-0.5).astype(bf16)
            s.bias_acc[pl.ds(2 * p + hh, 1), :] = same_sum
            s.bias_acc[pl.ds(8 + 2 * p + hh, 1), :] = all_sum
            dv.append(mm(s.probs[2 * p + hh].astype(bf16), dop))
            dk.append(mm(s.dscore[...], qp))
            dq.append(mm(kt[hh * 64 : (hh + 1) * 64, :], s.dscore[...]))
        dqs = jnp.transpose(jnp.concatenate(dq, axis=0)).astype(bf16).astype(f32)
        dks = jnp.where(low_head, dk[0], dk[1]).astype(bf16).astype(f32)
        s.dqkv[:, ps] = turn(dqs, -s.sin_t[...]).astype(bf16)
        s.dqkv[:, tile(p + 3, 128)] = turn(dks, -s.sin_t[...]).astype(bf16)
        s.dqkv[:, tile(p + 6, 128)] = jnp.where(low_head, dv[0], dv[1]).astype(bf16)

    for j in range(3):
        js = slice(j * D, (j + 1) * D)
        s.g_qkv[:, js] = mm_tn(s.normed_a[...], s.dqkv[:, js]).astype(bf16)
    send(M_QKV)
    s.inner[...] = mm_nt(s.dqkv[...], s.w_qkv[...])
    norm_back(s.stream, s.inv_a, 0, s.grad)
    s.vec_acc[3:4, :] = jnp.sum(jnp.where(flag, s.grad[...], 0.0), axis=0, keepdims=True)
    s.rounded[...] = jnp.where(flag, 0.0, s.grad[...]).astype(bf16)
    s.g_in[...] = mm_tn(s.x5[...], s.rounded[...]).astype(bf16)
    send(M_IN)

    sums = jnp.sum(s.bias_acc[...], axis=1, keepdims=True)
    sums = jnp.concatenate([sums[0:8], sums[8:16] - sums[0:8]], axis=0)
    diagonal = lax.broadcasted_iota(jnp.int32, (16, D), 0) == lax.broadcasted_iota(jnp.int32, (16, D), 1)
    bias_row = jnp.sum(jnp.where(diagonal, sums, 0.0), axis=0, keepdims=True)
    row = lax.broadcasted_iota(jnp.int32, (8, D), 0)
    small[...] = jnp.where(row == 4, jnp.sum(s.loss_acc[...]), jnp.where(row == 5, bias_row, s.vec_acc[...]))

    for m in range(6):
        pltpu.make_async_copy(grads[m], grads[m], g_sem.at[m]).wait()

    @pl.loop(0, slot_count)
    def _(i):
        @pl.when(marks[i] == 0)
        def _():
            pltpu.make_async_copy(s.zero_block, gout.at[i], g_sem.at[6]).wait()


def row_step(slots, lengths, bias, inv_count, patches, meta, vectors, gathered):
    freq = 10000.0 ** (-jnp.arange(HEAD_DIM // 2, dtype=f32) / (HEAD_DIM // 2))
    freq = jnp.tile(freq[None], (8, 4))
    smem = pl.BlockSpec(memory_space=pltpu.SMEM)
    vmem = pl.BlockSpec(memory_space=pltpu.VMEM)
    hbm = pl.BlockSpec(memory_space=pl.ANY)
    return pl.pallas_call(
        row_kernel,
        out_shape=(
            jax.ShapeDtypeStruct(gathered.shape, bf16),
            jax.ShapeDtypeStruct((8, D), f32),
        ),
        in_specs=[smem] * 4 + [vmem] * 4 + [hbm] * 2,
        out_specs=(hbm, vmem),
        scratch_shapes=[pltpu.VMEM(shape, dtype) for shape, dtype in SCRATCH.values()]
        + [
            pltpu.SMEM((gathered.shape[0],), jnp.int32),
            pltpu.SemaphoreType.DMA((6,)),
            pltpu.SemaphoreType.DMA,
            pltpu.SemaphoreType.DMA((7,)),
        ],
        compiler_params=pltpu.CompilerParams(vmem_limit_bytes=62 * 2**20),
        name="row",
    )(slots, lengths, bias, inv_count, patches, meta, vectors, freq, jnp.asarray(column_order(), bf16), gathered)


MESH = pl.DeviceIdType.MESH


def tok_dims(count):
    return {16: (4, 2, 2), 128: (4, 4, 8)}.get(count, (count, 1, 1))


class Place:
    def __init__(self, dims):
        self.dims = dims
        self.head = lax.axis_index("head")
        tok = lax.axis_index("tok")
        self.tok = tok
        self.strides = (dims[1] * dims[2], dims[2], 1)
        self.at = [lax.rem(lax.div(tok, s), n) for s, n in zip(self.strides, dims)]

    def coordinate(self, axis, step):
        return lax.rem(self.at[axis] + step, self.dims[axis])

    def peer(self, axis, step):
        return (self.head, self.tok + (self.coordinate(axis, step) - self.at[axis]) * self.strides[axis])

    def partner(self):
        return (1 - self.head, self.tok)

    def greet(self):
        barrier = pltpu.get_barrier_semaphore()
        others = [self.partner()] + [self.peer(a, j) for a in range(3) for j in range(1, self.dims[a])]
        for other in others:
            pl.semaphore_signal(barrier, inc=1, device_id=other, device_id_type=MESH)
        pl.semaphore_wait(barrier, len(others))

    def region(self, whole, fixed=None):
        fixed = fixed or {}
        return tuple(slice(None) if a in whole else fixed.get(a, self.at[a]) for a in range(3))


def remote(src, dst, send, recv, device):
    return pltpu.make_async_remote_copy(
        src_ref=src, dst_ref=dst, send_sem=send, recv_sem=recv, device_id=device, device_id_type=MESH
    )


def split_rows(rows, shares):
    units = rows // 16
    edges = [round(units * sum(shares[:i]) / sum(shares)) * 16 for i in range(len(shares) + 1)]
    return [(a, b - a) for a, b in zip(edges, edges[1:])]


def all_sum(place, values, buf, send, recv):
    steps = [None] + [a for a in range(3) if place.dims[a] > 1]
    total = values
    for k, axis in enumerate(steps):
        buf[k, 0] = total
        if axis is None:
            others = [place.partner()]
        else:
            others = [place.peer(axis, j) for j in range(1, place.dims[axis])]
        copies = [
            remote(buf.at[k, 0], buf.at[k, 1 + i], send.at[k, i], recv.at[k, i], other)
            for i, other in enumerate(others)
        ]
        for copy in copies:
            copy.start()
        yield None
        for copy in copies:
            copy.wait()
        for i in range(len(copies)):
            total = total + buf[k, 1 + i]
    yield total


def sum_shapes(dims, shape):
    most = max(max(dims), 2)
    return [
        pltpu.VMEM((4, most) + shape, f32),
        pltpu.SemaphoreType.DMA((4, most)),
        pltpu.SemaphoreType.DMA((4, most)),
    ]


GATHER_PARTS = (((0, 1, 2), 3), ((0, 2, 1), 3), ((2, 1, 0), 1), ((1, 2, 0), 1))


def gather_kernel(
    dims, master, patches, ints,
    gathered, row_patches, meta, count,
    mine, own_patch, land_patch, land_ints, sum_buf, sum_send, sum_recv, own_sem, send, recv, cross_send, cross_recv, swap_sem,
):
    place = Place(dims)
    rows = mine.shape[0]
    head = place.head
    place.greet()
    swaps = [
        remote(patches.at[1 - head, 0], land_patch, swap_sem.at[0], swap_sem.at[1], place.partner()),
        remote(ints.at[1 - head], land_ints, swap_sem.at[2], swap_sem.at[3], place.partner()),
    ]
    mine[...] = master[...].reshape(rows, SIDE).astype(bf16)
    parts = [(order, a, n) for (order, _), (a, n) in zip(GATHER_PARTS, split_rows(rows, [s for _, s in GATHER_PARTS])) if n]

    def block(head_index, whole, fixed, a, n):
        return gathered.at[(head_index,) + place.region(whole, fixed) + (pl.ds(a, n),)]

    started = []
    cross = []

    def start_phase(p, k):
        order, a, n = parts[p]
        axis, whole = order[k], order[:k]
        result = []
        for j in range(1, dims[axis]):
            src = mine.at[pl.ds(a, n)] if k == 0 else block(head, whole, None, a, n)
            copy = remote(src, block(head, whole, None, a, n), send.at[p, k, j], recv.at[p, k, j], place.peer(axis, j))
            copy.start()
            result.append(copy)
        started.extend(result)
        return result

    def start_cross(p, k):
        order, a, n = parts[p]
        if k == 0:
            views = [(mine.at[pl.ds(a, n)], block(head, (), None, a, n))]
        else:
            axis, whole = order[k - 1], order[: k - 1]
            views = []
            for j in range(1, dims[axis]):
                view = block(head, whole, {axis: place.coordinate(axis, dims[axis] - j)}, a, n)
                views.append((view, view))
        for j, (src, dst) in enumerate(views):
            copy = remote(src, dst, cross_send.at[p, k, j], cross_recv.at[p, k, j], place.partner())
            copy.start()
            cross.append(copy)

    current = [start_phase(p, 0) for p in range(len(parts))]
    own = pltpu.make_async_copy(mine, gathered.at[(head,) + place.region(())], own_sem)
    own.start()
    for copy in swaps:
        copy.start()
    codes, predict = ints[:, 0, :], ints[:, 2, :]
    sizes = jnp.zeros_like(codes)
    for c in range(PSIZES):
        sizes = sizes + jnp.where(codes == c, PMAX * 2**c // 2 ** (PSIZES - 1), 0)
    partial = (sizes * predict).astype(f32)
    partial = jnp.sum(partial[:, :128] + partial[:, 128:], axis=0, keepdims=True)
    counting = all_sum(place, jnp.concatenate([partial, jnp.zeros((7, 128), f32)], axis=0), sum_buf, sum_send, sum_recv)
    total = next(counting)
    for p in range(len(parts)):
        start_cross(p, 0)
    own.wait()
    for k in range(3):
        for p in range(len(parts)):
            for copy in current[p]:
                copy.wait_recv()
            if k < 2:
                current[p] = start_phase(p, k + 1)
            start_cross(p, k + 1)
        if total is None:
            total = next(counting)
    while total is None:
        total = next(counting)
    count[...] = jnp.broadcast_to(jnp.sum(total), count.shape)
    for copy in swaps:
        copy.wait()
    for h in range(2):

        @pl.when(head == h)
        def _():
            here, there = slice(h * 256, h * 256 + 256), slice((1 - h) * 256, (1 - h) * 256 + 256)
            row_patches[here, :] = patches[h, 0]
            row_patches[there, :] = land_patch[...]
            meta[:, here] = ints[h]
            meta[:, there] = land_ints[...]

    for copy in started:
        copy.wait_send()
    for copy in cross:
        copy.wait()


def gather_step(dims, master, patches, ints):
    slots = master.shape[0]
    rows = slots * SIDE
    parts = len(GATHER_PARTS)
    most = max(dims)
    vmem = pl.BlockSpec(memory_space=pltpu.VMEM)
    half = patches.shape[2]
    gathered, row_patches, meta, count = pl.pallas_call(
        functools.partial(gather_kernel, dims),
        out_shape=(
            jax.ShapeDtypeStruct((2,) + dims + (rows, SIDE), bf16),
            jax.ShapeDtypeStruct((2 * half, PMAX), bf16),
            jax.ShapeDtypeStruct((8, 2 * half), jnp.int32),
            jax.ShapeDtypeStruct((8, 128), f32),
        ),
        in_specs=[vmem] * 3,
        out_specs=(pl.BlockSpec(memory_space=pl.ANY), vmem, vmem, vmem),
        scratch_shapes=[
            pltpu.VMEM((rows, SIDE), bf16),
            pltpu.VMEM((8, 128), bf16),
            pltpu.VMEM((half, PMAX), bf16),
            pltpu.VMEM((8, half), jnp.int32),
            *sum_shapes(dims, (8, 128)),
            pltpu.SemaphoreType.DMA,
            pltpu.SemaphoreType.DMA((parts, 3, most)),
            pltpu.SemaphoreType.DMA((parts, 3, most)),
            pltpu.SemaphoreType.DMA((parts, 4, most)),
            pltpu.SemaphoreType.DMA((parts, 4, most)),
            pltpu.SemaphoreType.DMA((4,)),
        ],
        compiler_params=pltpu.CompilerParams(
            collective_id=0, has_side_effects=True, vmem_limit_bytes=32 * 2**20
        ),
        name="gather",
    )(master, patches, ints)
    return gathered.reshape(-1, SIDE, SIDE), row_patches, meta, count[0, 0]


REDUCE_PARTS = (((2, 1, 0), 3), ((1, 2, 0), 3), ((0, 1, 2), 1), ((0, 2, 1), 1))


def reduce_kernel(
    dims, grads, small,
    owned, small_total, square,
    acc, local, crossed, *rest,
):
    parts_count = len(REDUCE_PARTS)
    landing = rest[: 3 * parts_count]
    (vec_buf, vec_send, vec_recv, sq_buf, sq_send, sq_recv, local_sem, send, recv, cross_send, cross_recv) = rest[3 * parts_count :]
    place = Place(dims)
    head = place.head
    rows = owned.shape[0]
    parts = [(order, a, n) for (order, _), (a, n) in zip(REDUCE_PARTS, split_rows(rows, [s for _, s in REDUCE_PARTS]))]
    live = [p for p in range(parts_count) if parts[p][2]]
    everywhere = (slice(None),) * 3
    place.greet()
    crossing, loading = {}, {}
    for p in live:
        _, a, n = parts[p]
        view = (pl.ds(a, n),)
        crossing[p] = remote(
            grads.at[(1 - head,) + everywhere + view], crossed.at[everywhere + view], cross_send.at[p], cross_recv.at[p], place.partner()
        )
        crossing[p].start()
        loading[p] = pltpu.make_async_copy(
            grads.at[(head,) + everywhere + view], local.at[everywhere + view], local_sem.at[p]
        )
        loading[p].start()
    vec_sum = all_sum(place, small[...], vec_buf, vec_send, vec_recv)
    vec_total = next(vec_sum)

    started = []
    current = {}

    def start_phase(p, k):
        order, a, n = parts[p]
        axis, left = order[k], order[k + 1 :]
        current[p] = []
        for j in range(1, dims[axis]):
            src = acc.at[place.region(left, {axis: place.coordinate(axis, j)}) + (pl.ds(a, n),)]
            copy = remote(src, landing[3 * p + k].at[j - 1], send.at[p, k, j], recv.at[p, k, j], place.peer(axis, j))
            copy.start()
            current[p].append(copy)
        started.extend(current[p])

    def add_up(p, k):
        order, a, n = parts[p]
        left = order[k + 1 :]
        region = place.region(left)
        steps = [dims[i] for i in sorted(left)]
        for copy in current[p]:
            copy.wait_recv()

        def body(*index):
            full = tuple(index[sorted(left).index(i)] if i in left else region[i] for i in range(3))
            value = acc[full + (pl.ds(a, n),)].astype(f32)
            for j in range(1, dims[order[k]]):
                value = value + landing[3 * p + k][(j - 1,) + index].astype(f32)
            if k < 2:
                acc[full + (pl.ds(a, n),)] = value.astype(bf16)
            else:
                owned[a : a + n, :] = value

        if k == 2:
            body()
        elif k == 1:
            pl.loop(0, steps[0])(body)
        else:

            @pl.loop(0, steps[0])
            def _(i):
                pl.loop(0, steps[1])(lambda j: body(i, j))

    for p in live:
        _, a, n = parts[p]
        loading[p].wait()
        crossing[p].wait_recv()

        @pl.loop(0, dims[0])
        def _(i):
            @pl.loop(0, dims[1])
            def _(j):
                for m in range(dims[2]):
                    at = (i, j, m, pl.ds(a, n))
                    acc[at] = (local[at].astype(f32) + crossed[at].astype(f32)).astype(bf16)

        start_phase(p, 0)
    for k in range(3):
        for p in live:
            add_up(p, k)
            if k < 2:
                start_phase(p, k + 1)
        if vec_total is None:
            vec_total = next(vec_sum)
    while vec_total is None:
        vec_total = next(vec_sum)
    small_total[...] = vec_total
    part_square = jnp.zeros((8, 128), f32)
    for a in range(0, rows, 128):
        piece = owned[a : a + 128, :]
        part_square = part_square + jnp.sum((piece * piece).reshape(16, 8, 128), axis=0)
    sq_sum = all_sum(place, part_square, sq_buf, sq_send, sq_recv)
    total = None
    while total is None:
        total = next(sq_sum)
    square[...] = jnp.broadcast_to(jnp.sum(total), (8, 128))
    for copy in started:
        copy.wait_send()
    for p in live:
        crossing[p].wait_send()


def reduce_step(dims, grads, small):
    slots = grads.shape[0] // (2 * dims[0] * dims[1] * dims[2])
    rows = slots * SIDE
    vmem = pl.BlockSpec(memory_space=pltpu.VMEM)
    most = max(dims)
    parts = split_rows(rows, [s for _, s in REDUCE_PARTS])
    landing = []
    for (order, _), (_, n) in zip(REDUCE_PARTS, parts):
        for k in range(3):
            left = [dims[i] for i in sorted(order[k + 1 :])]
            landing.append(pltpu.VMEM((max(dims[order[k]] - 1, 1), *left, max(n, 16), SIDE), bf16))
    sems = pltpu.SemaphoreType.DMA
    return pl.pallas_call(
        functools.partial(reduce_kernel, dims),
        out_shape=(
            jax.ShapeDtypeStruct((rows, SIDE), f32),
            jax.ShapeDtypeStruct(small.shape, f32),
            jax.ShapeDtypeStruct((8, 128), f32),
        ),
        in_specs=[pl.BlockSpec(memory_space=pl.ANY), vmem],
        out_specs=(vmem, vmem, vmem),
        scratch_shapes=[
            *[pltpu.VMEM(dims + (rows, SIDE), bf16)] * 3,
            *landing,
            *sum_shapes(dims, small.shape),
            *sum_shapes(dims, (8, 128)),
            sems((len(parts),)),
            sems((len(parts), 3, most)),
            sems((len(parts), 3, most)),
            sems((len(parts),)),
            sems((len(parts),)),
        ],
        compiler_params=pltpu.CompilerParams(
            collective_id=1, has_side_effects=True, vmem_limit_bytes=48 * 2**20
        ),
        name="reduce",
    )(grads.reshape((2,) + dims + (rows, SIDE)), small)


def shampoo(gradients, left, right, left_root, right_root, master):
    left_next = stat_beta * left + (1.0 - stat_beta) * jnp.einsum(
        "sij,skj->sik", gradients, gradients, precision=highest
    )
    right_next = stat_beta * right + (1.0 - stat_beta) * jnp.einsum(
        "sji,sjk->sik", gradients, gradients, precision=highest
    )
    shaped = jnp.einsum("sij,sjk->sik", left_root, gradients, precision=highest)
    shaped = jnp.einsum("sij,sjk->sik", shaped, right_root, precision=highest)
    unit = shaped * lax.rsqrt(jnp.mean(shaped * shaped, axis=(1, 2), keepdims=True) + root_eps)
    return (left_next, right_next, master - mat_rate * (unit + decay_rate * master))


def adamw(gradients, first_moment, second_moment, values):
    first_next = beta_one * first_moment + (1.0 - beta_one) * gradients
    second_next = beta_two * second_moment + (1.0 - beta_two) * gradients * gradients
    ratio = (
        first_next
        / (1.0 - beta_one**STEP)
        / (jnp.sqrt(second_next / (1.0 - beta_two**STEP)) + adam_eps)
    )
    return (second_next, values - vec_rate * (ratio + decay_rate * values))


def shards(
    dims,
    patches, patch_sizes, sample_lengths, variate_ids, time_ids, predict_mask, block_owner_slot,
    master_blocks, left_stats, right_stats, left_roots, right_roots,
    vectors, vector_first, vector_second, var_bias, bias_first, bias_second,
):
    head = lax.axis_index("head")
    mine = lax.dynamic_slice_in_dim(variate_ids, head * (SEQ // 2), SEQ // 2, 2)
    ints = jnp.concatenate([patch_sizes, time_ids, predict_mask, mine] + [jnp.zeros_like(mine)] * 4, axis=1)
    gathered, row_patches, meta, count = gather_step(dims, master_blocks, patches, ints)
    lengths = lax.dynamic_index_in_dim(sample_lengths, head, 0, False)[0]
    grad_slots, small = row_step(
        block_owner_slot, lengths, var_bias[0], (1.0 / count)[None], row_patches, meta, vectors, gathered
    )
    owned, small_total, square = reduce_step(dims, grad_slots, small)
    owned = owned.reshape(master_blocks.shape)
    vector_total = small_total[0:4]
    loss_sum = small_total[4, 0]
    bias_total = jnp.concatenate([small_total[5, 0:HEADS], small_total[5, 8 : 8 + HEADS]])[None]
    block_square = square[0, 0]
    grad_norm = jnp.sqrt(
        block_square + jnp.sum(vector_total * vector_total) + jnp.sum(bias_total * bias_total)
    )
    factor_value = jnp.minimum(1.0, clip_limit / grad_norm)
    clipped_block_gradient = owned * factor_value
    left_new, right_new, master_new = shampoo(
        clipped_block_gradient, left_stats, right_stats, left_roots, right_roots, master_blocks
    )
    vector_grads = vector_total * factor_value
    vector_second_new, vector_new = adamw(vector_grads, vector_first, vector_second, vectors)
    bias_grads = bias_total * factor_value
    bias_second_new, bias_new = adamw(bias_grads, bias_first, bias_second, var_bias)
    return (
        loss_sum, count, grad_norm, clipped_block_gradient, left_new, right_new, master_new,
        vector_grads, vector_second_new, vector_new, bias_grads, bias_second_new, bias_new,
    )


def solution(mesh):
    rep = P()
    dims = tok_dims(mesh.shape["tok"])
    slot = P(("head", "tok"), None, None)
    return jax.shard_map(
        functools.partial(shards, dims),
        mesh=mesh,
        in_specs=(
            P(None, "tok", "head", None), P(None, "tok", "head"), P(None, "tok", None), P(None, "tok", None),
            P(None, "tok", "head"), P(None, "tok", "head"), rep, slot, slot, slot, slot, slot,
            rep, rep, rep, rep, rep, rep,
        ),
        out_specs=(rep, rep, rep, slot, slot, slot, slot, rep, rep, rep, rep, rep, rep),
        check_vma=False,
    )
```

```python
import functools

import jax
import jax.numpy as jnp
import numpy as np
from jax import lax
from jax.experimental import pallas as pl
from jax.experimental.pallas import tpu as pltpu
from jax.sharding import PartitionSpec as P

D = 384
FF = 1024
HEADS = 6
HEAD_DIM = 64
PSIZES = 5
PMAX = 128
COMPS = 4
SEQ = 512
SIDE = 128
STEP = 10
HEADCOLS = 3 * COMPS * PMAX
BLOCKS = 159

norm_eps = 1e-06
scale_floor = 0.05
half_log_tau = 0.9189385332046727
clip_limit = 0.02
mat_rate = 0.01
vec_rate = 0.3
decay_rate = 0.01
beta_one = 0.9
beta_two = 0.95
stat_beta = 0.99
root_eps = 1e-06
adam_eps = 1e-08
highest = lax.Precision.HIGHEST
f32 = jnp.float32
bf16 = jnp.bfloat16

GRIDS = ((5, 3), (3, 12), (3, 9), (3, 3), (3, 16), (8, 3))
FIRSTS = (0, 15, 51, 78, 87, 135)
M_IN, M_HEAD, M_QKV, M_OUT, M_GU, M_DOWN = range(6)


def mm(a, b):
    return jnp.dot(a, b, preferred_element_type=f32)


def mm_nt(a, b):
    return lax.dot_general(a, b, (((1,), (1,)), ((), ())), preferred_element_type=f32)


def mm_tn(a, b):
    return lax.dot_general(a, b, (((0,), (0,)), ((), ())), preferred_element_type=f32)


GROUP = 384


def group_order():
    order = np.zeros((GROUP, GROUP), np.float32)
    for col in range(GROUP):
        order[col, (col % 12) * 32 + col // 12] = 1.0
    return order


def swap_quarters(parts):
    lane = lax.broadcasted_iota(jnp.int32, (1, 128), 1)
    low, even = lane < 64, lane % 64 < 32
    a, b, c, d = parts
    a, c = jnp.where(low, a, pltpu.roll(c, 64, 1)), jnp.where(low, pltpu.roll(a, 64, 1), c)
    b, d = jnp.where(low, b, pltpu.roll(d, 64, 1)), jnp.where(low, pltpu.roll(b, 64, 1), d)
    a, b = jnp.where(even, a, pltpu.roll(b, 32, 1)), jnp.where(even, pltpu.roll(a, 96, 1), b)
    c, d = jnp.where(even, c, pltpu.roll(d, 32, 1)), jnp.where(even, pltpu.roll(c, 96, 1), d)
    return a, b, c, d


SCRATCH = dict(
    w_in=((640, D), bf16), w_head=((D, HEADCOLS), bf16), w_qkv=((D, 3 * D), bf16), w_out=((D, D), bf16),
    w_gu=((D, 2 * FF), bf16), w_down=((FF, D), bf16), w_headp=((D, HEADCOLS), bf16),
    blocks=((BLOCKS + 1, SIDE, SIDE), bf16),
    x5=((SEQ, 640), bf16), weight=((SEQ, PMAX), f32), flag=((SEQ, 128), f32),
    cos_t=((SEQ, 128), f32), sin_t=((SEQ, 128), f32),
    code_t=((SEQ, SEQ), f32), probs=((HEADS, SEQ, SEQ), f32),
    stream=((SEQ, D), f32), middle=((SEQ, D), f32), last=((SEQ, D), f32), grad=((SEQ, D), f32), inner=((SEQ, D), f32),
    inv_a=((SEQ, 128), f32), inv_b=((SEQ, 128), f32), inv_f=((SEQ, 128), f32),
    normed=((SEQ, D), bf16), na_t=((D, SEQ), bf16), nb_t=((D, SEQ), bf16), nf_t=((D, SEQ), bf16),
    qs=((SEQ, D), bf16), ks=((SEQ, D), bf16), vs=((SEQ, D), bf16), merged=((SEQ, D), bf16), merged_t=((D, SEQ), bf16),
    gate=((SEQ, FF), f32), upper=((SEQ, FF), f32), hidden=((SEQ, FF), bf16),
    params=((SEQ, HEADCOLS), f32), gparams=((SEQ, HEADCOLS), bf16), ggu=((SEQ, 2 * FF), bf16),
    dqkv=((SEQ, 3 * D), bf16), dscore=((SEQ, SEQ), bf16),
    loss_acc=((32, 128), f32), bias_acc=((16, 128), f32), vec_acc=((8, D), f32),
    meta=((8, SEQ), jnp.int32), row_patches=((SEQ, PMAX), bf16),
)


def tile(i, size):
    return pl.ds(pl.multiple_of(i * size, size), size)


MESH = pl.DeviceIdType.MESH


def tok_dims(count):
    return {16: (4, 2, 2), 128: (4, 4, 8)}.get(count, (count, 1, 1))


class Place:
    def __init__(self, dims):
        self.dims = dims
        self.head = lax.axis_index("head")
        tok = lax.axis_index("tok")
        self.tok = tok
        self.strides = (dims[1] * dims[2], dims[2], 1)
        self.at = [lax.rem(lax.div(tok, s), n) for s, n in zip(self.strides, dims)]

    def coordinate(self, axis, step):
        return lax.rem(self.at[axis] + step, self.dims[axis])

    def peer(self, axis, step):
        return (self.head, self.tok + (self.coordinate(axis, step) - self.at[axis]) * self.strides[axis])

    def partner(self):
        return (1 - self.head, self.tok)

    def greet(self):
        barrier = pltpu.get_barrier_semaphore()
        others = [self.partner()] + [self.peer(a, j) for a in range(3) for j in range(1, self.dims[a])]
        for other in others:
            pl.semaphore_signal(barrier, inc=1, device_id=other, device_id_type=MESH)
        pl.semaphore_wait(barrier, len(others))

    def region(self, whole, fixed=None):
        fixed = fixed or {}
        return tuple(slice(None) if a in whole else fixed.get(a, self.at[a]) for a in range(3))


def remote(src, dst, send, recv, device):
    return pltpu.make_async_remote_copy(
        src_ref=src, dst_ref=dst, send_sem=send, recv_sem=recv, device_id=device, device_id_type=MESH
    )


def split_rows(rows, shares):
    units = rows // 16
    edges = [round(units * sum(shares[:i]) / sum(shares)) * 16 for i in range(len(shares) + 1)]
    return [(a, b - a) for a, b in zip(edges, edges[1:])]


def all_sum(place, values, buf, send, recv):
    steps = [None] + [a for a in range(3) if place.dims[a] > 1]
    total = values
    for k, axis in enumerate(steps):
        buf[k, 0] = total
        if axis is None:
            others = [place.partner()]
        else:
            others = [place.peer(axis, j) for j in range(1, place.dims[axis])]
        copies = [
            remote(buf.at[k, 0], buf.at[k, 1 + i], send.at[k, i], recv.at[k, i], other)
            for i, other in enumerate(others)
        ]
        for copy in copies:
            copy.start()
        yield None
        for copy in copies:
            copy.wait()
        for i in range(len(copies)):
            total = total + buf[k, 1 + i]
    yield total


def sum_shapes(dims, shape):
    most = max(max(dims), 2)
    return [
        pltpu.VMEM((4, most) + shape, f32),
        pltpu.SemaphoreType.DMA((4, most)),
        pltpu.SemaphoreType.DMA((4, most)),
    ]


GATHER_PARTS = (((0, 1, 2), 3), ((0, 2, 1), 3), ((2, 1, 0), 1), ((1, 2, 0), 1))
REDUCE_PARTS = (((2, 1, 0), 3), ((1, 2, 0), 3), ((0, 1, 2), 1), ((0, 2, 1), 1))


def cut_parts(table):
    return [(order, a, n) for (order, _), (a, n) in zip(table, split_rows(SIDE, [s for _, s in table])) if n]


def step_kernel(
    dims, places, holder, lengths, bias, master, patches, sizes, times_in, predict_in, variates_in, vectors, freq, order,
    owned, small_total, square, count_out, *rest,
):
    names = list(SCRATCH)
    s = type("S", (), dict(zip(names, rest)))
    rest = rest[len(names) :]
    mine, gathered, crossed, land_patch, land_ints, own_ints = rest[:6]
    (cnt_buf, cnt_send, cnt_recv, vec_buf, vec_send, vec_recv, sq_buf, sq_send, sq_recv) = rest[6:15]
    own_sem, send, recv, cross_send, cross_recv, swap_sem, r_send, r_recv, rc_send, rc_recv = rest[15:25]
    landing = rest[25:]
    place = Place(dims)
    per = mine.shape[0]
    head = place.head
    lane = lax.broadcasted_iota(jnp.int32, (1, 128), 1)
    first_half = lane % HEAD_DIM < HEAD_DIM // 2
    low_head = lane < HEAD_DIM
    weights = (s.w_in, s.w_head, s.w_qkv, s.w_out, s.w_gu, s.w_down)

    def keep(m, r0, c0, value):
        value = value.astype(bf16)
        cols = GRIDS[m][1]
        for r in range(value.shape[0] // SIDE):
            for c in range(value.shape[1] // SIDE):
                piece = value[r * SIDE : (r + 1) * SIDE, c * SIDE : (c + 1) * SIDE]
                s.blocks[FIRSTS[m] + (r0 + r) * cols + c0 + c] = piece

    place.greet()
    for k, ref in enumerate((sizes, times_in, predict_in)):
        own_ints[k, :, :] = ref[:, 0, :]
    swaps = [
        remote(patches.at[1 - head, 0], land_patch, swap_sem.at[0], swap_sem.at[1], place.partner()),
        remote(own_ints, land_ints, swap_sem.at[2], swap_sem.at[3], place.partner()),
    ]
    for copy in swaps:
        copy.start()
    mine[...] = master[...].astype(bf16)
    parts = cut_parts(GATHER_PARTS)

    def block(head_index, whole, fixed, a, n):
        return gathered.at[(head_index,) + place.region(whole, fixed) + (slice(None), pl.ds(a, n))]

    started, cross = [], []

    def start_phase(p, k):
        axes, a, n = parts[p]
        axis, whole = axes[k], axes[:k]
        result = []
        for j in range(1, dims[axis]):
            src = mine.at[:, pl.ds(a, n)] if k == 0 else block(head, whole, None, a, n)
            copy = remote(src, block(head, whole, None, a, n), send.at[p, k, j], recv.at[p, k, j], place.peer(axis, j))
            copy.start()
            result.append(copy)
        started.extend(result)
        return result

    def start_cross(p, k):
        axes, a, n = parts[p]
        if k == 0:
            views = [(mine.at[:, pl.ds(a, n)], block(head, (), None, a, n))]
        else:
            axis, whole = axes[k - 1], axes[: k - 1]
            views = []
            for j in range(1, dims[axis]):
                view = block(head, whole, {axis: place.coordinate(axis, dims[axis] - j)}, a, n)
                views.append((view, view))
        for j, (src, dst) in enumerate(views):
            copy = remote(src, dst, cross_send.at[p, k, j], cross_recv.at[p, k, j], place.partner())
            copy.start()
            cross.append(copy)

    current = [start_phase(p, 0) for p in range(len(parts))]
    own = pltpu.make_async_copy(mine, gathered.at[(head,) + place.region(())], own_sem)
    own.start()
    wide_size = jnp.zeros_like(own_ints[0])
    for c in range(PSIZES):
        wide_size = wide_size + jnp.where(own_ints[0] == c, PMAX * 2**c // 2 ** (PSIZES - 1), 0)
    partial = (wide_size * own_ints[2]).astype(f32)
    partial = jnp.sum(partial[:, :128] + partial[:, 128:], axis=0, keepdims=True)
    counting = all_sum(place, jnp.concatenate([partial, jnp.zeros((7, 128), f32)], axis=0), cnt_buf, cnt_send, cnt_recv)
    counted = next(counting)
    for p in range(len(parts)):
        start_cross(p, 0)
    own.wait()
    for copy in swaps:
        copy.wait()
    half = SEQ // 2
    for h in range(2):

        @pl.when(head == h)
        def _():
            here, there = slice(h * half, (h + 1) * half), slice((1 - h) * half, (2 - h) * half)
            s.row_patches[here, :] = patches[h, 0]
            s.row_patches[there, :] = land_patch[...]
            for k in range(3):
                s.meta[k : k + 1, here] = own_ints[k, h : h + 1, :]
                s.meta[k : k + 1, there] = land_ints[k, h : h + 1, :]
            s.meta[3:4, :] = variates_in[h]

    s.meta[4:8, :] = jnp.zeros((4, SEQ), jnp.int32)

    def prepare_tokens():
        metaf = s.meta[...].astype(f32)
        columns = jnp.transpose(metaf)
        codes, times, flag = columns[:, 0:1], columns[:, 1:2], columns[:, 2:3]
        position = lax.broadcasted_iota(jnp.int32, (1, SEQ), 1)
        ids = jnp.zeros((1, SEQ), f32)
        end = jnp.int32(0)
        for j in range(lengths.shape[2]):
            end = end + lengths[head, 0, j]
            ids = ids + jnp.where(position >= end, 1.0, 0.0)
        variates = metaf[3:4]
        id_columns = jnp.transpose(jnp.concatenate([ids] * 8, axis=0))[:, 0:1]
        var_columns = columns[:, 3:4]
        for c in range(4):
            cs = slice(c * 128, (c + 1) * 128)
            same_sample = id_columns == ids[:, cs]
            same_var = var_columns == variates[:, cs]
            s.code_t[:, cs] = jnp.where(same_sample, jnp.where(same_var, 2.0, 1.0), 0.0)
        s.flag[...] = jnp.broadcast_to(flag, (SEQ, 128))
        angle = times * freq[0:1, :]
        s.cos_t[...] = jnp.cos(angle)
        s.sin_t[...] = jnp.where(first_half, -1.0, 1.0) * jnp.sin(angle)

        wide = s.row_patches[...].astype(f32)
        weight = jnp.zeros((SEQ, PMAX), f32)
        for c in range(PSIZES):
            keep = (codes == float(c)) & (lane < PMAX * 2**c // 2 ** (PSIZES - 1))
            s.x5[:, c * 128 : (c + 1) * 128] = jnp.where(keep, wide, 0.0).astype(bf16)
            weight = jnp.where(keep, 1.0, weight)
        s.weight[...] = jnp.where(flag == 1.0, weight, 0.0)
    for k in range(3):
        for p in range(len(parts)):
            for copy in current[p]:
                copy.wait_recv()
            if k < 2:
                current[p] = start_phase(p, k + 1)
            start_cross(p, k + 1)
        if counted is None:
            counted = next(counting)
        if k == 0:
            prepare_tokens()
    while counted is None:
        counted = next(counting)
    value_count = jnp.sum(counted)
    count_out[...] = jnp.broadcast_to(value_count, count_out.shape)
    for copy in cross:
        copy.wait_recv()

    def load(m):
        n_rows, cols = GRIDS[m]

        @pl.loop(0, n_rows)
        def _(r):
            for c in range(cols):
                b = FIRSTS[m] + r * cols + c
                weights[m][tile(r, SIDE), c * SIDE : (c + 1) * SIDE] = gathered[tuple(places[k, b] for k in range(5))]

    for m in range(6):
        load(m)

    def turn(v, sine):
        swapped = jnp.where(first_half, pltpu.roll(v, 96, 1), pltpu.roll(v, 32, 1))
        return v * s.cos_t[...] + swapped * sine

    embedded = mm(s.x5[...], s.w_in[...])
    for c in range(3):
        cs = slice(c * 128, (c + 1) * 128)
        s.stream[:, cs] = jnp.where(s.flag[...] == 1.0, vectors[3:4, cs], embedded[:, cs])

    def norm(src, inv_ref, gain, dst_t):
        @pl.loop(0, SEQ // 128)
        def _(i):
            rs = tile(i, 128)
            v = src[rs, :]
            inverse = lax.rsqrt(jnp.sum(v * v, axis=-1, keepdims=True) / D + norm_eps)
            inv_ref[rs, :] = jnp.broadcast_to(inverse, (128, 128))
            s.normed[rs, :] = (v * inverse * gain).astype(bf16)

        dst_t[...] = jnp.transpose(s.normed[...])

    def norm_back(src, inv_ref, row, extra):
        gain = vectors[row : row + 1, :]

        @pl.loop(0, SEQ // 128)
        def _(i):
            rs = tile(i, 128)
            up = s.inner[rs, :]
            inverse = inv_ref[rs, 0:1]
            scaled = src[rs, :] * inverse
            inner = up * gain
            mean = jnp.sum(inner * scaled, axis=-1, keepdims=True) / D
            result = inverse * (inner - scaled * mean)
            s.grad[rs, :] = result if extra is None else result + extra[rs, :]
            s.vec_acc[row : row + 1, :] += jnp.sum(up * scaled, axis=0, keepdims=True)

    s.vec_acc[...] = jnp.zeros_like(s.vec_acc)
    norm(s.stream, s.inv_a, vectors[0:1, :], s.na_t)
    for part, dst in ((0, s.qs), (1, s.ks), (2, s.vs)):
        mixed = mm(s.normed[...], s.w_qkv[:, part * D : (part + 1) * D])
        for c in range(3):
            piece = mixed[:, c * 128 : (c + 1) * 128]
            if part < 2:
                piece = turn(piece, s.sin_t[...])
            dst[:, c * 128 : (c + 1) * 128] = piece.astype(bf16)

    @pl.loop(0, HEADS // 2)
    def _(p):
        ps = tile(p, 128)
        qp, kp = s.qs[:, ps], s.ks[:, ps]
        vt = jnp.transpose(s.vs[:, ps])
        outs = []
        for hh in range(2):
            mine = low_head if hh == 0 else jnp.logical_not(low_head)
            qm = jnp.where(mine, qp.astype(f32) * HEAD_DIM**-0.5, 0.0).astype(bf16)
            b0 = bias[2 * p + hh]
            b1 = bias[HEADS + 2 * p + hh]
            parts = []
            for c in range(4):
                cs = slice(c * 128, (c + 1) * 128)
                code = s.code_t[:, cs]
                score = mm_nt(kp, qm[cs, :])
                score = jnp.where(code > 0.5, score + jnp.where(code > 1.5, b0, b1), -1e30)
                raised = jnp.exp(score - jnp.max(score, axis=0, keepdims=True))
                prob = raised * (1.0 / jnp.sum(raised, axis=0, keepdims=True))
                s.probs[2 * p + hh, :, cs] = prob
                parts.append(mm(vt[hh * 64 : (hh + 1) * 64, :], prob.astype(bf16)))
            outs.append(jnp.concatenate(parts, axis=1))
        out_t = jnp.concatenate(outs, axis=0).astype(bf16)
        s.merged_t[ps, :] = out_t
        s.merged[:, ps] = jnp.transpose(out_t)

    s.middle[...] = s.stream[...] + mm(s.merged[...], s.w_out[...])
    norm(s.middle, s.inv_b, vectors[1:2, :], s.nb_t)

    @pl.loop(0, FF // 256)
    def _(j):
        js = tile(j, 256)
        opening = mm(s.normed[...], s.w_gu[:, js])
        up = mm(s.normed[...], s.w_gu[:, tile(j + FF // 256, 256)])
        s.gate[:, js] = opening
        s.upper[:, js] = up
        s.hidden[:, js] = (opening * (1.0 / (1.0 + jnp.exp(-opening))) * up).astype(bf16)

    s.last[...] = s.middle[...] + mm(s.hidden[...], s.w_down[...])
    norm(s.last, s.inv_f, vectors[2:3, :], s.nf_t)


    for kind in range(3):
        pieces = [
            mm(s.w_head[:, g * GROUP : (g + 1) * GROUP], order[:, kind * 128 : (kind + 1) * 128]) for g in range(4)
        ]
        for k, piece in enumerate(swap_quarters(pieces)):
            at = (4 * kind + k) * 128
            s.w_headp[:, at : at + 128] = piece.astype(bf16)

    @pl.loop(0, HEADCOLS // 256)
    def _(j):
        js = tile(j, 256)
        s.params[:, js] = mm(s.normed[...], s.w_headp[:, js])

    inv_n = 1.0 / value_count
    s.loss_acc[...] = jnp.zeros_like(s.loss_acc)

    @pl.loop(0, SEQ // 32)
    def _(i):
        rs = tile(i, 32)
        y = s.row_patches[rs, :].astype(f32)
        weight = s.weight[rs, :]
        logits, means, raws = [
            [s.params[rs, (4 * kind + k) * 128 : (4 * kind + k + 1) * 128] for k in range(COMPS)] for kind in range(3)
        ]
        top = jnp.maximum(jnp.maximum(logits[0], logits[1]), jnp.maximum(logits[2], logits[3]))
        shifted = [v - top for v in logits]
        raised = [jnp.exp(v) for v in shifted]
        total = raised[0] + raised[1] + raised[2] + raised[3]
        log_total = jnp.log(total)
        inv_total = 1.0 / total
        terms, zs, inv_widths = [], [], []
        for k in range(COMPS):
            width = jnp.maximum(raws[k], 0.0) + jnp.log1p(jnp.exp(-jnp.abs(raws[k]))) + scale_floor
            inv_width = 1.0 / width
            z = (y - means[k]) * inv_width
            terms.append((shifted[k] - log_total) - 0.5 * z * z - jnp.log(width) - half_log_tau)
            zs.append(z)
            inv_widths.append(inv_width)
        best = jnp.maximum(jnp.maximum(terms[0], terms[1]), jnp.maximum(terms[2], terms[3]))
        lifted = [jnp.exp(t - best) for t in terms]
        lift_total = lifted[0] + lifted[1] + lifted[2] + lifted[3]
        inv_lift = 1.0 / lift_total
        s.loss_acc[...] += jnp.where(weight > 0.0, -(best + jnp.log(lift_total)), 0.0)
        scale = -(weight * inv_n)
        for k in range(COMPS):
            share = lifted[k] * inv_lift
            d_term = scale * share
            ratio = zs[k] * inv_widths[k]
            d_logit = scale * (share - raised[k] * inv_total)
            d_width = d_term * (zs[k] * ratio - inv_widths[k])
            sigma = 1.0 / (1.0 + jnp.exp(-raws[k]))
            for kind, value in ((0, d_logit), (1, d_term * ratio), (2, d_width * sigma)):
                at = (4 * kind + k) * 128
                s.gparams[rs, at : at + 128] = value.astype(bf16)

    for kind in range(3):
        ks = slice(kind * 512, (kind + 1) * 512)
        wide = mm(s.nf_t[...], s.gparams[:, ks])
        pieces = swap_quarters([wide[:, k * 128 : (k + 1) * 128] for k in range(4)])
        for g in range(4):
            s.w_head[:, (3 * g + kind) * 128 : (3 * g + kind + 1) * 128] = pieces[g].astype(bf16)
    for g in range(4):
        gs = slice(g * GROUP, (g + 1) * GROUP)
        keep(M_HEAD, 0, 3 * g, mm_nt(s.w_head[:, gs], order[...]))
    s.inner[...] = mm_nt(s.gparams[...], s.w_headp[...])
    norm_back(s.last, s.inv_f, 2, None)

    s.normed[...] = s.grad[...].astype(bf16)

    @pl.loop(0, FF // 256)
    def _(j):
        js = tile(j, 256)
        keep(M_DOWN, 2 * j, 0, mm_tn(s.hidden[:, js], s.normed[...]))
        up_grad = mm_nt(s.normed[...], s.w_down[js, :])
        opening = s.gate[:, js]
        sigma = 1.0 / (1.0 + jnp.exp(-opening))
        s.ggu[:, js] = (up_grad * s.upper[:, js] * sigma * (1.0 + opening * (1.0 - sigma))).astype(bf16)
        s.ggu[:, tile(j + FF // 256, 256)] = (up_grad * opening * sigma).astype(bf16)


    @pl.loop(0, 2 * FF // 256)
    def _(j):
        js = tile(j, 256)
        keep(M_GU, 0, 2 * j, mm(s.nb_t[...], s.ggu[:, js]))

    s.inner[...] = mm_nt(s.ggu[...], s.w_gu[...])
    norm_back(s.middle, s.inv_b, 1, s.grad)

    s.normed[...] = s.grad[...].astype(bf16)
    keep(M_OUT, 0, 0, mm(s.merged_t[...], s.normed[...]))
    s.merged[...] = mm_nt(s.normed[...], s.w_out[...]).astype(bf16)
    s.bias_acc[...] = jnp.zeros_like(s.bias_acc)

    @pl.loop(0, HEADS // 2)
    def _(p):
        ps = tile(p, 128)
        qp, kp, vp, dop = s.qs[:, ps], s.ks[:, ps], s.vs[:, ps], s.merged[:, ps]
        kt = jnp.transpose(kp)
        dq, dk, dv = [], [], []
        for hh in range(2):
            mine = low_head if hh == 0 else jnp.logical_not(low_head)
            dom = jnp.where(mine, dop.astype(f32), 0.0).astype(bf16)
            same_sum = jnp.zeros((1, 128), f32)
            all_sum = jnp.zeros((1, 128), f32)
            for c in range(4):
                cs = slice(c * 128, (c + 1) * 128)
                prob = s.probs[2 * p + hh, :, cs]
                d_prob = mm_nt(vp, dom[cs, :])
                d_score = prob * (d_prob - jnp.sum(prob * d_prob, axis=0, keepdims=True))
                same_sum += jnp.sum(jnp.where(s.code_t[:, cs] > 1.5, d_score, 0.0), axis=0, keepdims=True)
                all_sum += jnp.sum(d_score, axis=0, keepdims=True)
                s.dscore[:, cs] = (d_score * HEAD_DIM**-0.5).astype(bf16)
            s.bias_acc[pl.ds(2 * p + hh, 1), :] = same_sum
            s.bias_acc[pl.ds(8 + 2 * p + hh, 1), :] = all_sum
            dv.append(mm(s.probs[2 * p + hh].astype(bf16), dop))
            dk.append(mm(s.dscore[...], qp))
            dq.append(mm(kt[hh * 64 : (hh + 1) * 64, :], s.dscore[...]))
        dqs = jnp.transpose(jnp.concatenate(dq, axis=0)).astype(bf16).astype(f32)
        dks = jnp.where(low_head, dk[0], dk[1]).astype(bf16).astype(f32)
        s.dqkv[:, ps] = turn(dqs, -s.sin_t[...]).astype(bf16)
        s.dqkv[:, tile(p + 3, 128)] = turn(dks, -s.sin_t[...]).astype(bf16)
        s.dqkv[:, tile(p + 6, 128)] = jnp.where(low_head, dv[0], dv[1]).astype(bf16)

    for j in range(3):
        js = slice(j * D, (j + 1) * D)
        keep(M_QKV, 0, 3 * j, mm(s.na_t[...], s.dqkv[:, js]))
    s.inner[...] = mm_nt(s.dqkv[...], s.w_qkv[...])
    norm_back(s.stream, s.inv_a, 0, s.grad)
    for c in range(3):
        cs = slice(c * 128, (c + 1) * 128)
        hidden_token = s.flag[...] == 1.0
        s.vec_acc[3:4, cs] = jnp.sum(jnp.where(hidden_token, s.grad[:, cs], 0.0), axis=0, keepdims=True)
        s.normed[:, cs] = jnp.where(hidden_token, 0.0, s.grad[:, cs]).astype(bf16)
    keep(M_IN, 0, 0, mm_tn(s.x5[...], s.normed[...]))

    sums = jnp.sum(s.bias_acc[...], axis=1, keepdims=True)
    sums = jnp.concatenate([sums[0:8], sums[8:16] - sums[0:8]], axis=0)
    diagonal = lax.broadcasted_iota(jnp.int32, (16, D), 0) == lax.broadcasted_iota(jnp.int32, (16, D), 1)
    bias_row = jnp.sum(jnp.where(diagonal, sums, 0.0), axis=0, keepdims=True)
    row = lax.broadcasted_iota(jnp.int32, (8, D), 0)
    small_sum = jnp.where(row == 4, jnp.sum(s.loss_acc[...]), jnp.where(row == 5, bias_row, s.vec_acc[...]))
    for copy in started:
        copy.wait_send()
    for copy in cross:
        copy.wait_send()
    s.blocks[BLOCKS] = jnp.zeros((SIDE, SIDE), bf16)
    toks = dims[0] * dims[1] * dims[2]

    def fill(h):
        @pl.loop(0, toks)
        def _(t):
            for i in range(per):
                at = (h, t // (dims[1] * dims[2]), t // dims[2] % dims[1], t % dims[2], i)
                gathered[at] = s.blocks[holder[(h * toks + t) * per + i]]

    everywhere = (slice(None),) * 3
    parts = cut_parts(REDUCE_PARTS)
    fill(1 - head)
    crossing = []
    for p, (_, a, n) in enumerate(parts):
        view = everywhere + (slice(None), pl.ds(a, n))
        copy = remote(gathered.at[(1 - head,) + view], crossed.at[view], rc_send.at[p], rc_recv.at[p], place.partner())
        copy.start()
        crossing.append(copy)
    vec_sum = all_sum(place, small_sum, vec_buf, vec_send, vec_recv)
    vec_total = next(vec_sum)
    fill(head)
    r_started = []
    r_current = {}

    def start_reduce(p, k):
        axes, a, n = parts[p]
        axis, left = axes[k], axes[k + 1 :]
        r_current[p] = []
        for j in range(1, dims[axis]):
            src = gathered.at[(head,) + place.region(left, {axis: place.coordinate(axis, j)}) + (slice(None), pl.ds(a, n))]
            copy = remote(src, landing[3 * p + k].at[j - 1], r_send.at[p, k, j], r_recv.at[p, k, j], place.peer(axis, j))
            copy.start()
            r_current[p].append(copy)
        r_started.extend(r_current[p])

    def add_up(p, k):
        axes, a, n = parts[p]
        left = sorted(axes[k + 1 :])
        region = place.region(left)
        for copy in r_current[p]:
            copy.wait_recv()

        def body(*index):
            at = (head,) + tuple(index[left.index(i)] if i in left else region[i] for i in range(3)) + (slice(None), pl.ds(a, n))
            value = gathered[at].astype(f32)
            for j in range(1, dims[axes[k]]):
                value = value + landing[3 * p + k][(j - 1,) + index].astype(f32)
            if k < 2:
                gathered[at] = value.astype(bf16)
            else:
                owned[:, a : a + n, :] = value

        if k == 2:
            body()
        elif k == 1:
            pl.loop(0, dims[left[0]])(body)
        else:

            @pl.loop(0, dims[left[0]])
            def _(i):
                pl.loop(0, dims[left[1]])(lambda j: body(i, j))

    for p, (_, a, n) in enumerate(parts):
        crossing[p].wait_recv()

        @pl.loop(0, dims[0])
        def _(i):
            @pl.loop(0, dims[1])
            def _(j):
                for m in range(dims[2]):
                    at = (i, j, m, slice(None), pl.ds(a, n))
                    gathered[(head,) + at] = (gathered[(head,) + at].astype(f32) + crossed[at].astype(f32)).astype(bf16)

        start_reduce(p, 0)
    for k in range(3):
        for p in range(len(parts)):
            add_up(p, k)
            if k < 2:
                start_reduce(p, k + 1)
        if vec_total is None:
            vec_total = next(vec_sum)
    while vec_total is None:
        vec_total = next(vec_sum)
    small_total[...] = vec_total
    part_square = jnp.zeros((8, 128), f32)
    for i in range(per):
        piece = owned[i]
        part_square = part_square + jnp.sum((piece * piece).reshape(16, 8, 128), axis=0)
    sq_sum = all_sum(place, part_square, sq_buf, sq_send, sq_recv)
    total = None
    while total is None:
        total = next(sq_sum)
    square[...] = jnp.broadcast_to(jnp.sum(total), (8, 128))
    for copy in r_started:
        copy.wait_send()
    for copy in crossing:
        copy.wait_send()


def step_call(dims, places, holder, lengths, bias, master, patches, sizes, times, predict, variates, vectors):
    freq = (10000.0 ** (-np.arange(HEAD_DIM // 2) / (HEAD_DIM // 2))).astype(np.float32)
    freq = jnp.asarray(np.tile(freq[None], (8, 4)))
    per = master.shape[0]
    half = patches.shape[2]
    most = max(dims)
    smem = pl.BlockSpec(memory_space=pltpu.SMEM)
    vmem = pl.BlockSpec(memory_space=pltpu.VMEM)
    sems = pltpu.SemaphoreType.DMA
    gather_parts, reduce_parts = cut_parts(GATHER_PARTS), cut_parts(REDUCE_PARTS)
    landing = []
    for axes, _, n in reduce_parts:
        for k in range(3):
            left = [dims[i] for i in sorted(axes[k + 1 :])]
            landing.append(pltpu.VMEM((max(dims[axes[k]] - 1, 1), *left, per, n, SIDE), bf16))
    return pl.pallas_call(
        functools.partial(step_kernel, dims),
        out_shape=(
            jax.ShapeDtypeStruct((per, SIDE, SIDE), f32),
            jax.ShapeDtypeStruct((8, D), f32),
            jax.ShapeDtypeStruct((8, 128), f32),
            jax.ShapeDtypeStruct((8, 128), f32),
        ),
        in_specs=[smem] * 4 + [vmem] * 9,
        out_specs=(vmem,) * 4,
        scratch_shapes=[pltpu.VMEM(shape, dtype) for shape, dtype in SCRATCH.values()]
        + [
            pltpu.VMEM((per, SIDE, SIDE), bf16),
            pltpu.VMEM((2,) + dims + (per, SIDE, SIDE), bf16),
            pltpu.VMEM(dims + (per, SIDE, SIDE), bf16),
            pltpu.VMEM((half, PMAX), bf16),
            pltpu.VMEM((3, 2, half), jnp.int32),
            pltpu.VMEM((3, 2, half), jnp.int32),
            *sum_shapes(dims, (8, 128)),
            *sum_shapes(dims, (8, D)),
            *sum_shapes(dims, (8, 128)),
            sems,
            sems((len(gather_parts), 3, most)),
            sems((len(gather_parts), 3, most)),
            sems((len(gather_parts), 4, most)),
            sems((len(gather_parts), 4, most)),
            sems((4,)),
            sems((len(reduce_parts), 3, most)),
            sems((len(reduce_parts), 3, most)),
            sems((len(reduce_parts),)),
            sems((len(reduce_parts),)),
            *landing,
        ],
        compiler_params=pltpu.CompilerParams(
            collective_id=0, has_side_effects=True, vmem_limit_bytes=63 * 2**20
        ),
        name="step",
    )(places, holder, lengths, bias, master, patches, sizes, times, predict, variates, vectors, freq,
      jnp.asarray(group_order(), bf16))


def shampoo(gradients, left, right, left_root, right_root, master):
    left_next = stat_beta * left + (1.0 - stat_beta) * jnp.einsum(
        "sij,skj->sik", gradients, gradients, precision=highest
    )
    right_next = stat_beta * right + (1.0 - stat_beta) * jnp.einsum(
        "sji,sjk->sik", gradients, gradients, precision=highest
    )
    shaped = jnp.einsum("sij,sjk->sik", left_root, gradients, precision=highest)
    shaped = jnp.einsum("sij,sjk->sik", shaped, right_root, precision=highest)
    unit = shaped * lax.rsqrt(jnp.mean(shaped * shaped, axis=(1, 2), keepdims=True) + root_eps)
    return (left_next, right_next, master - mat_rate * (unit + decay_rate * master))


def adamw(gradients, first_moment, second_moment, values):
    first_next = beta_one * first_moment + (1.0 - beta_one) * gradients
    second_next = beta_two * second_moment + (1.0 - beta_two) * gradients * gradients
    ratio = (
        first_next
        / (1.0 - beta_one**STEP)
        / (jnp.sqrt(second_next / (1.0 - beta_two**STEP)) + adam_eps)
    )
    return (second_next, values - vec_rate * (ratio + decay_rate * values))


def shards(
    dims,
    patches, patch_sizes, sample_lengths, variate_ids, time_ids, predict_mask, block_owner_slot,
    master_blocks, left_stats, right_stats, left_roots, right_roots,
    vectors, vector_first, vector_second, var_bias, bias_first, bias_second,
):
    slot_count = master_blocks.shape[0] * lax.axis_size("head") * lax.axis_size("tok")
    match = block_owner_slot[None, :] == jnp.arange(slot_count)[:, None]
    holder = BLOCKS + jnp.sum(jnp.where(match, jnp.arange(BLOCKS)[None, :] - BLOCKS, 0), axis=1)
    device, inside = block_owner_slot // master_blocks.shape[0], block_owner_slot % master_blocks.shape[0]
    places = [device // (dims[0] * dims[1] * dims[2])]
    places += [device // (dims[1] * dims[2]) % dims[0], device // dims[2] % dims[1], device % dims[2], inside]
    owned, small_total, square, count = step_call(
        dims, jnp.stack(places), holder, sample_lengths, var_bias[0], master_blocks, patches, patch_sizes, time_ids,
        predict_mask, variate_ids, vectors,
    )
    count = count[0, 0]
    vector_total = small_total[0:4]
    loss_sum = small_total[4, 0]
    bias_total = jnp.concatenate([small_total[5, 0:HEADS], small_total[5, 8 : 8 + HEADS]])[None]
    block_square = square[0, 0]
    grad_norm = jnp.sqrt(
        block_square + jnp.sum(vector_total * vector_total) + jnp.sum(bias_total * bias_total)
    )
    factor_value = jnp.minimum(1.0, clip_limit / grad_norm)
    clipped_block_gradient = owned * factor_value
    left_new, right_new, master_new = shampoo(
        clipped_block_gradient, left_stats, right_stats, left_roots, right_roots, master_blocks
    )
    vector_grads = vector_total * factor_value
    vector_second_new, vector_new = adamw(vector_grads, vector_first, vector_second, vectors)
    bias_grads = bias_total * factor_value
    bias_second_new, bias_new = adamw(bias_grads, bias_first, bias_second, var_bias)
    return (
        loss_sum, count, grad_norm, clipped_block_gradient, left_new, right_new, master_new,
        vector_grads, vector_second_new, vector_new, bias_grads, bias_second_new, bias_new,
    )


def solution(mesh):
    rep = P()
    dims = tok_dims(mesh.shape["tok"])
    slot = P(("head", "tok"), None, None)
    return jax.shard_map(
        functools.partial(shards, dims),
        mesh=mesh,
        in_specs=(
            P(None, "tok", "head", None), P(None, "tok", "head"), P(None, "tok", None), P(None, "tok", None),
            P(None, "tok", "head"), P(None, "tok", "head"), rep, slot, slot, slot, slot, slot,
            rep, rep, rep, rep, rep, rep,
        ),
        out_specs=(rep, rep, rep, slot, slot, slot, slot, rep, rep, rep, rep, rep, rep),
        check_vma=False,
    )
```

```python
import functools
import itertools
import math

import jax
import jax.numpy as jnp
import numpy as np
from jax import lax
from jax.experimental import pallas as pl
from jax.experimental.pallas import tpu as pltpu
from jax.sharding import PartitionSpec as P

D = 384
FF = 1024
HEADS = 6
HEAD_DIM = 64
PSIZES = 5
PMAX = 128
COMPS = 4
SEQ = 512
SIDE = 128
STEP = 10
HEADCOLS = 3 * COMPS * PMAX
BLOCKS = 159

norm_eps = 1e-06
scale_floor = 0.05
half_log_tau = 0.9189385332046727
clip_limit = 0.02
mat_rate = 0.01
vec_rate = 0.3
decay_rate = 0.01
beta_one = 0.9
beta_two = 0.95
stat_beta = 0.99
root_eps = 1e-06
adam_eps = 1e-08
highest = lax.Precision.HIGHEST
f32 = jnp.float32
bf16 = jnp.bfloat16

GRIDS = ((5, 3), (3, 12), (3, 9), (3, 3), (3, 16), (8, 3))
FIRSTS = (0, 15, 51, 78, 87, 135)
M_IN, M_HEAD, M_QKV, M_OUT, M_GU, M_DOWN = range(6)


def mm(a, b):
    return jnp.dot(a, b, preferred_element_type=f32)


def mm_nt(a, b):
    return lax.dot_general(a, b, (((1,), (1,)), ((), ())), preferred_element_type=f32)


def mm_tn(a, b):
    return lax.dot_general(a, b, (((0,), (0,)), ((), ())), preferred_element_type=f32)


GROUP = 384


def group_order():
    order = np.zeros((GROUP, GROUP), np.float32)
    for col in range(GROUP):
        order[col, (col % 12) * 32 + col // 12] = 1.0
    return order


def swap_quarters(parts):
    lane = lax.broadcasted_iota(jnp.int32, (1, 128), 1)
    low, even = lane < 64, lane % 64 < 32
    a, b, c, d = parts
    a, c = jnp.where(low, a, pltpu.roll(c, 64, 1)), jnp.where(low, pltpu.roll(a, 64, 1), c)
    b, d = jnp.where(low, b, pltpu.roll(d, 64, 1)), jnp.where(low, pltpu.roll(b, 64, 1), d)
    a, b = jnp.where(even, a, pltpu.roll(b, 32, 1)), jnp.where(even, pltpu.roll(a, 96, 1), b)
    c, d = jnp.where(even, c, pltpu.roll(d, 32, 1)), jnp.where(even, pltpu.roll(c, 96, 1), d)
    return a, b, c, d


SCRATCH = dict(
    w_in=((640, D), bf16), w_head=((D, HEADCOLS), bf16), w_qkv=((D, 3 * D), bf16), w_out=((D, D), bf16),
    w_gu=((D, 2 * FF), bf16), w_down=((FF, D), bf16), w_headp=((D, HEADCOLS), bf16),
    blocks=((BLOCKS + 1, SIDE, SIDE), bf16),
    x5=((SEQ, 640), bf16), weight=((SEQ, PMAX), f32), flag=((SEQ, 128), f32),
    cos_t=((SEQ, 128), f32), sin_t=((SEQ, 128), f32),
    code_t=((SEQ, SEQ), f32), probs=((HEADS, SEQ, SEQ), f32),
    stream=((SEQ, D), f32), middle=((SEQ, D), f32), last=((SEQ, D), f32), grad=((SEQ, D), f32), inner=((SEQ, D), f32),
    inv_a=((SEQ, 128), f32), inv_b=((SEQ, 128), f32), inv_f=((SEQ, 128), f32),
    normed=((SEQ, D), bf16), na_t=((D, SEQ), bf16), nb_t=((D, SEQ), bf16), nf_t=((D, SEQ), bf16),
    qs=((SEQ, D), bf16), ks=((SEQ, D), bf16), vs=((SEQ, D), bf16), merged=((SEQ, D), bf16), merged_t=((D, SEQ), bf16),
    gate=((SEQ, FF), f32), upper=((SEQ, FF), f32), hidden=((SEQ, FF), bf16),
    params=((SEQ, HEADCOLS), f32), gparams=((SEQ, HEADCOLS), bf16), ggu=((SEQ, 2 * FF), bf16),
    loss_acc=((32, 128), f32), bias_acc=((16, 128), f32), vec_acc=((8, D), f32),
    meta=((8, SEQ), jnp.int32), row_patches=((SEQ, PMAX), bf16),
)


def tile(i, size):
    return pl.ds(pl.multiple_of(i * size, size), size)


MESH = pl.DeviceIdType.MESH


def tok_dims(count):
    return {16: (4, 2, 2), 128: (4, 4, 8)}.get(count, (count, 1, 1))


class Place:
    def __init__(self, dims):
        self.dims = dims
        self.head = lax.axis_index("head")
        tok = lax.axis_index("tok")
        self.tok = tok
        self.strides = (dims[1] * dims[2], dims[2], 1)
        self.at = [lax.rem(lax.div(tok, s), n) for s, n in zip(self.strides, dims)]

    def coordinate(self, axis, step):
        return lax.rem(self.at[axis] + step, self.dims[axis])

    def peer(self, axis, step):
        return (self.head, self.tok + (self.coordinate(axis, step) - self.at[axis]) * self.strides[axis])

    def partner(self):
        return (1 - self.head, self.tok)

    def groups(self):
        result, size = [[None]], 2
        for axis in (1, 2, 0):
            if self.dims[axis] == 1:
                continue
            if size * self.dims[axis] > 8:
                result.append([])
                size = 1
            result[-1].append(axis)
            size *= self.dims[axis]
        return result

    def members(self, group):
        sizes = [2 if axis is None else self.dims[axis] for axis in group]
        mine = 0
        for axis, n in zip(group, sizes):
            mine = mine * n + (self.head if axis is None else self.at[axis])
        others = []
        for steps in itertools.product(*[range(n) for n in sizes]):
            head, tok = self.head, self.tok
            for axis, step in zip(group, steps):
                if axis is None:
                    head = lax.rem(head + step, 2)
                else:
                    tok = tok + (self.coordinate(axis, step) - self.at[axis]) * self.strides[axis]
            if any(steps):
                others.append((head, tok))
        return mine, math.prod(sizes), others

    def greet(self):
        barrier = pltpu.get_barrier_semaphore()
        groups = self.groups()
        others = [other for group in groups for other in self.members(group)[2]]
        joint = [group for group in groups if len(group) > 1]
        singles = {group[0] for group in groups if len(group) == 1} | {a for group in joint for a in group}
        others += [self.peer(a, j) for a in range(3) if a not in singles for j in range(1, self.dims[a])]
        for other in others:
            pl.semaphore_signal(barrier, inc=1, device_id=other, device_id_type=MESH)
        pl.semaphore_wait(barrier, len(others))

    def region(self, whole, fixed=None):
        fixed = fixed or {}
        return tuple(slice(None) if a in whole else fixed.get(a, self.at[a]) for a in range(3))


def remote(src, dst, send, recv, device):
    return pltpu.make_async_remote_copy(
        src_ref=src, dst_ref=dst, send_sem=send, recv_sem=recv, device_id=device, device_id_type=MESH
    )


def split_rows(rows, shares):
    units = rows // 16
    edges = [round(units * sum(shares[:i]) / sum(shares)) * 16 for i in range(len(shares) + 1)]
    return [(a, b - a) for a, b in zip(edges, edges[1:])]


class Pool:
    def __init__(self, ref):
        self.ref, self.used = ref, 0

    def __call__(self):
        self.used += 1
        return self.ref.at[self.used - 1]


def all_sum(place, values, buf, send, recv):
    total = values
    for k, group in enumerate(place.groups()):
        mine, size, others = place.members(group)
        buf[k, mine] = total
        copies = [remote(buf.at[k, mine], buf.at[k, mine], send(), recv(), other) for other in others]
        for copy in copies:
            copy.start()
        yield None
        for copy in copies:
            copy.wait()
        total = buf[k, 0]
        for i in range(1, size):
            total = total + buf[k, i]
    yield total


def sum_sizes(dims):
    place = Place.__new__(Place)
    place.dims = dims
    return [math.prod(2 if a is None else dims[a] for a in group) for group in place.groups()]


def sum_shape(dims, shape):
    sizes = sum_sizes(dims)
    return pltpu.VMEM((len(sizes), max(sizes)) + shape, f32)


GATHER_PARTS = (((0, 1, 2), 1), ((0, 2, 1), 1)) * 4
GATHER_GROUPS = ((0, 1), (2, 3), (4, 5), (6, 7))
GATHER_WINDOW = 1
REDUCE_PARTS = (((2, 1, 0), 1), ((1, 2, 0), 1)) * 4
REDUCE_GROUPS = ((0, 1), (2, 3), (4, 5), (6, 7))
REDUCE_WINDOW = 4


def cut_parts(table):
    return [(order, a, n) for (order, _), (a, n) in zip(table, split_rows(SIDE, [s for _, s in table]))]


def pipeline(groups, phases, window, start, finish):
    for group in groups[:window]:
        for p in group:
            start(p, 0)
    for t in range(len(groups) + phases - 1):
        for k in range(phases):
            if not 0 <= t - k < len(groups):
                continue
            for p in groups[t - k]:
                finish(p, k)
                if k + 1 < phases:
                    start(p, k + 1)
            if k == 0:
                for p in groups[t + window] if t + window < len(groups) else ():
                    start(p, 0)


def semaphores(dims):
    steps = sum(n - 1 for n in dims)
    sums = sum(n - 1 for n in sum_sizes(dims))
    gather = sum(steps + 1 + sum(dims[a] - 1 for a in order[1:]) for order, _ in GATHER_PARTS) + 2 + sums
    reduce = len(REDUCE_PARTS) * (steps + 1) + 2 * sums
    return gather + reduce, max(gather, reduce)


def step_kernel(
    dims, places, holder, lengths, bias, master, patches, sizes, times_in, predict_in, variates_in, vectors, freq, order,
    loss_out, count_out, norm_out, factor_out, small_out, owned, gram_left, gram_right, *rest,
):
    names = list(SCRATCH)
    s = type("S", (), dict(zip(names, rest)))
    rest = rest[len(names) :]
    mine, gathered, crossed, land_patch, land_ints, own_ints = rest[:6]
    cnt_buf, vec_buf, sq_buf, own_sem, send_pool, recv_pool = rest[6:12]
    send, recv = Pool(send_pool), Pool(recv_pool)
    landing = rest[12:]
    place = Place(dims)
    per = mine.shape[0]
    head = place.head
    lane = lax.broadcasted_iota(jnp.int32, (1, 128), 1)
    first_half = lane % HEAD_DIM < HEAD_DIM // 2
    low_head = lane < HEAD_DIM
    weights = (s.w_in, s.w_head, s.w_qkv, s.w_out, s.w_gu, s.w_down)

    def keep(m, r0, c0, value):
        value = value.astype(bf16)
        cols = GRIDS[m][1]
        for r in range(value.shape[0] // SIDE):
            for c in range(value.shape[1] // SIDE):
                piece = value[r * SIDE : (r + 1) * SIDE, c * SIDE : (c + 1) * SIDE]
                s.blocks[FIRSTS[m] + (r0 + r) * cols + c0 + c] = piece

    place.greet()
    for k, ref in enumerate((sizes, times_in, predict_in)):
        own_ints[k, :, :] = ref[:, 0, :]
    swaps = [
        remote(patches.at[1 - head, 0], land_patch, send(), recv(), place.partner()),
        remote(own_ints, land_ints, send(), recv(), place.partner()),
    ]
    for copy in swaps:
        copy.start()
    mine[...] = master[...].astype(bf16)
    parts = cut_parts(GATHER_PARTS)

    def block(head_index, whole, fixed, a, n):
        return gathered.at[(head_index,) + place.region(whole, fixed) + (slice(None), pl.ds(a, n))]

    arriving, outgoing, cross = {}, list(swaps), []
    own = pltpu.make_async_copy(mine, gathered.at[(head,) + place.region(())], own_sem)
    own.start()

    def start_gather(p, k):
        axes, a, n = parts[p]
        axis, whole = axes[k], axes[:k]
        arriving[p] = []
        for j in range(1, dims[axis]):
            src = mine.at[:, pl.ds(a, n)] if k == 0 else block(head, whole, None, a, n)
            copy = remote(src, block(head, whole, None, a, n), send(), recv(), place.peer(axis, j))
            copy.start()
            arriving[p].append(copy)
        outgoing.extend(arriving[p])

    def end_gather(p, k):
        axes, a, n = parts[p]
        for copy in arriving[p]:
            copy.wait_recv()
        axis, whole = axes[k], axes[:k]
        if k == 0:
            views = [block(head, axes[:1], None, a, n)]
        else:
            views = [
                block(head, whole, {axis: place.coordinate(axis, dims[axis] - j)}, a, n) for j in range(1, dims[axis])
            ]
        for view in views:
            copy = remote(view, view, send(), recv(), place.partner())
            copy.start()
            cross.append(copy)

    for p in GATHER_GROUPS[0]:
        start_gather(p, 0)
    wide_size = jnp.zeros_like(own_ints[0])
    for c in range(PSIZES):
        wide_size = wide_size + jnp.where(own_ints[0] == c, PMAX * 2**c // 2 ** (PSIZES - 1), 0)
    partial = (wide_size * own_ints[2]).astype(f32)
    partial = jnp.sum(partial[:, :128] + partial[:, 128:], axis=0, keepdims=True)
    counting = all_sum(place, jnp.concatenate([partial, jnp.zeros((7, 128), f32)], axis=0), cnt_buf, send, recv)
    counted = next(counting)
    own.wait()
    for copy in swaps:
        copy.wait_recv()
    half = SEQ // 2
    for h in range(2):

        @pl.when(head == h)
        def _():
            here, there = slice(h * half, (h + 1) * half), slice((1 - h) * half, (2 - h) * half)
            s.row_patches[here, :] = patches[h, 0]
            s.row_patches[there, :] = land_patch[...]
            for k in range(3):
                s.meta[k : k + 1, here] = own_ints[k, h : h + 1, :]
                s.meta[k : k + 1, there] = land_ints[k, h : h + 1, :]
            s.meta[3:4, :] = variates_in[h]

    s.meta[4:8, :] = jnp.zeros((4, SEQ), jnp.int32)

    def prepare_tokens():
        metaf = s.meta[...].astype(f32)
        columns = jnp.transpose(metaf)
        codes, times, flag = columns[:, 0:1], columns[:, 1:2], columns[:, 2:3]
        position = lax.broadcasted_iota(jnp.int32, (1, SEQ), 1)
        ids = jnp.zeros((1, SEQ), f32)
        end = jnp.int32(0)
        for j in range(lengths.shape[2]):
            end = end + lengths[head, 0, j]
            ids = ids + jnp.where(position >= end, 1.0, 0.0)
        variates = metaf[3:4]
        id_columns = jnp.transpose(jnp.concatenate([ids] * 8, axis=0))[:, 0:1]
        var_columns = columns[:, 3:4]
        for c in range(4):
            cs = slice(c * 128, (c + 1) * 128)
            same_sample = id_columns == ids[:, cs]
            same_var = var_columns == variates[:, cs]
            s.code_t[:, cs] = jnp.where(same_sample, jnp.where(same_var, 2.0, 1.0), 0.0)
        s.flag[...] = jnp.broadcast_to(flag, (SEQ, 128))
        angle = times * freq[0:1, :]
        s.cos_t[...] = jnp.cos(angle)
        s.sin_t[...] = jnp.where(first_half, -1.0, 1.0) * jnp.sin(angle)

        wide = s.row_patches[...].astype(f32)
        weight = jnp.zeros((SEQ, PMAX), f32)
        for c in range(PSIZES):
            keep = (codes == float(c)) & (lane < PMAX * 2**c // 2 ** (PSIZES - 1))
            s.x5[:, c * 128 : (c + 1) * 128] = jnp.where(keep, wide, 0.0).astype(bf16)
            weight = jnp.where(keep, 1.0, weight)
        s.weight[...] = jnp.where(flag == 1.0, weight, 0.0)
    begun = set(GATHER_GROUPS[0])
    ended = []

    def start(p, k):
        if k > 0 or p not in begun:
            start_gather(p, k)

    def finish(p, k):
        nonlocal counted
        end_gather(p, k)
        if counted is None:
            counted = next(counting)
        ended.append(p)
        if len(ended) == len(GATHER_GROUPS[0]):
            prepare_tokens()

    pipeline(GATHER_GROUPS, 3, GATHER_WINDOW, start, finish)
    while counted is None:
        counted = next(counting)
    value_count = jnp.sum(counted)
    count_out[0, 0] = value_count
    for copy in cross:
        copy.wait_recv()

    def load(m):
        n_rows, cols = GRIDS[m]

        @pl.loop(0, n_rows)
        def _(r):
            for c in range(cols):
                b = FIRSTS[m] + r * cols + c
                weights[m][tile(r, SIDE), c * SIDE : (c + 1) * SIDE] = gathered[tuple(places[k, b] for k in range(5))]

    for m in range(6):
        load(m)

    def turn(v, sine):
        swapped = jnp.where(first_half, pltpu.roll(v, 96, 1), pltpu.roll(v, 32, 1))
        return v * s.cos_t[...] + swapped * sine

    embedded = mm(s.x5[...], s.w_in[...])
    for c in range(3):
        cs = slice(c * 128, (c + 1) * 128)
        s.stream[:, cs] = jnp.where(s.flag[...] == 1.0, vectors[3:4, cs], embedded[:, cs])

    def norm(src, inv_ref, gain, dst_t):
        @pl.loop(0, SEQ // 128)
        def _(i):
            rs = tile(i, 128)
            v = src[rs, :]
            inverse = lax.rsqrt(jnp.sum(v * v, axis=-1, keepdims=True) / D + norm_eps)
            inv_ref[rs, :] = jnp.broadcast_to(inverse, (128, 128))
            s.normed[rs, :] = (v * inverse * gain).astype(bf16)

        dst_t[...] = jnp.transpose(s.normed[...])

    def norm_back(src, inv_ref, row, extra):
        gain = vectors[row : row + 1, :]

        @pl.loop(0, SEQ // 128)
        def _(i):
            rs = tile(i, 128)
            up = s.inner[rs, :]
            inverse = inv_ref[rs, 0:1]
            scaled = src[rs, :] * inverse
            inner = up * gain
            mean = jnp.sum(inner * scaled, axis=-1, keepdims=True) / D
            result = inverse * (inner - scaled * mean)
            s.grad[rs, :] = result if extra is None else result + extra[rs, :]
            s.vec_acc[row : row + 1, :] += jnp.sum(up * scaled, axis=0, keepdims=True)

    s.vec_acc[...] = jnp.zeros_like(s.vec_acc)
    norm(s.stream, s.inv_a, vectors[0:1, :], s.na_t)
    for part, dst in ((0, s.qs), (1, s.ks), (2, s.vs)):
        mixed = mm(s.normed[...], s.w_qkv[:, part * D : (part + 1) * D])
        for c in range(3):
            piece = mixed[:, c * 128 : (c + 1) * 128]
            if part < 2:
                piece = turn(piece, s.sin_t[...])
            dst[:, c * 128 : (c + 1) * 128] = piece.astype(bf16)

    @pl.loop(0, HEADS // 2)
    def _(p):
        ps = tile(p, 128)
        qp, kp = s.qs[:, ps], s.ks[:, ps]
        vt = jnp.transpose(s.vs[:, ps])
        outs = []
        for hh in range(2):
            mine = low_head if hh == 0 else jnp.logical_not(low_head)
            qm = jnp.where(mine, qp.astype(f32) * HEAD_DIM**-0.5, 0.0).astype(bf16)
            b0 = bias[2 * p + hh]
            b1 = bias[HEADS + 2 * p + hh]
            parts = []
            for c in range(4):
                cs = slice(c * 128, (c + 1) * 128)
                code = s.code_t[:, cs]
                score = mm_nt(kp, qm[cs, :])
                score = jnp.where(code > 0.5, score + jnp.where(code > 1.5, b0, b1), -1e30)
                raised = jnp.exp(score - jnp.max(score, axis=0, keepdims=True))
                prob = raised * (1.0 / jnp.sum(raised, axis=0, keepdims=True))
                s.probs[2 * p + hh, :, cs] = prob
                parts.append(mm(vt[hh * 64 : (hh + 1) * 64, :], prob.astype(bf16)))
            outs.append(jnp.concatenate(parts, axis=1))
        out_t = jnp.concatenate(outs, axis=0).astype(bf16)
        s.merged_t[ps, :] = out_t
        s.merged[:, ps] = jnp.transpose(out_t)

    s.middle[...] = s.stream[...] + mm(s.merged[...], s.w_out[...])
    norm(s.middle, s.inv_b, vectors[1:2, :], s.nb_t)

    @pl.loop(0, FF // 256)
    def _(j):
        js = tile(j, 256)
        opening = mm(s.normed[...], s.w_gu[:, js])
        up = mm(s.normed[...], s.w_gu[:, tile(j + FF // 256, 256)])
        s.gate[:, js] = opening
        s.upper[:, js] = up
        s.hidden[:, js] = (opening * (1.0 / (1.0 + jnp.exp(-opening))) * up).astype(bf16)

    s.last[...] = s.middle[...] + mm(s.hidden[...], s.w_down[...])
    norm(s.last, s.inv_f, vectors[2:3, :], s.nf_t)


    for kind in range(3):
        pieces = [
            mm(s.w_head[:, g * GROUP : (g + 1) * GROUP], order[:, kind * 128 : (kind + 1) * 128]) for g in range(4)
        ]
        for k, piece in enumerate(swap_quarters(pieces)):
            at = (4 * kind + k) * 128
            s.w_headp[:, at : at + 128] = piece.astype(bf16)

    @pl.loop(0, HEADCOLS // 256)
    def _(j):
        js = tile(j, 256)
        s.params[:, js] = mm(s.normed[...], s.w_headp[:, js])

    inv_n = 1.0 / value_count
    s.loss_acc[...] = jnp.zeros_like(s.loss_acc)

    @pl.loop(0, SEQ // 32)
    def _(i):
        rs = tile(i, 32)
        y = s.row_patches[rs, :].astype(f32)
        weight = s.weight[rs, :]
        logits, means, raws = [
            [s.params[rs, (4 * kind + k) * 128 : (4 * kind + k + 1) * 128] for k in range(COMPS)] for kind in range(3)
        ]
        top = jnp.maximum(jnp.maximum(logits[0], logits[1]), jnp.maximum(logits[2], logits[3]))
        shifted = [v - top for v in logits]
        raised = [jnp.exp(v) for v in shifted]
        total = raised[0] + raised[1] + raised[2] + raised[3]
        log_total = jnp.log(total)
        inv_total = 1.0 / total
        terms, zs, inv_widths = [], [], []
        for k in range(COMPS):
            width = jnp.maximum(raws[k], 0.0) + jnp.log1p(jnp.exp(-jnp.abs(raws[k]))) + scale_floor
            inv_width = 1.0 / width
            z = (y - means[k]) * inv_width
            terms.append((shifted[k] - log_total) - 0.5 * z * z - jnp.log(width) - half_log_tau)
            zs.append(z)
            inv_widths.append(inv_width)
        best = jnp.maximum(jnp.maximum(terms[0], terms[1]), jnp.maximum(terms[2], terms[3]))
        lifted = [jnp.exp(t - best) for t in terms]
        lift_total = lifted[0] + lifted[1] + lifted[2] + lifted[3]
        inv_lift = 1.0 / lift_total
        s.loss_acc[...] += jnp.where(weight > 0.0, -(best + jnp.log(lift_total)), 0.0)
        scale = -(weight * inv_n)
        for k in range(COMPS):
            share = lifted[k] * inv_lift
            d_term = scale * share
            ratio = zs[k] * inv_widths[k]
            d_logit = scale * (share - raised[k] * inv_total)
            d_width = d_term * (zs[k] * ratio - inv_widths[k])
            sigma = 1.0 / (1.0 + jnp.exp(-raws[k]))
            for kind, value in ((0, d_logit), (1, d_term * ratio), (2, d_width * sigma)):
                at = (4 * kind + k) * 128
                s.gparams[rs, at : at + 128] = value.astype(bf16)

    for kind in range(3):
        ks = slice(kind * 512, (kind + 1) * 512)
        wide = mm(s.nf_t[...], s.gparams[:, ks])
        pieces = swap_quarters([wide[:, k * 128 : (k + 1) * 128] for k in range(4)])
        for g in range(4):
            s.w_head[:, (3 * g + kind) * 128 : (3 * g + kind + 1) * 128] = pieces[g].astype(bf16)
    for g in range(4):
        gs = slice(g * GROUP, (g + 1) * GROUP)
        keep(M_HEAD, 0, 3 * g, mm_nt(s.w_head[:, gs], order[...]))
    s.inner[...] = mm_nt(s.gparams[...], s.w_headp[...])
    norm_back(s.last, s.inv_f, 2, None)

    s.normed[...] = s.grad[...].astype(bf16)

    @pl.loop(0, FF // 256)
    def _(j):
        js = tile(j, 256)
        keep(M_DOWN, 2 * j, 0, mm_tn(s.hidden[:, js], s.normed[...]))
        up_grad = mm_nt(s.normed[...], s.w_down[js, :])
        opening = s.gate[:, js]
        sigma = 1.0 / (1.0 + jnp.exp(-opening))
        s.ggu[:, js] = (up_grad * s.upper[:, js] * sigma * (1.0 + opening * (1.0 - sigma))).astype(bf16)
        s.ggu[:, tile(j + FF // 256, 256)] = (up_grad * opening * sigma).astype(bf16)


    @pl.loop(0, 2 * FF // 256)
    def _(j):
        js = tile(j, 256)
        keep(M_GU, 0, 2 * j, mm(s.nb_t[...], s.ggu[:, js]))

    s.inner[...] = mm_nt(s.ggu[...], s.w_gu[...])
    norm_back(s.middle, s.inv_b, 1, s.grad)

    s.normed[...] = s.grad[...].astype(bf16)
    keep(M_OUT, 0, 0, mm(s.merged_t[...], s.normed[...]))
    s.merged[...] = mm_nt(s.normed[...], s.w_out[...]).astype(bf16)
    s.bias_acc[...] = jnp.zeros_like(s.bias_acc)

    @pl.loop(0, HEADS // 2)
    def _(p):
        ps = tile(p, 128)
        qp, kp, vp, dop = s.qs[:, ps], s.ks[:, ps], s.vs[:, ps], s.merged[:, ps]
        kt = jnp.transpose(kp)
        dq, dk, dv = [], [], []
        for hh in range(2):
            mine = low_head if hh == 0 else jnp.logical_not(low_head)
            dom = jnp.where(mine, dop.astype(f32), 0.0).astype(bf16)
            same_sum = jnp.zeros((1, 128), f32)
            all_sum = jnp.zeros((1, 128), f32)
            for c in range(4):
                cs = slice(c * 128, (c + 1) * 128)
                prob = s.probs[2 * p + hh, :, cs]
                d_prob = mm_nt(vp, dom[cs, :])
                d_score = prob * (d_prob - jnp.sum(prob * d_prob, axis=0, keepdims=True))
                same_sum += jnp.sum(jnp.where(s.code_t[:, cs] > 1.5, d_score, 0.0), axis=0, keepdims=True)
                all_sum += jnp.sum(d_score, axis=0, keepdims=True)
                s.ggu[:, cs] = (d_score * HEAD_DIM**-0.5).astype(bf16)
            s.bias_acc[pl.ds(2 * p + hh, 1), :] = same_sum
            s.bias_acc[pl.ds(8 + 2 * p + hh, 1), :] = all_sum
            dv.append(mm(s.probs[2 * p + hh].astype(bf16), dop))
            dk.append(mm(s.ggu[:, :SEQ], qp))
            dq.append(mm(kt[hh * 64 : (hh + 1) * 64, :], s.ggu[:, :SEQ]))
        dqs = jnp.transpose(jnp.concatenate(dq, axis=0)).astype(bf16).astype(f32)
        dks = jnp.where(low_head, dk[0], dk[1]).astype(bf16).astype(f32)
        s.gparams[:, ps] = turn(dqs, -s.sin_t[...]).astype(bf16)
        s.gparams[:, tile(p + 3, 128)] = turn(dks, -s.sin_t[...]).astype(bf16)
        s.gparams[:, tile(p + 6, 128)] = jnp.where(low_head, dv[0], dv[1]).astype(bf16)

    for j in range(3):
        js = slice(j * D, (j + 1) * D)
        keep(M_QKV, 0, 3 * j, mm(s.na_t[...], s.gparams[:, js]))
    s.inner[...] = mm_nt(s.gparams[:, : 3 * D], s.w_qkv[...])
    norm_back(s.stream, s.inv_a, 0, s.grad)
    for c in range(3):
        cs = slice(c * 128, (c + 1) * 128)
        hidden_token = s.flag[...] == 1.0
        s.vec_acc[3:4, cs] = jnp.sum(jnp.where(hidden_token, s.grad[:, cs], 0.0), axis=0, keepdims=True)
        s.normed[:, cs] = jnp.where(hidden_token, 0.0, s.grad[:, cs]).astype(bf16)
    keep(M_IN, 0, 0, mm_tn(s.x5[...], s.normed[...]))

    sums = jnp.sum(s.bias_acc[...], axis=1, keepdims=True)
    sums = jnp.concatenate([sums[0:8], sums[8:16] - sums[0:8]], axis=0)
    entry = lax.broadcasted_iota(jnp.int32, (16, D), 0)
    target = jnp.where(entry < HEADS, entry, jnp.where((entry >= 8) & (entry < 8 + HEADS), entry - 8 + HEADS, -1))
    bias_row = jnp.sum(
        jnp.where(target == lax.broadcasted_iota(jnp.int32, (16, D), 1), sums, 0.0), axis=0, keepdims=True
    )
    row = lax.broadcasted_iota(jnp.int32, (8, D), 0)
    small_sum = jnp.where(row == 4, jnp.sum(s.loss_acc[...]), jnp.where(row == 5, bias_row, s.vec_acc[...]))
    for copy in outgoing + cross:
        copy.wait_send()
    send = Pool(send_pool)
    s.blocks[BLOCKS] = jnp.zeros((SIDE, SIDE), bf16)
    toks = dims[0] * dims[1] * dims[2]

    def fill(h):
        @pl.loop(0, toks)
        def _(t):
            for i in range(per):
                at = (h, t // (dims[1] * dims[2]), t // dims[2] % dims[1], t % dims[2], i)
                gathered[at] = s.blocks[holder[(h * toks + t) * per + i]]

    everywhere = (slice(None),) * 3
    parts = cut_parts(REDUCE_PARTS)
    fill(1 - head)
    arriving, outgoing = {}, []

    def start_reduce(p, k):
        axes, a, n = parts[p]
        if k == 0:
            view = everywhere + (slice(None), pl.ds(a, n))
            copies = [remote(gathered.at[(1 - head,) + view], crossed.at[view], send(), recv(), place.partner())]
        else:
            axis, left = axes[k - 1], axes[k:]
            copies = []
            for j in range(1, dims[axis]):
                region = place.region(left, {axis: place.coordinate(axis, j)})
                src = gathered.at[(head,) + region + (slice(None), pl.ds(a, n))]
                copies.append(remote(src, landing[3 * p + k - 1].at[j - 1], send(), recv(), place.peer(axis, j)))
        for copy in copies:
            copy.start()
        arriving[p] = copies
        outgoing.extend(copies)

    def end_reduce(p, k):
        axes, a, n = parts[p]
        left = sorted(axes[k:])
        region = place.region(left)
        for copy in arriving[p]:
            copy.wait_recv()

        def body(*index):
            at = tuple(index[left.index(i)] if i in left else region[i] for i in range(3)) + (slice(None), pl.ds(a, n))
            value = gathered[(head,) + at].astype(f32)
            if k == 0:
                value = value + crossed[at].astype(f32)
            else:
                for j in range(1, dims[axes[k - 1]]):
                    value = value + landing[3 * p + k - 1][(j - 1,) + index].astype(f32)
            if k < 3:
                gathered[(head,) + at] = value.astype(bf16)
            else:
                owned[:, a : a + n, :] = value

        def loops(index):
            if len(index) == len(left):
                body(*index)
            else:
                pl.loop(0, dims[left[len(index)]])(lambda i: loops(index + (i,)))

        loops(())

    begun = set()
    for group in REDUCE_GROUPS[:REDUCE_WINDOW]:
        for p in group:
            start_reduce(p, 0)
            begun.add(p)
    vec_sum = all_sum(place, small_sum, vec_buf, send, recv)
    vec_total = next(vec_sum)
    fill(head)

    def start(p, k):
        if k > 0 or p not in begun:
            start_reduce(p, k)

    def finish(p, k):
        nonlocal vec_total
        end_reduce(p, k)
        if vec_total is None and k == 1:
            vec_total = next(vec_sum)

    pipeline(REDUCE_GROUPS, 4, REDUCE_WINDOW, start, finish)
    while vec_total is None:
        vec_total = next(vec_sum)
    part_square = jnp.zeros((8, 128), f32)
    for i in range(per):
        piece = owned[i]
        part_square = part_square + jnp.sum((piece * piece).reshape(16, 8, 128), axis=0)
    sq_sum = all_sum(place, part_square, sq_buf, send, recv)
    total = next(sq_sum)
    for i in range(per):
        grad = owned[i]
        gram_left[i] = lax.dot_general(grad, grad, (((1,), (1,)), ((), ())), precision=highest, preferred_element_type=f32)
        turned = jnp.transpose(grad)
        gram_right[i] = jnp.dot(turned, grad, precision=highest, preferred_element_type=f32)
    while total is None:
        total = next(sq_sum)

    grads4 = vec_total[0:4]
    bias_total = vec_total[5:6, 0 : 2 * HEADS]
    square = jnp.sum(total) + jnp.sum(grads4 * grads4) + jnp.sum(bias_total * bias_total)
    grad_norm = jnp.sqrt(jnp.broadcast_to(square, (8, 128)))
    factor = jnp.minimum(1.0, clip_limit / grad_norm)
    loss_out[0, 0] = vec_total[4, 0]
    norm_out[0, 0] = jnp.max(grad_norm)
    factor_out[0, 0] = jnp.max(factor)
    small_out[...] = vec_total
    for copy in outgoing:
        copy.wait_send()


def update_kernel(
    factor_ref, small, vectors, vector_first, vector_second, var_bias, bias_first, bias_second, *rest,
):
    sources, rest = rest[:8], rest[8:]
    clipped_out, left_out, right_out, master_out = rest[:4]
    vector_grads, vector_second_new, vector_new, bias_grads, bias_second_new, bias_new = rest[4:10]
    held, made, in_sem, out_sem = rest[10:]
    fetches = [pltpu.make_async_copy(ref, held.at[k], in_sem.at[k]) for k, ref in enumerate(sources)]
    for copy in fetches:
        copy.start()
    owned, left_root, right_root, gram_left, left, gram_right, right, master = (held.at[k] for k in range(8))
    sends = [
        pltpu.make_async_copy(made.at[k], ref, out_sem.at[k])
        for k, ref in enumerate((clipped_out, left_out, right_out, master_out))
    ]
    factor = factor_ref[0, 0]
    per = owned.shape[0]
    fetches[0].wait()
    fetches[1].wait()
    grads = [owned[i] * factor for i in range(per)]
    for i in range(per):
        made[0, i] = grads[i]
    sends[0].start()
    shaped = [jnp.dot(left_root[i], grads[i], precision=highest, preferred_element_type=f32) for i in range(per)]
    fetches[2].wait()
    shaped = [jnp.dot(shaped[i], right_root[i], precision=highest, preferred_element_type=f32) for i in range(per)]
    for copy in fetches[3:]:
        copy.wait()
    for k, (stat, gram) in enumerate(((left, gram_left), (right, gram_right))):
        for i in range(per):
            scaled = jnp.where(factor > 0.0, gram[i] * factor * factor, 0.0)
            made[1 + k, i] = stat_beta * stat[i] + (1.0 - stat_beta) * scaled
        sends[1 + k].start()
    for i in range(per):
        unit = shaped[i] * lax.rsqrt(jnp.sum(shaped[i] * shaped[i]) / (SIDE * SIDE) + root_eps)
        made[3, i] = master[i] - mat_rate * (unit + decay_rate * master[i])
    sends[3].start()

    def adamw(gradient, first, second, old, grad_out, second_out, new_out):
        gradient = gradient * factor
        grad_out[...] = gradient
        first_next = beta_one * first[...] + (1.0 - beta_one) * gradient
        second_next = beta_two * second[...] + (1.0 - beta_two) * gradient * gradient
        ratio = first_next / (1.0 - beta_one**STEP) / (jnp.sqrt(second_next / (1.0 - beta_two**STEP)) + adam_eps)
        second_out[...] = second_next
        new_out[...] = old[...] - vec_rate * (ratio + decay_rate * old[...])

    adamw(small[0:4], vector_first, vector_second, vectors, vector_grads, vector_second_new, vector_new)
    adamw(small[5:6, 0 : 2 * HEADS], bias_first, bias_second, var_bias, bias_grads, bias_second_new, bias_new)
    for copy in sends:
        copy.wait()


def update_call(factor, small, owned, gram_left, gram_right, master, left, right, left_root, right_root, *rest):
    vmem, hbm = pl.BlockSpec(memory_space=pltpu.VMEM), pl.BlockSpec(memory_space=pl.ANY)
    sources = (owned, left_root, right_root, gram_left, left, gram_right, right, master)
    vectors, var_bias = rest[0], rest[3]
    outs = [master] * 4 + [vectors] * 3 + [var_bias] * 3
    return pl.pallas_call(
        update_kernel,
        out_shape=tuple(jax.ShapeDtypeStruct(a.shape, f32) for a in outs),
        in_specs=[pl.BlockSpec(memory_space=pltpu.SMEM)] + [vmem] * (1 + len(rest)) + [hbm] * 8,
        out_specs=(hbm,) * 4 + (vmem,) * 6,
        scratch_shapes=[
            pltpu.VMEM((8,) + master.shape, f32),
            pltpu.VMEM((4,) + master.shape, f32),
            pltpu.SemaphoreType.DMA((8,)),
            pltpu.SemaphoreType.DMA((4,)),
        ],
        compiler_params=pltpu.CompilerParams(vmem_limit_bytes=60 * 2**20),
        name="update",
    )(factor, small, *rest, *sources)


def step_call(dims, places, holder, lengths, bias, master, patches, sizes, times, predict, variates, vectors):
    freq = (10000.0 ** (-np.arange(HEAD_DIM // 2) / (HEAD_DIM // 2))).astype(np.float32)
    freq = jnp.asarray(np.tile(freq[None], (8, 4)))
    per = master.shape[0]
    half = patches.shape[2]
    received, sent = semaphores(dims)
    smem = pl.BlockSpec(memory_space=pltpu.SMEM)
    vmem = pl.BlockSpec(memory_space=pltpu.VMEM)
    sems = pltpu.SemaphoreType.DMA
    landing = []
    for axes, _, n in cut_parts(REDUCE_PARTS):
        for k in range(3):
            wide = [dims[i] for i in sorted(axes[k + 1 :])]
            landing.append(pltpu.VMEM((max(dims[axes[k]] - 1, 1), *wide, per, n, SIDE), bf16))
    return pl.pallas_call(
        functools.partial(step_kernel, dims),
        out_shape=tuple(
            jax.ShapeDtypeStruct(shape, f32)
            for shape in [(1, 1)] * 4 + [(8, D)] + [(per, SIDE, SIDE)] * 3
        ),
        in_specs=[smem] * 4 + [vmem] * 9,
        out_specs=(smem,) * 4 + (vmem,) * 4,
        scratch_shapes=[pltpu.VMEM(shape, dtype) for shape, dtype in SCRATCH.values()]
        + [
            pltpu.VMEM((per, SIDE, SIDE), bf16),
            pltpu.VMEM((2,) + dims + (per, SIDE, SIDE), bf16),
            pltpu.VMEM(dims + (per, SIDE, SIDE), bf16),
            pltpu.VMEM((half, PMAX), bf16),
            pltpu.VMEM((3, 2, half), jnp.int32),
            pltpu.VMEM((3, 2, half), jnp.int32),
            sum_shape(dims, (8, 128)),
            sum_shape(dims, (8, D)),
            sum_shape(dims, (8, 128)),
            sems,
            sems((sent,)),
            sems((received,)),
            *landing,
        ],
        compiler_params=pltpu.CompilerParams(
            collective_id=0, has_side_effects=True, vmem_limit_bytes=63 * 2**20
        ),
        name="step",
    )(places, holder, lengths, bias, master, patches, sizes, times, predict, variates, vectors, freq,
      jnp.asarray(group_order(), bf16))


def shards(
    dims,
    patches, patch_sizes, sample_lengths, variate_ids, time_ids, predict_mask, block_owner_slot,
    master_blocks, left_stats, right_stats, left_roots, right_roots,
    vectors, vector_first, vector_second, var_bias, bias_first, bias_second,
):
    slot_count = master_blocks.shape[0] * lax.axis_size("head") * lax.axis_size("tok")
    match = block_owner_slot[None, :] == jnp.arange(slot_count)[:, None]
    holder = BLOCKS + jnp.sum(jnp.where(match, jnp.arange(BLOCKS)[None, :] - BLOCKS, 0), axis=1)
    device, inside = block_owner_slot // master_blocks.shape[0], block_owner_slot % master_blocks.shape[0]
    places = [device // (dims[0] * dims[1] * dims[2])]
    places += [device // (dims[1] * dims[2]) % dims[0], device // dims[2] % dims[1], device % dims[2], inside]
    loss_sum, count, grad_norm, factor, small, owned, gram_left, gram_right = step_call(
        dims, jnp.stack(places), holder, sample_lengths, var_bias[0], master_blocks, patches, patch_sizes, time_ids,
        predict_mask, variate_ids, vectors,
    )
    outs = update_call(
        factor, small, owned, gram_left, gram_right, master_blocks, left_stats, right_stats, left_roots, right_roots,
        vectors, vector_first, vector_second, var_bias, bias_first, bias_second,
    )
    return (loss_sum.reshape(()), count.reshape(()), grad_norm.reshape(())) + tuple(outs)


def solution(mesh):
    rep = P()
    dims = tok_dims(mesh.shape["tok"])
    slot = P(("head", "tok"), None, None)
    return jax.shard_map(
        functools.partial(shards, dims),
        mesh=mesh,
        in_specs=(
            P(None, "tok", "head", None), P(None, "tok", "head"), P(None, "tok", None), P(None, "tok", None),
            P(None, "tok", "head"), P(None, "tok", "head"), rep, slot, slot, slot, slot, slot,
            rep, rep, rep, rep, rep, rep,
        ),
        out_specs=(rep, rep, rep, slot, slot, slot, slot, rep, rep, rep, rep, rep, rep),
        check_vma=False,
    )
```

```python
import functools
import itertools
import math

import jax
import jax.numpy as jnp
import numpy as np
from jax import lax
from jax.experimental import pallas as pl
from jax.experimental.pallas import tpu as pltpu
from jax.sharding import PartitionSpec as P

D = 384
FF = 1024
HEADS = 6
HEAD_DIM = 64
PSIZES = 5
PMAX = 128
COMPS = 4
SEQ = 512
SIDE = 128
STEP = 10
HEADCOLS = 3 * COMPS * PMAX
BLOCKS = 159

norm_eps = 1e-06
scale_floor = 0.05
half_log_tau = 0.9189385332046727
clip_limit = 0.02
mat_rate = 0.01
vec_rate = 0.3
decay_rate = 0.01
beta_one = 0.9
beta_two = 0.95
stat_beta = 0.99
root_eps = 1e-06
adam_eps = 1e-08
highest = lax.Precision.HIGHEST
f32 = jnp.float32
bf16 = jnp.bfloat16

GRIDS = ((5, 3), (3, 12), (3, 9), (3, 3), (3, 16), (8, 3))
FIRSTS = (0, 15, 51, 78, 87, 135)
M_IN, M_HEAD, M_QKV, M_OUT, M_GU, M_DOWN = range(6)


def mm(a, b):
    return jnp.dot(a, b, preferred_element_type=f32)


def mm_nt(a, b):
    return lax.dot_general(a, b, (((1,), (1,)), ((), ())), preferred_element_type=f32)


def mm_tn(a, b):
    return lax.dot_general(a, b, (((0,), (0,)), ((), ())), preferred_element_type=f32)


GROUP = 384


def group_order():
    order = np.zeros((GROUP, GROUP), np.float32)
    for col in range(GROUP):
        order[col, (col % 12) * 32 + col // 12] = 1.0
    return order


def swap_quarters(parts):
    lane = lax.broadcasted_iota(jnp.int32, (1, 128), 1)
    low, even = lane < 64, lane % 64 < 32
    a, b, c, d = parts
    a, c = jnp.where(low, a, pltpu.roll(c, 64, 1)), jnp.where(low, pltpu.roll(a, 64, 1), c)
    b, d = jnp.where(low, b, pltpu.roll(d, 64, 1)), jnp.where(low, pltpu.roll(b, 64, 1), d)
    a, b = jnp.where(even, a, pltpu.roll(b, 32, 1)), jnp.where(even, pltpu.roll(a, 96, 1), b)
    c, d = jnp.where(even, c, pltpu.roll(d, 32, 1)), jnp.where(even, pltpu.roll(c, 96, 1), d)
    return a, b, c, d


SCRATCH = dict(
    w_in=((640, D), bf16), w_head=((D, HEADCOLS), bf16), w_qkv=((D, 3 * D), bf16), w_out=((D, D), bf16),
    w_gu=((D, 2 * FF), bf16), w_down=((FF, D), bf16), w_headp=((D, HEADCOLS), bf16),
    blocks=((BLOCKS + 1, SIDE, SIDE), bf16),
    x5=((SEQ, 640), bf16), weight=((SEQ, PMAX), f32), flag=((SEQ, 128), f32),
    cos_t=((SEQ, 128), f32), sin_t=((SEQ, 128), f32),
    code_t=((SEQ, SEQ), f32), probs=((HEADS, SEQ, SEQ), f32),
    stream=((SEQ, D), f32), middle=((SEQ, D), f32), last=((SEQ, D), f32), grad=((SEQ, D), f32), inner=((SEQ, D), f32),
    inv_a=((SEQ, 128), f32), inv_b=((SEQ, 128), f32), inv_f=((SEQ, 128), f32),
    normed=((SEQ, D), bf16), na_t=((D, SEQ), bf16), nb_t=((D, SEQ), bf16), nf_t=((D, SEQ), bf16),
    qs=((SEQ, D), bf16), ks=((SEQ, D), bf16), vs=((SEQ, D), bf16), merged=((SEQ, D), bf16), merged_t=((D, SEQ), bf16),
    silu=((SEQ, FF), f32), slope=((SEQ, FF), f32), hidden=((SEQ, FF), bf16),
    params=((SEQ, HEADCOLS), f32), gparams=((SEQ, HEADCOLS), bf16), ggu=((SEQ, 2 * FF), bf16),
    loss_acc=((32, 128), f32), bias_acc=((16, 128), f32), vec_acc=((8, D), f32),
    meta=((8, SEQ), jnp.int32), row_patches=((SEQ, PMAX), bf16),
)


def tile(i, size):
    return pl.ds(pl.multiple_of(i * size, size), size)


MESH = pl.DeviceIdType.MESH


def tok_dims(count):
    return {16: (4, 2, 2), 128: (4, 4, 8)}.get(count, (count, 1, 1))


class Place:
    def __init__(self, dims):
        self.dims = dims
        self.head = lax.axis_index("head")
        tok = lax.axis_index("tok")
        self.tok = tok
        self.strides = (dims[1] * dims[2], dims[2], 1)
        self.at = [lax.rem(lax.div(tok, s), n) for s, n in zip(self.strides, dims)]

    def coordinate(self, axis, step):
        return lax.rem(self.at[axis] + step, self.dims[axis])

    def peer(self, axis, step):
        return (self.head, self.tok + (self.coordinate(axis, step) - self.at[axis]) * self.strides[axis])

    def partner(self):
        return (1 - self.head, self.tok)

    def groups(self):
        result, size = [[None]], 2
        for axis in (1, 2, 0):
            if self.dims[axis] == 1:
                continue
            if size * self.dims[axis] > 8:
                result.append([])
                size = 1
            result[-1].append(axis)
            size *= self.dims[axis]
        return result

    def members(self, group):
        sizes = [2 if axis is None else self.dims[axis] for axis in group]
        mine = 0
        for axis, n in zip(group, sizes):
            mine = mine * n + (self.head if axis is None else self.at[axis])
        others = []
        for steps in itertools.product(*[range(n) for n in sizes]):
            head, tok = self.head, self.tok
            for axis, step in zip(group, steps):
                if axis is None:
                    head = lax.rem(head + step, 2)
                else:
                    tok = tok + (self.coordinate(axis, step) - self.at[axis]) * self.strides[axis]
            if any(steps):
                others.append((head, tok))
        return mine, math.prod(sizes), others

    def greet(self, meanwhile):
        barrier = pltpu.get_barrier_semaphore()
        groups = self.groups()
        others = [other for group in groups for other in self.members(group)[2]]
        joint = [group for group in groups if len(group) > 1]
        singles = {group[0] for group in groups if len(group) == 1} | {a for group in joint for a in group}
        others += [self.peer(a, j) for a in range(3) if a not in singles for j in range(1, self.dims[a])]
        for other in others:
            pl.semaphore_signal(barrier, inc=1, device_id=other, device_id_type=MESH)
        meanwhile()
        pl.semaphore_wait(barrier, len(others))

    def region(self, whole, fixed=None):
        fixed = fixed or {}
        return tuple(slice(None) if a in whole else fixed.get(a, self.at[a]) for a in range(3))


def remote(src, dst, send, recv, device):
    return pltpu.make_async_remote_copy(
        src_ref=src, dst_ref=dst, send_sem=send, recv_sem=recv, device_id=device, device_id_type=MESH
    )


def split_rows(rows, shares):
    units = rows // 16
    edges = [round(units * sum(shares[:i]) / sum(shares)) * 16 for i in range(len(shares) + 1)]
    return [(a, b - a) for a, b in zip(edges, edges[1:])]


class Pool:
    def __init__(self, ref):
        self.ref, self.used = ref, 0

    def __call__(self):
        self.used += 1
        return self.ref.at[self.used - 1]


def all_sum(place, values, buf, send, recv):
    total = values
    for k, group in enumerate(place.groups()):
        mine, size, others = place.members(group)
        buf[k, mine] = total
        copies = [remote(buf.at[k, mine], buf.at[k, mine], send(), recv(), other) for other in others]
        for copy in copies:
            copy.start()
        yield None
        for copy in copies:
            copy.wait()
        total = buf[k, 0]
        for i in range(1, size):
            total = total + buf[k, i]
    yield total


def sum_sizes(dims):
    place = Place.__new__(Place)
    place.dims = dims
    return [math.prod(2 if a is None else dims[a] for a in group) for group in place.groups()]


def sum_shape(dims, shape):
    sizes = sum_sizes(dims)
    return pltpu.VMEM((len(sizes), max(sizes)) + shape, f32)


GATHER_PARTS = (((0, 1, 2), 1), ((0, 2, 1), 1)) * 4
GATHER_GROUPS = ((0, 1), (2, 3), (4, 5), (6, 7))
GATHER_WINDOW = 1
REDUCE_PARTS = (((2, 1, 0), 1), ((1, 2, 0), 1)) * 4
REDUCE_GROUPS = ((0, 1), (2, 3), (4, 5), (6, 7))
REDUCE_WINDOW = 4


def cut_parts(table):
    return [(order, a, n) for (order, _), (a, n) in zip(table, split_rows(SIDE, [s for _, s in table]))]


def pipeline(groups, phases, window, start, finish):
    for group in groups[:window]:
        for p in group:
            start(p, 0)
    for t in range(len(groups) + phases - 1):
        for k in range(phases):
            if not 0 <= t - k < len(groups):
                continue
            for p in groups[t - k]:
                finish(p, k)
                if k + 1 < phases:
                    start(p, k + 1)
            if k == 0:
                for p in groups[t + window] if t + window < len(groups) else ():
                    start(p, 0)


def semaphores(dims):
    steps = sum(n - 1 for n in dims)
    sums = sum(n - 1 for n in sum_sizes(dims))
    gather = sum(steps + 1 + sum(dims[a] - 1 for a in order[1:]) for order, _ in GATHER_PARTS) + 2 + sums
    reduce = len(REDUCE_PARTS) * (steps + 1) + 2 * sums
    return gather + reduce, max(gather, reduce)


def step_kernel(
    dims, places, holder, lengths, bias, master, patches, sizes, times_in, predict_in, variates_in, vectors, freq, order,
    loss_out, count_out, norm_out, factor_out, small_out, owned, gram_left, gram_right, *rest,
):
    names = list(SCRATCH)
    s = type("S", (), dict(zip(names, rest)))
    rest = rest[len(names) :]
    mine, gathered, crossed, land_patch, land_ints, own_ints = rest[:6]
    cnt_buf, vec_buf, sq_buf, own_sem, send_pool, recv_pool = rest[6:12]
    send, recv = Pool(send_pool), Pool(recv_pool)
    landing = rest[12:]
    place = Place(dims)
    per = mine.shape[0]
    head = place.head
    lane = lax.broadcasted_iota(jnp.int32, (1, 128), 1)
    first_half = lane % HEAD_DIM < HEAD_DIM // 2
    low_head = lane < HEAD_DIM
    weights = (s.w_in, s.w_head, s.w_qkv, s.w_out, s.w_gu, s.w_down)

    def keep(m, r0, c0, value):
        value = value.astype(bf16)
        cols = GRIDS[m][1]
        for r in range(value.shape[0] // SIDE):
            for c in range(value.shape[1] // SIDE):
                piece = value[r * SIDE : (r + 1) * SIDE, c * SIDE : (c + 1) * SIDE]
                s.blocks[FIRSTS[m] + (r0 + r) * cols + c0 + c] = piece

    half = SEQ // 2
    s.meta[4:8, :] = jnp.zeros((4, SEQ), jnp.int32)

    def local_work():
        mine[...] = master[...].astype(bf16)
        for k, ref in enumerate((sizes, times_in, predict_in)):
            own_ints[k, :, :] = ref[:, 0, :]
        for h in range(2):

            @pl.when(head == h)
            def _():
                here = slice(h * half, (h + 1) * half)
                s.row_patches[here, :] = patches[h, 0]
                for k, ref in enumerate((sizes, times_in, predict_in)):
                    s.meta[k : k + 1, here] = ref[h]
                s.meta[3:4, :] = variates_in[h]

    place.greet(local_work)
    swaps = [
        remote(patches.at[1 - head, 0], land_patch, send(), recv(), place.partner()),
        remote(own_ints, land_ints, send(), recv(), place.partner()),
    ]
    for copy in swaps:
        copy.start()
    parts = cut_parts(GATHER_PARTS)

    def block(head_index, whole, fixed, a, n):
        return gathered.at[(head_index,) + place.region(whole, fixed) + (slice(None), pl.ds(a, n))]

    arriving, outgoing, cross = {}, list(swaps), []
    own = pltpu.make_async_copy(mine, gathered.at[(head,) + place.region(())], own_sem)
    own.start()

    def start_gather(p, k):
        axes, a, n = parts[p]
        axis, whole = axes[k], axes[:k]
        arriving[p] = []
        for j in range(1, dims[axis]):
            src = mine.at[:, pl.ds(a, n)] if k == 0 else block(head, whole, None, a, n)
            copy = remote(src, block(head, whole, None, a, n), send(), recv(), place.peer(axis, j))
            copy.start()
            arriving[p].append(copy)
        outgoing.extend(arriving[p])

    def end_gather(p, k):
        axes, a, n = parts[p]
        for copy in arriving[p]:
            copy.wait_recv()
        axis, whole = axes[k], axes[:k]
        if k == 0:
            views = [block(head, axes[:1], None, a, n)]
        else:
            views = [
                block(head, whole, {axis: place.coordinate(axis, dims[axis] - j)}, a, n) for j in range(1, dims[axis])
            ]
        for view in views:
            copy = remote(view, view, send(), recv(), place.partner())
            copy.start()
            cross.append(copy)

    for p in GATHER_GROUPS[0]:
        start_gather(p, 0)
    wide_size = jnp.zeros_like(own_ints[0])
    for c in range(PSIZES):
        wide_size = wide_size + jnp.where(own_ints[0] == c, PMAX * 2**c // 2 ** (PSIZES - 1), 0)
    partial = (wide_size * own_ints[2]).astype(f32)
    partial = jnp.sum(partial[:, :128] + partial[:, 128:], axis=0, keepdims=True)
    counting = all_sum(place, jnp.concatenate([partial, jnp.zeros((7, 128), f32)], axis=0), cnt_buf, send, recv)
    counted = next(counting)
    own.wait()
    for copy in swaps:
        copy.wait_recv()
    for h in range(2):

        @pl.when(head == h)
        def _():
            there = slice((1 - h) * half, (2 - h) * half)
            s.row_patches[there, :] = land_patch[...]
            for k in range(3):
                s.meta[k : k + 1, there] = land_ints[k, h : h + 1, :]

    def prepare_tokens():
        metaf = s.meta[...].astype(f32)
        columns = jnp.transpose(metaf)
        codes, times, flag = columns[:, 0:1], columns[:, 1:2], columns[:, 2:3]
        position = lax.broadcasted_iota(jnp.int32, (1, SEQ), 1)
        ids = jnp.zeros((1, SEQ), f32)
        end = jnp.int32(0)
        for j in range(lengths.shape[2]):
            end = end + lengths[head, 0, j]
            ids = ids + jnp.where(position >= end, 1.0, 0.0)
        variates = metaf[3:4]
        id_columns = jnp.transpose(jnp.concatenate([ids] * 8, axis=0))[:, 0:1]
        var_columns = columns[:, 3:4]
        for c in range(4):
            cs = slice(c * 128, (c + 1) * 128)
            same_sample = id_columns == ids[:, cs]
            same_var = var_columns == variates[:, cs]
            s.code_t[:, cs] = jnp.where(same_sample, jnp.where(same_var, 2.0, 1.0), 0.0)
        s.flag[...] = jnp.broadcast_to(flag, (SEQ, 128))
        angle = times * freq[0:1, :]
        s.cos_t[...] = jnp.cos(angle)
        s.sin_t[...] = jnp.where(first_half, -1.0, 1.0) * jnp.sin(angle)

        wide = s.row_patches[...].astype(f32)
        weight = jnp.zeros((SEQ, PMAX), f32)
        for c in range(PSIZES):
            keep = (codes == float(c)) & (lane < PMAX * 2**c // 2 ** (PSIZES - 1))
            s.x5[:, c * 128 : (c + 1) * 128] = jnp.where(keep, wide, 0.0).astype(bf16)
            weight = jnp.where(keep, 1.0, weight)
        s.weight[...] = jnp.where(flag == 1.0, weight, 0.0)
    begun = set(GATHER_GROUPS[0])
    ended = []

    def start(p, k):
        if k > 0 or p not in begun:
            start_gather(p, k)

    def finish(p, k):
        nonlocal counted
        end_gather(p, k)
        if counted is None:
            counted = next(counting)
        ended.append(p)
        if len(ended) == len(GATHER_GROUPS[0]):
            prepare_tokens()

    pipeline(GATHER_GROUPS, 3, GATHER_WINDOW, start, finish)
    while counted is None:
        counted = next(counting)
    value_count = jnp.sum(counted)
    count_out[0, 0] = value_count
    for copy in cross:
        copy.wait_recv()

    def load(m):
        n_rows, cols = GRIDS[m]

        @pl.loop(0, n_rows)
        def _(r):
            for c in range(cols):
                b = FIRSTS[m] + r * cols + c
                weights[m][tile(r, SIDE), c * SIDE : (c + 1) * SIDE] = gathered[tuple(places[k, b] for k in range(5))]

    for m in range(6):
        load(m)

    def turn(v, sine):
        swapped = jnp.where(first_half, pltpu.roll(v, 96, 1), pltpu.roll(v, 32, 1))
        return v * s.cos_t[...] + swapped * sine

    embedded = mm(s.x5[...], s.w_in[...])
    for c in range(3):
        cs = slice(c * 128, (c + 1) * 128)
        s.stream[:, cs] = jnp.where(s.flag[...] == 1.0, vectors[3:4, cs], embedded[:, cs])

    def norm(src, inv_ref, gain, dst_t):
        @pl.loop(0, SEQ // 128)
        def _(i):
            rs = tile(i, 128)
            v = src[rs, :]
            inverse = lax.rsqrt(jnp.sum(v * v, axis=-1, keepdims=True) / D + norm_eps)
            inv_ref[rs, :] = jnp.broadcast_to(inverse, (128, 128))
            s.normed[rs, :] = (v * inverse * gain).astype(bf16)

        dst_t[...] = jnp.transpose(s.normed[...])

    def norm_back(src, inv_ref, row, extra):
        gain = vectors[row : row + 1, :]

        @pl.loop(0, SEQ // 128)
        def _(i):
            rs = tile(i, 128)
            up = s.inner[rs, :]
            inverse = inv_ref[rs, 0:1]
            scaled = src[rs, :] * inverse
            inner = up * gain
            mean = jnp.sum(inner * scaled, axis=-1, keepdims=True) / D
            result = inverse * (inner - scaled * mean)
            s.grad[rs, :] = result if extra is None else result + extra[rs, :]
            s.vec_acc[row : row + 1, :] += jnp.sum(up * scaled, axis=0, keepdims=True)

    s.vec_acc[...] = jnp.zeros_like(s.vec_acc)
    norm(s.stream, s.inv_a, vectors[0:1, :], s.na_t)
    for part, dst in ((0, s.qs), (1, s.ks), (2, s.vs)):
        mixed = mm(s.normed[...], s.w_qkv[:, part * D : (part + 1) * D])
        for c in range(3):
            piece = mixed[:, c * 128 : (c + 1) * 128]
            if part < 2:
                piece = turn(piece, s.sin_t[...])
            dst[:, c * 128 : (c + 1) * 128] = piece.astype(bf16)

    @pl.loop(0, HEADS // 2)
    def _(p):
        ps = tile(p, 128)
        qp, kp = s.qs[:, ps], s.ks[:, ps]
        vt = jnp.transpose(s.vs[:, ps])
        outs = []
        for hh in range(2):
            mine = low_head if hh == 0 else jnp.logical_not(low_head)
            qm = jnp.where(mine, qp.astype(f32) * HEAD_DIM**-0.5, 0.0).astype(bf16)
            b0 = bias[2 * p + hh]
            b1 = bias[HEADS + 2 * p + hh]
            parts = []
            for c in range(1):
                cs = slice(c * 512, (c + 1) * 512)
                code = s.code_t[:, cs]
                score = mm_nt(kp, qm[cs, :])
                score = jnp.where(code > 0.5, score + jnp.where(code > 1.5, b0, b1), -1e30)
                raised = jnp.exp(score - jnp.max(score, axis=0, keepdims=True))
                prob = raised * (1.0 / jnp.sum(raised, axis=0, keepdims=True))
                s.probs[2 * p + hh, :, cs] = prob
                parts.append(mm(vt[hh * 64 : (hh + 1) * 64, :], prob.astype(bf16)))
            outs.append(jnp.concatenate(parts, axis=1))
        out_t = jnp.concatenate(outs, axis=0).astype(bf16)
        s.merged_t[ps, :] = out_t
        s.merged[:, ps] = jnp.transpose(out_t)

    s.middle[...] = s.stream[...] + mm(s.merged[...], s.w_out[...])
    norm(s.middle, s.inv_b, vectors[1:2, :], s.nb_t)

    @pl.loop(0, FF // 1024)
    def _(j):
        js = tile(j, 1024)
        opening = mm(s.normed[...], s.w_gu[:, js])
        up = mm(s.normed[...], s.w_gu[:, tile(j + FF // 1024, 1024)])
        sigma = 1.0 / (1.0 + jnp.exp(-opening))
        silu = opening * sigma
        s.silu[:, js] = silu
        s.slope[:, js] = up * sigma * (1.0 + opening * (1.0 - sigma))
        s.hidden[:, js] = (silu * up).astype(bf16)

    s.last[...] = s.middle[...] + mm(s.hidden[...], s.w_down[...])
    norm(s.last, s.inv_f, vectors[2:3, :], s.nf_t)


    for kind in range(3):
        pieces = [
            mm(s.w_head[:, g * GROUP : (g + 1) * GROUP], order[:, kind * 128 : (kind + 1) * 128]) for g in range(4)
        ]
        for k, piece in enumerate(swap_quarters(pieces)):
            at = (4 * kind + k) * 128
            s.w_headp[:, at : at + 128] = piece.astype(bf16)

    @pl.loop(0, HEADCOLS // 512)
    def _(j):
        js = tile(j, 512)
        s.params[:, js] = mm(s.normed[...], s.w_headp[:, js])

    inv_n = 1.0 / value_count
    s.loss_acc[...] = jnp.zeros_like(s.loss_acc)

    @pl.loop(0, SEQ // 32)
    def _(i):
        rs = tile(i, 32)
        y = s.row_patches[rs, :].astype(f32)
        weight = s.weight[rs, :]
        logits, means, raws = [
            [s.params[rs, (4 * kind + k) * 128 : (4 * kind + k + 1) * 128] for k in range(COMPS)] for kind in range(3)
        ]
        top = jnp.maximum(jnp.maximum(logits[0], logits[1]), jnp.maximum(logits[2], logits[3]))
        shifted = [v - top for v in logits]
        raised = [jnp.exp(v) for v in shifted]
        total = raised[0] + raised[1] + raised[2] + raised[3]
        log_total = jnp.log(total)
        inv_total = 1.0 / total
        terms, zs, inv_widths = [], [], []
        for k in range(COMPS):
            width = jnp.maximum(raws[k], 0.0) + jnp.log1p(jnp.exp(-jnp.abs(raws[k]))) + scale_floor
            inv_width = 1.0 / width
            z = (y - means[k]) * inv_width
            terms.append((shifted[k] - log_total) - 0.5 * z * z - jnp.log(width) - half_log_tau)
            zs.append(z)
            inv_widths.append(inv_width)
        best = jnp.maximum(jnp.maximum(terms[0], terms[1]), jnp.maximum(terms[2], terms[3]))
        lifted = [jnp.exp(t - best) for t in terms]
        lift_total = lifted[0] + lifted[1] + lifted[2] + lifted[3]
        inv_lift = 1.0 / lift_total
        s.loss_acc[...] += jnp.where(weight > 0.0, -(best + jnp.log(lift_total)), 0.0)
        scale = -(weight * inv_n)
        for k in range(COMPS):
            share = lifted[k] * inv_lift
            d_term = scale * share
            ratio = zs[k] * inv_widths[k]
            d_logit = scale * (share - raised[k] * inv_total)
            d_width = d_term * (zs[k] * ratio - inv_widths[k])
            sigma = 1.0 / (1.0 + jnp.exp(-raws[k]))
            for kind, value in ((0, d_logit), (1, d_term * ratio), (2, d_width * sigma)):
                at = (4 * kind + k) * 128
                s.gparams[rs, at : at + 128] = value.astype(bf16)

    for kind in range(3):
        ks = slice(kind * 512, (kind + 1) * 512)
        wide = mm(s.nf_t[...], s.gparams[:, ks])
        pieces = swap_quarters([wide[:, k * 128 : (k + 1) * 128] for k in range(4)])
        for g in range(4):
            s.w_head[:, (3 * g + kind) * 128 : (3 * g + kind + 1) * 128] = pieces[g].astype(bf16)
    for g in range(4):
        gs = slice(g * GROUP, (g + 1) * GROUP)
        keep(M_HEAD, 0, 3 * g, mm_nt(s.w_head[:, gs], order[...]))
    s.inner[...] = mm_nt(s.gparams[...], s.w_headp[...])
    norm_back(s.last, s.inv_f, 2, None)

    s.normed[...] = s.grad[...].astype(bf16)

    @pl.loop(0, FF // 1024)
    def _(j):
        js = tile(j, 1024)
        keep(M_DOWN, 8 * j, 0, mm_tn(s.hidden[:, js], s.normed[...]))
        up_grad = mm_nt(s.normed[...], s.w_down[js, :])
        s.ggu[:, js] = (up_grad * s.slope[:, js]).astype(bf16)
        s.ggu[:, tile(j + FF // 1024, 1024)] = (up_grad * s.silu[:, js]).astype(bf16)

    @pl.loop(0, 2 * FF // 512)
    def _(j):
        keep(M_GU, 0, 4 * j, mm(s.nb_t[...], s.ggu[:, tile(j, 512)]))

    s.inner[...] = mm_nt(s.ggu[...], s.w_gu[...])
    norm_back(s.middle, s.inv_b, 1, s.grad)

    s.normed[...] = s.grad[...].astype(bf16)
    keep(M_OUT, 0, 0, mm(s.merged_t[...], s.normed[...]))
    s.merged[...] = mm_nt(s.normed[...], s.w_out[...]).astype(bf16)
    s.bias_acc[...] = jnp.zeros_like(s.bias_acc)

    @pl.loop(0, HEADS // 2)
    def _(p):
        ps = tile(p, 128)
        qp, kp, vp, dop = s.qs[:, ps], s.ks[:, ps], s.vs[:, ps], s.merged[:, ps]
        kt = jnp.transpose(kp)
        dq, dk, dv = [], [], []
        for hh in range(2):
            mine = low_head if hh == 0 else jnp.logical_not(low_head)
            dom = jnp.where(mine, dop.astype(f32), 0.0).astype(bf16)
            same_sum = jnp.zeros((1, 256), f32)
            all_sum = jnp.zeros((1, 256), f32)
            for c in range(2):
                cs = slice(c * 256, (c + 1) * 256)
                prob = s.probs[2 * p + hh, :, cs]
                d_prob = mm_nt(vp, dom[cs, :])
                d_score = prob * (d_prob - jnp.sum(prob * d_prob, axis=0, keepdims=True))
                same_sum += jnp.sum(jnp.where(s.code_t[:, cs] > 1.5, d_score, 0.0), axis=0, keepdims=True)
                all_sum += jnp.sum(d_score, axis=0, keepdims=True)
                s.ggu[:, hh * SEQ + c * 256 : hh * SEQ + (c + 1) * 256] = (d_score * HEAD_DIM**-0.5).astype(bf16)
            s.bias_acc[pl.ds(2 * p + hh, 1), :] = same_sum[:, :128] + same_sum[:, 128:]
            s.bias_acc[pl.ds(8 + 2 * p + hh, 1), :] = all_sum[:, :128] + all_sum[:, 128:]
            dv.append(mm(s.probs[2 * p + hh].astype(bf16), dop))
            dk.append(mm(s.ggu[:, hh * SEQ : (hh + 1) * SEQ], qp))
            dq.append(mm(kt[hh * 64 : (hh + 1) * 64, :], s.ggu[:, hh * SEQ : (hh + 1) * SEQ]))
        dqs = jnp.transpose(jnp.concatenate(dq, axis=0)).astype(bf16).astype(f32)
        dks = jnp.where(low_head, dk[0], dk[1]).astype(bf16).astype(f32)
        s.gparams[:, ps] = turn(dqs, -s.sin_t[...]).astype(bf16)
        s.gparams[:, tile(p + 3, 128)] = turn(dks, -s.sin_t[...]).astype(bf16)
        s.gparams[:, tile(p + 6, 128)] = jnp.where(low_head, dv[0], dv[1]).astype(bf16)

    for j in range(3):
        js = slice(j * D, (j + 1) * D)
        keep(M_QKV, 0, 3 * j, mm(s.na_t[...], s.gparams[:, js]))
    s.inner[...] = mm_nt(s.gparams[:, : 3 * D], s.w_qkv[...])
    norm_back(s.stream, s.inv_a, 0, s.grad)
    for c in range(3):
        cs = slice(c * 128, (c + 1) * 128)
        hidden_token = s.flag[...] == 1.0
        s.vec_acc[3:4, cs] = jnp.sum(jnp.where(hidden_token, s.grad[:, cs], 0.0), axis=0, keepdims=True)
        s.normed[:, cs] = jnp.where(hidden_token, 0.0, s.grad[:, cs]).astype(bf16)
    keep(M_IN, 0, 0, mm_tn(s.x5[...], s.normed[...]))

    sums = jnp.sum(s.bias_acc[...], axis=1, keepdims=True)
    sums = jnp.concatenate([sums[0:8], sums[8:16] - sums[0:8]], axis=0)
    entry = lax.broadcasted_iota(jnp.int32, (16, D), 0)
    target = jnp.where(entry < HEADS, entry, jnp.where((entry >= 8) & (entry < 8 + HEADS), entry - 8 + HEADS, -1))
    bias_row = jnp.sum(
        jnp.where(target == lax.broadcasted_iota(jnp.int32, (16, D), 1), sums, 0.0), axis=0, keepdims=True
    )
    row = lax.broadcasted_iota(jnp.int32, (8, D), 0)
    small_sum = jnp.where(row == 4, jnp.sum(s.loss_acc[...]), jnp.where(row == 5, bias_row, s.vec_acc[...]))
    for copy in outgoing + cross:
        copy.wait_send()
    send = Pool(send_pool)
    s.blocks[BLOCKS] = jnp.zeros((SIDE, SIDE), bf16)
    toks = dims[0] * dims[1] * dims[2]

    def fill(h):
        @pl.loop(0, toks)
        def _(t):
            for i in range(per):
                at = (h, t // (dims[1] * dims[2]), t // dims[2] % dims[1], t % dims[2], i)
                gathered[at] = s.blocks[holder[(h * toks + t) * per + i]]

    everywhere = (slice(None),) * 3
    parts = cut_parts(REDUCE_PARTS)
    fill(1 - head)
    arriving, outgoing = {}, []

    def start_reduce(p, k):
        axes, a, n = parts[p]
        if k == 0:
            view = everywhere + (slice(None), pl.ds(a, n))
            copies = [remote(gathered.at[(1 - head,) + view], crossed.at[view], send(), recv(), place.partner())]
        else:
            axis, left = axes[k - 1], axes[k:]
            copies = []
            for j in range(1, dims[axis]):
                region = place.region(left, {axis: place.coordinate(axis, j)})
                src = gathered.at[(head,) + region + (slice(None), pl.ds(a, n))]
                copies.append(remote(src, landing[3 * p + k - 1].at[j - 1], send(), recv(), place.peer(axis, j)))
        for copy in copies:
            copy.start()
        arriving[p] = copies
        outgoing.extend(copies)

    def end_reduce(p, k):
        axes, a, n = parts[p]
        left = sorted(axes[k:])
        region = place.region(left)
        for copy in arriving[p]:
            copy.wait_recv()

        def body(*index):
            at = tuple(index[left.index(i)] if i in left else region[i] for i in range(3)) + (slice(None), pl.ds(a, n))
            value = gathered[(head,) + at].astype(f32)
            if k == 0:
                value = value + crossed[at].astype(f32)
            else:
                for j in range(1, dims[axes[k - 1]]):
                    value = value + landing[3 * p + k - 1][(j - 1,) + index].astype(f32)
            if k < 3:
                gathered[(head,) + at] = value.astype(bf16)
            else:
                owned[:, a : a + n, :] = value

        def loops(index):
            if len(index) == len(left):
                body(*index)
            else:
                pl.loop(0, dims[left[len(index)]])(lambda i: loops(index + (i,)))

        loops(())

    begun = set()
    for group in REDUCE_GROUPS[:REDUCE_WINDOW]:
        for p in group:
            start_reduce(p, 0)
            begun.add(p)
    vec_sum = all_sum(place, small_sum, vec_buf, send, recv)
    vec_total = next(vec_sum)
    fill(head)

    def start(p, k):
        if k > 0 or p not in begun:
            start_reduce(p, k)

    def finish(p, k):
        nonlocal vec_total
        end_reduce(p, k)
        if vec_total is None and k == 1:
            vec_total = next(vec_sum)

    pipeline(REDUCE_GROUPS, 4, REDUCE_WINDOW, start, finish)
    while vec_total is None:
        vec_total = next(vec_sum)
    part_square = jnp.zeros((8, 128), f32)
    for i in range(per):
        piece = owned[i]
        part_square = part_square + jnp.sum((piece * piece).reshape(16, 8, 128), axis=0)
    sq_sum = all_sum(place, part_square, sq_buf, send, recv)
    total = next(sq_sum)
    for i in range(per):
        grad = owned[i]
        gram_left[i] = lax.dot_general(grad, grad, (((1,), (1,)), ((), ())), precision=highest, preferred_element_type=f32)
        turned = jnp.transpose(grad)
        gram_right[i] = jnp.dot(turned, grad, precision=highest, preferred_element_type=f32)
    while total is None:
        total = next(sq_sum)

    grads4 = vec_total[0:4]
    bias_total = vec_total[5:6, 0 : 2 * HEADS]
    square = jnp.sum(total) + jnp.sum(grads4 * grads4) + jnp.sum(bias_total * bias_total)
    grad_norm = jnp.sqrt(jnp.broadcast_to(square, (8, 128)))
    factor = jnp.minimum(1.0, clip_limit / grad_norm)
    loss_out[0, 0] = vec_total[4, 0]
    norm_out[0, 0] = jnp.max(grad_norm)
    factor_out[0, 0] = jnp.max(factor)
    small_out[...] = vec_total
    for copy in outgoing:
        copy.wait_send()


def update_kernel(
    factor_ref, small, vectors, vector_first, vector_second, var_bias, bias_first, bias_second, *rest,
):
    sources, rest = rest[:8], rest[8:]
    clipped_out, left_out, right_out, master_out = rest[:4]
    vector_grads, vector_second_new, vector_new, bias_grads, bias_second_new, bias_new = rest[4:10]
    held, made, in_sem, out_sem = rest[10:]
    fetches = [pltpu.make_async_copy(ref, held.at[k], in_sem.at[k]) for k, ref in enumerate(sources)]
    for copy in fetches:
        copy.start()
    owned, left_root, right_root, gram_left, left, gram_right, right, master = (held.at[k] for k in range(8))
    sends = [
        pltpu.make_async_copy(made.at[k], ref, out_sem.at[k])
        for k, ref in enumerate((clipped_out, left_out, right_out, master_out))
    ]
    factor = factor_ref[0, 0]
    per = owned.shape[0]
    fetches[0].wait()
    fetches[1].wait()
    grads = [owned[i] * factor for i in range(per)]
    for i in range(per):
        made[0, i] = grads[i]
    sends[0].start()
    shaped = [jnp.dot(left_root[i], grads[i], precision=highest, preferred_element_type=f32) for i in range(per)]
    fetches[2].wait()
    shaped = [jnp.dot(shaped[i], right_root[i], precision=highest, preferred_element_type=f32) for i in range(per)]
    for copy in fetches[3:]:
        copy.wait()
    for k, (stat, gram) in enumerate(((left, gram_left), (right, gram_right))):
        for i in range(per):
            scaled = jnp.where(factor > 0.0, gram[i] * factor * factor, 0.0)
            made[1 + k, i] = stat_beta * stat[i] + (1.0 - stat_beta) * scaled
        sends[1 + k].start()
    for i in range(per):
        unit = shaped[i] * lax.rsqrt(jnp.sum(shaped[i] * shaped[i]) / (SIDE * SIDE) + root_eps)
        made[3, i] = master[i] - mat_rate * (unit + decay_rate * master[i])
    sends[3].start()

    def adamw(gradient, first, second, old, grad_out, second_out, new_out):
        gradient = gradient * factor
        grad_out[...] = gradient
        first_next = beta_one * first[...] + (1.0 - beta_one) * gradient
        second_next = beta_two * second[...] + (1.0 - beta_two) * gradient * gradient
        ratio = first_next / (1.0 - beta_one**STEP) / (jnp.sqrt(second_next / (1.0 - beta_two**STEP)) + adam_eps)
        second_out[...] = second_next
        new_out[...] = old[...] - vec_rate * (ratio + decay_rate * old[...])

    adamw(small[0:4], vector_first, vector_second, vectors, vector_grads, vector_second_new, vector_new)
    adamw(small[5:6, 0 : 2 * HEADS], bias_first, bias_second, var_bias, bias_grads, bias_second_new, bias_new)
    for copy in sends:
        copy.wait()


def update_call(factor, small, owned, gram_left, gram_right, master, left, right, left_root, right_root, *rest):
    vmem, hbm = pl.BlockSpec(memory_space=pltpu.VMEM), pl.BlockSpec(memory_space=pl.ANY)
    sources = (owned, left_root, right_root, gram_left, left, gram_right, right, master)
    vectors, var_bias = rest[0], rest[3]
    outs = [master] * 4 + [vectors] * 3 + [var_bias] * 3
    return pl.pallas_call(
        update_kernel,
        out_shape=tuple(jax.ShapeDtypeStruct(a.shape, f32) for a in outs),
        in_specs=[pl.BlockSpec(memory_space=pltpu.SMEM)] + [vmem] * (1 + len(rest)) + [hbm] * 8,
        out_specs=(hbm,) * 4 + (vmem,) * 6,
        scratch_shapes=[
            pltpu.VMEM((8,) + master.shape, f32),
            pltpu.VMEM((4,) + master.shape, f32),
            pltpu.SemaphoreType.DMA((8,)),
            pltpu.SemaphoreType.DMA((4,)),
        ],
        compiler_params=pltpu.CompilerParams(vmem_limit_bytes=60 * 2**20),
        name="update",
    )(factor, small, *rest, *sources)


def step_call(dims, places, holder, lengths, bias, master, patches, sizes, times, predict, variates, vectors):
    freq = (10000.0 ** (-np.arange(HEAD_DIM // 2) / (HEAD_DIM // 2))).astype(np.float32)
    freq = jnp.asarray(np.tile(freq[None], (8, 4)))
    per = master.shape[0]
    half = patches.shape[2]
    received, sent = semaphores(dims)
    smem = pl.BlockSpec(memory_space=pltpu.SMEM)
    vmem = pl.BlockSpec(memory_space=pltpu.VMEM)
    sems = pltpu.SemaphoreType.DMA
    landing = []
    for axes, _, n in cut_parts(REDUCE_PARTS):
        for k in range(3):
            wide = [dims[i] for i in sorted(axes[k + 1 :])]
            landing.append(pltpu.VMEM((max(dims[axes[k]] - 1, 1), *wide, per, n, SIDE), bf16))
    return pl.pallas_call(
        functools.partial(step_kernel, dims),
        out_shape=tuple(
            jax.ShapeDtypeStruct(shape, f32)
            for shape in [(1, 1)] * 4 + [(8, D)] + [(per, SIDE, SIDE)] * 3
        ),
        in_specs=[smem] * 4 + [vmem] * 9,
        out_specs=(smem,) * 4 + (vmem,) * 4,
        scratch_shapes=[pltpu.VMEM(shape, dtype) for shape, dtype in SCRATCH.values()]
        + [
            pltpu.VMEM((per, SIDE, SIDE), bf16),
            pltpu.VMEM((2,) + dims + (per, SIDE, SIDE), bf16),
            pltpu.VMEM(dims + (per, SIDE, SIDE), bf16),
            pltpu.VMEM((half, PMAX), bf16),
            pltpu.VMEM((3, 2, half), jnp.int32),
            pltpu.VMEM((3, 2, half), jnp.int32),
            sum_shape(dims, (8, 128)),
            sum_shape(dims, (8, D)),
            sum_shape(dims, (8, 128)),
            sems,
            sems((sent,)),
            sems((received,)),
            *landing,
        ],
        compiler_params=pltpu.CompilerParams(
            collective_id=0, has_side_effects=True, vmem_limit_bytes=63 * 2**20
        ),
        name="step",
    )(places, holder, lengths, bias, master, patches, sizes, times, predict, variates, vectors, freq,
      jnp.asarray(group_order(), bf16))


def shards(
    dims,
    patches, patch_sizes, sample_lengths, variate_ids, time_ids, predict_mask, block_owner_slot,
    master_blocks, left_stats, right_stats, left_roots, right_roots,
    vectors, vector_first, vector_second, var_bias, bias_first, bias_second,
):
    slot_count = master_blocks.shape[0] * lax.axis_size("head") * lax.axis_size("tok")
    match = block_owner_slot[None, :] == jnp.arange(slot_count)[:, None]
    holder = BLOCKS + jnp.sum(jnp.where(match, jnp.arange(BLOCKS)[None, :] - BLOCKS, 0), axis=1)
    device, inside = block_owner_slot // master_blocks.shape[0], block_owner_slot % master_blocks.shape[0]
    places = [device // (dims[0] * dims[1] * dims[2])]
    places += [device // (dims[1] * dims[2]) % dims[0], device // dims[2] % dims[1], device % dims[2], inside]
    loss_sum, count, grad_norm, factor, small, owned, gram_left, gram_right = step_call(
        dims, jnp.stack(places), holder, sample_lengths, var_bias[0], master_blocks, patches, patch_sizes, time_ids,
        predict_mask, variate_ids, vectors,
    )
    outs = update_call(
        factor, small, owned, gram_left, gram_right, master_blocks, left_stats, right_stats, left_roots, right_roots,
        vectors, vector_first, vector_second, var_bias, bias_first, bias_second,
    )
    return (loss_sum.reshape(()), count.reshape(()), grad_norm.reshape(())) + tuple(outs)


def solution(mesh):
    rep = P()
    dims = tok_dims(mesh.shape["tok"])
    slot = P(("head", "tok"), None, None)
    return jax.shard_map(
        functools.partial(shards, dims),
        mesh=mesh,
        in_specs=(
            P(None, "tok", "head", None), P(None, "tok", "head"), P(None, "tok", None), P(None, "tok", None),
            P(None, "tok", "head"), P(None, "tok", "head"), rep, slot, slot, slot, slot, slot,
            rep, rep, rep, rep, rep, rep,
        ),
        out_specs=(rep, rep, rep, slot, slot, slot, slot, rep, rep, rep, rep, rep, rep),
        check_vma=False,
    )
```

```python
import functools
import itertools
import math

import jax
import jax.numpy as jnp
import numpy as np
from jax import lax
from jax.experimental import pallas as pl
from jax.experimental.pallas import tpu as pltpu
from jax.sharding import PartitionSpec as P

D = 384
FF = 1024
HEADS = 6
HEAD_DIM = 64
PSIZES = 5
PMAX = 128
COMPS = 4
SEQ = 512
SIDE = 128
STEP = 10
HEADCOLS = 3 * COMPS * PMAX
BLOCKS = 159

norm_eps = 1e-06
scale_floor = 0.05
half_log_tau = 0.9189385332046727
clip_limit = 0.02
mat_rate = 0.01
vec_rate = 0.3
decay_rate = 0.01
beta_one = 0.9
beta_two = 0.95
stat_beta = 0.99
root_eps = 1e-06
adam_eps = 1e-08
highest = lax.Precision.HIGHEST
f32 = jnp.float32
bf16 = jnp.bfloat16

GRIDS = ((5, 3), (3, 12), (3, 9), (3, 3), (3, 16), (8, 3))
FIRSTS = (0, 15, 51, 78, 87, 135)
M_IN, M_HEAD, M_QKV, M_OUT, M_GU, M_DOWN = range(6)


def mm(a, b):
    return jnp.dot(a, b, preferred_element_type=f32)


def mm_nt(a, b):
    return lax.dot_general(a, b, (((1,), (1,)), ((), ())), preferred_element_type=f32)


def mm_tn(a, b):
    return lax.dot_general(a, b, (((0,), (0,)), ((), ())), preferred_element_type=f32)


GROUP = 384


def group_order():
    order = np.zeros((GROUP, GROUP), np.float32)
    for col in range(GROUP):
        order[col, (col % 12) * 32 + col // 12] = 1.0
    return order


def swap_quarters(parts):
    lane = lax.broadcasted_iota(jnp.int32, (1, 128), 1)
    low, even = lane < 64, lane % 64 < 32
    a, b, c, d = parts
    a, c = jnp.where(low, a, pltpu.roll(c, 64, 1)), jnp.where(low, pltpu.roll(a, 64, 1), c)
    b, d = jnp.where(low, b, pltpu.roll(d, 64, 1)), jnp.where(low, pltpu.roll(b, 64, 1), d)
    a, b = jnp.where(even, a, pltpu.roll(b, 32, 1)), jnp.where(even, pltpu.roll(a, 96, 1), b)
    c, d = jnp.where(even, c, pltpu.roll(d, 32, 1)), jnp.where(even, pltpu.roll(c, 96, 1), d)
    return a, b, c, d


SCRATCH = dict(
    w_in=((640, D), bf16), w_head=((D, HEADCOLS), bf16), w_qkv=((D, 3 * D), bf16), w_out=((D, D), bf16),
    w_gu=((D, 2 * FF), bf16), w_down=((FF, D), bf16), w_headp=((D, HEADCOLS), bf16),
    blocks=((BLOCKS + 1, SIDE, SIDE), bf16),
    x5=((SEQ, 640), bf16), weight=((SEQ, PMAX), f32), flag=((SEQ, 128), f32),
    cos_t=((SEQ, 128), f32), sin_t=((SEQ, 128), f32),
    code_t=((SEQ, SEQ), f32), probs=((HEADS, SEQ, SEQ), f32),
    stream=((SEQ, D), f32), middle=((SEQ, D), f32), last=((SEQ, D), f32), grad=((SEQ, D), f32), inner=((SEQ, D), f32),
    inv_a=((SEQ, 128), f32), inv_b=((SEQ, 128), f32), inv_f=((SEQ, 128), f32),
    normed=((SEQ, D), bf16), na_t=((D, SEQ), bf16), nb_t=((D, SEQ), bf16), nf_t=((D, SEQ), bf16),
    qs=((SEQ, D), bf16), ks=((SEQ, D), bf16), vs=((SEQ, D), bf16), merged=((SEQ, D), bf16), merged_t=((D, SEQ), bf16),
    silu=((SEQ, FF), f32), slope=((SEQ, FF), f32), hidden=((SEQ, FF), bf16),
    params=((SEQ, HEADCOLS), f32), gparams=((SEQ, HEADCOLS), bf16), ggu=((SEQ, 2 * FF), bf16),
    loss_acc=((32, 128), f32), bias_acc=((16, 128), f32), vec_acc=((8, D), f32),
    meta=((8, SEQ), jnp.int32), row_patches=((SEQ, PMAX), bf16),
)


def tile(i, size):
    return pl.ds(pl.multiple_of(i * size, size), size)


MESH = pl.DeviceIdType.MESH


def tok_dims(count):
    return {16: (4, 2, 2), 128: (4, 4, 8)}.get(count, (count, 1, 1))


class Place:
    def __init__(self, dims):
        self.dims = dims
        self.head = lax.axis_index("head")
        tok = lax.axis_index("tok")
        self.tok = tok
        self.strides = (dims[1] * dims[2], dims[2], 1)
        self.at = [lax.rem(lax.div(tok, s), n) for s, n in zip(self.strides, dims)]

    def coordinate(self, axis, step):
        return lax.rem(self.at[axis] + step, self.dims[axis])

    def peer(self, axis, step):
        return (self.head, self.tok + (self.coordinate(axis, step) - self.at[axis]) * self.strides[axis])

    def partner(self):
        return (1 - self.head, self.tok)

    def groups(self):
        result, size = [[None]], 2
        for axis in (1, 2, 0):
            if self.dims[axis] == 1:
                continue
            if size * self.dims[axis] > 8:
                result.append([])
                size = 1
            result[-1].append(axis)
            size *= self.dims[axis]
        return result

    def members(self, group):
        sizes = [2 if axis is None else self.dims[axis] for axis in group]
        mine = 0
        for axis, n in zip(group, sizes):
            mine = mine * n + (self.head if axis is None else self.at[axis])
        others = []
        for steps in itertools.product(*[range(n) for n in sizes]):
            head, tok = self.head, self.tok
            for axis, step in zip(group, steps):
                if axis is None:
                    head = lax.rem(head + step, 2)
                else:
                    tok = tok + (self.coordinate(axis, step) - self.at[axis]) * self.strides[axis]
            if any(steps):
                others.append((head, tok))
        return mine, math.prod(sizes), others

    def greet(self, meanwhile):
        barrier = pltpu.get_barrier_semaphore()
        groups = self.groups()
        others = [other for group in groups for other in self.members(group)[2]]
        joint = [group for group in groups if len(group) > 1]
        singles = {group[0] for group in groups if len(group) == 1} | {a for group in joint for a in group}
        others += [self.peer(a, j) for a in range(3) if a not in singles for j in range(1, self.dims[a])]
        for other in others:
            pl.semaphore_signal(barrier, inc=1, device_id=other, device_id_type=MESH)
        meanwhile()
        pl.semaphore_wait(barrier, len(others))

    def region(self, whole, fixed=None):
        fixed = fixed or {}
        return tuple(slice(None) if a in whole else fixed.get(a, self.at[a]) for a in range(3))


def remote(src, dst, send, recv, device):
    return pltpu.make_async_remote_copy(
        src_ref=src, dst_ref=dst, send_sem=send, recv_sem=recv, device_id=device, device_id_type=MESH
    )


def split_rows(rows, shares):
    units = rows // 16
    edges = [round(units * sum(shares[:i]) / sum(shares)) * 16 for i in range(len(shares) + 1)]
    return [(a, b - a) for a, b in zip(edges, edges[1:])]


class Pool:
    def __init__(self, ref):
        self.ref, self.used = ref, 0

    def __call__(self):
        self.used += 1
        return self.ref.at[self.used - 1]


def all_sum(place, values, buf, send, recv):
    total = values
    for k, group in enumerate(place.groups()):
        mine, size, others = place.members(group)
        buf[k, mine] = total
        copies = [remote(buf.at[k, mine], buf.at[k, mine], send(), recv(), other) for other in others]
        for copy in copies:
            copy.start()
        yield None
        for copy in copies:
            copy.wait()
        total = buf[k, 0]
        for i in range(1, size):
            total = total + buf[k, i]
    yield total


def sum_sizes(dims):
    place = Place.__new__(Place)
    place.dims = dims
    return [math.prod(2 if a is None else dims[a] for a in group) for group in place.groups()]


def sum_shape(dims, shape):
    sizes = sum_sizes(dims)
    return pltpu.VMEM((len(sizes), max(sizes)) + shape, f32)


GATHER_PARTS = (
    ((1, 2, 0), 1), ((0, 1, 2), 1), ((0, 2, 1), 1), ((0, 1, 2), 1), ((0, 1, 2), 1), ((0, 2, 1), 1), ((1, 0, 2), 1), ((2, 0, 1), 1),
)
PREPARE_AFTER = 2
GATHER_PLAN = (
    0, 10, 20, 60, 100, 1, 30, 70, 110, 11, 50, 120, 21, 130, 31, 40, 111, 12, 160, 61, 150, 51, 170, 71,
    121, 22, 140, 41, 131, 32, 141, 42, 151, 52, 101, 2, 122, 171, 72, 112, 161, 62, 172, 132, 142, 102, 152, 162,
)
REDUCE_PARTS = (
    ((2, 0, 1), 1), ((0, 1, 2), 1), ((2, 1, 0), 1), ((1, 2, 0), 1), ((2, 1, 0), 1), ((1, 0, 2), 1), ((1, 2, 0), 1), ((2, 1, 0), 1),
)
REDUCE_PLAN = (
    100, 1, 110, 11, 120, 21, 130, 31, 140, 41, 150, 51, 101, 2, 111, 12, 131, 32, 160, 61, 121, 22, 170, 71,
    151, 52, 112, 13, 122, 23, 141, 42, 161, 62, 132, 33, 152, 53, 171, 72, 102, 3, 142, 43, 162, 63, 133, 172,
    73, 143, 163, 153, 113, 123, 103, 173,
)


def cut_parts(table):
    return [(order, a, n) for (order, _), (a, n) in zip(table, split_rows(SIDE, [s for _, s in table]))]


def semaphores(dims):
    steps = sum(n - 1 for n in dims)
    sums = sum(n - 1 for n in sum_sizes(dims))
    gather = sum(steps + 1 + sum(dims[a] - 1 for a in order[1:]) for order, _ in GATHER_PARTS) + 2 + sums
    reduce = len(REDUCE_PARTS) * (steps + 1) + 2 * sums
    return gather + reduce, max(gather, reduce)


def step_kernel(
    dims, slots, places, holder, lengths, bias, master, patches, sizes, times_in, predict_in, variates_in, vectors, freq, order,
    loss_out, count_out, norm_out, factor_out, small_out, owned, gram_left, gram_right, *rest,
):
    names = list(SCRATCH)
    s = type("S", (), dict(zip(names, rest)))
    rest = rest[len(names) :]
    mine, gathered, crossed, land_patch, land_ints, own_ints = rest[:6]
    cnt_buf, vec_buf, sq_buf, own_sem, send_pool, recv_pool = rest[6:12]
    send, recv = Pool(send_pool), Pool(recv_pool)
    landing = rest[12:]
    place = Place(dims)
    per = mine.shape[0]
    head = place.head
    lane = lax.broadcasted_iota(jnp.int32, (1, 128), 1)
    first_half = lane % HEAD_DIM < HEAD_DIM // 2
    low_head = lane < HEAD_DIM
    weights = (s.w_in, s.w_head, s.w_qkv, s.w_out, s.w_gu, s.w_down)

    def keep(m, r0, c0, value):
        value = value.astype(bf16)
        cols = GRIDS[m][1]
        for r in range(value.shape[0] // SIDE):
            for c in range(value.shape[1] // SIDE):
                piece = value[r * SIDE : (r + 1) * SIDE, c * SIDE : (c + 1) * SIDE]
                s.blocks[FIRSTS[m] + (r0 + r) * cols + c0 + c] = piece

    half = SEQ // 2
    s.meta[4:8, :] = jnp.zeros((4, SEQ), jnp.int32)

    def local_work():
        mine[...] = master[...].astype(bf16)
        for k, ref in enumerate((sizes, times_in, predict_in)):
            own_ints[k, :, :] = ref[:, 0, :]
        for h in range(2):

            @pl.when(head == h)
            def _():
                here = slice(h * half, (h + 1) * half)
                s.row_patches[here, :] = patches[h, 0]
                for k, ref in enumerate((sizes, times_in, predict_in)):
                    s.meta[k : k + 1, here] = ref[h]
                s.meta[3:4, :] = variates_in[h]

    place.greet(local_work)
    swaps = [
        remote(patches.at[1 - head, 0], land_patch, send(), recv(), place.partner()),
        remote(own_ints, land_ints, send(), recv(), place.partner()),
    ]
    for copy in swaps:
        copy.start()
    parts = cut_parts(GATHER_PARTS)

    def block(head_index, whole, fixed, a, n):
        return gathered.at[(head_index,) + place.region(whole, fixed) + (slice(None), pl.ds(a, n))]

    arriving, outgoing, cross = {}, list(swaps), []
    own = pltpu.make_async_copy(mine, gathered.at[(head,) + place.region(())], own_sem)
    own.start()

    def start_gather(p, k):
        axes, a, n = parts[p]
        axis, whole = axes[k], axes[:k]
        arriving[p] = []
        for j in range(1, dims[axis]):
            src = mine.at[:, pl.ds(a, n)] if k == 0 else block(head, whole, None, a, n)
            copy = remote(src, block(head, whole, None, a, n), send(), recv(), place.peer(axis, j))
            copy.start()
            arriving[p].append(copy)
        outgoing.extend(arriving[p])

    def end_gather(p, k):
        axes, a, n = parts[p]
        for copy in arriving[p]:
            copy.wait_recv()
        axis, whole = axes[k], axes[:k]
        if k == 0:
            views = [block(head, axes[:1], None, a, n)]
        else:
            views = [
                block(head, whole, {axis: place.coordinate(axis, dims[axis] - j)}, a, n) for j in range(1, dims[axis])
            ]
        for view in views:
            copy = remote(view, view, send(), recv(), place.partner())
            copy.start()
            cross.append(copy)

    first = next(i for i, step in enumerate(GATHER_PLAN) if step >= 100)
    for step in GATHER_PLAN[:first]:
        start_gather(step // 10, step % 10)
    wide_size = jnp.zeros_like(own_ints[0])
    for c in range(PSIZES):
        wide_size = wide_size + jnp.where(own_ints[0] == c, PMAX * 2**c // 2 ** (PSIZES - 1), 0)
    partial = (wide_size * own_ints[2]).astype(f32)
    partial = jnp.sum(partial[:, :128] + partial[:, 128:], axis=0, keepdims=True)
    counting = all_sum(place, jnp.concatenate([partial, jnp.zeros((7, 128), f32)], axis=0), cnt_buf, send, recv)
    counted = next(counting)
    own.wait()
    for copy in swaps:
        copy.wait_recv()
    for h in range(2):

        @pl.when(head == h)
        def _():
            there = slice((1 - h) * half, (2 - h) * half)
            s.row_patches[there, :] = land_patch[...]
            for k in range(3):
                s.meta[k : k + 1, there] = land_ints[k, h : h + 1, :]

    def prepare_tokens():
        metaf = s.meta[...].astype(f32)
        columns = jnp.transpose(metaf)
        codes, times, flag = columns[:, 0:1], columns[:, 1:2], columns[:, 2:3]
        position = lax.broadcasted_iota(jnp.int32, (1, SEQ), 1)
        ids = jnp.zeros((1, SEQ), f32)
        end = jnp.int32(0)
        for j in range(lengths.shape[2]):
            end = end + lengths[head, 0, j]
            ids = ids + jnp.where(position >= end, 1.0, 0.0)
        variates = metaf[3:4]
        id_columns = jnp.transpose(jnp.concatenate([ids] * 8, axis=0))[:, 0:1]
        var_columns = columns[:, 3:4]
        for c in range(4):
            cs = slice(c * 128, (c + 1) * 128)
            same_sample = id_columns == ids[:, cs]
            same_var = var_columns == variates[:, cs]
            s.code_t[:, cs] = jnp.where(same_sample, jnp.where(same_var, 2.0, 1.0), 0.0)
        s.flag[...] = jnp.broadcast_to(flag, (SEQ, 128))
        angle = times * freq[0:1, :]
        s.cos_t[...] = jnp.cos(angle)
        s.sin_t[...] = jnp.where(first_half, -1.0, 1.0) * jnp.sin(angle)

        wide = s.row_patches[...].astype(f32)
        weight = jnp.zeros((SEQ, PMAX), f32)
        for c in range(PSIZES):
            keep = (codes == float(c)) & (lane < PMAX * 2**c // 2 ** (PSIZES - 1))
            s.x5[:, c * 128 : (c + 1) * 128] = jnp.where(keep, wide, 0.0).astype(bf16)
            weight = jnp.where(keep, 1.0, weight)
        s.weight[...] = jnp.where(flag == 1.0, weight, 0.0)
    ended = 0
    for step in GATHER_PLAN[first:]:
        if step < 100:
            start_gather(step // 10, step % 10)
            continue
        end_gather(step // 10 % 10, step % 10)
        ended += 1
        if counted is None and ended in (4, 8):
            counted = next(counting)
        if ended == PREPARE_AFTER:
            prepare_tokens()
    while counted is None:
        counted = next(counting)
    value_count = jnp.sum(counted)
    count_out[0, 0] = value_count
    for copy in cross:
        copy.wait_recv()

    def load(m):
        n_rows, cols = GRIDS[m]

        @pl.loop(0, n_rows)
        def _(r):
            for c in range(cols):
                slot = slots[FIRSTS[m] + r * cols + c]
                where = tuple(places[k, slot] for k in range(5))
                weights[m][tile(r, SIDE), c * SIDE : (c + 1) * SIDE] = gathered[where]

    for m in range(6):
        load(m)

    def turn(v, sine):
        swapped = jnp.where(first_half, pltpu.roll(v, 96, 1), pltpu.roll(v, 32, 1))
        return v * s.cos_t[...] + swapped * sine

    embedded = mm(s.x5[...], s.w_in[...])
    for c in range(3):
        cs = slice(c * 128, (c + 1) * 128)
        s.stream[:, cs] = jnp.where(s.flag[...] == 1.0, vectors[3:4, cs], embedded[:, cs])

    def norm(src, inv_ref, gain, dst_t):
        @pl.loop(0, SEQ // 128)
        def _(i):
            rs = tile(i, 128)
            v = src[rs, :]
            inverse = lax.rsqrt(jnp.sum(v * v, axis=-1, keepdims=True) / D + norm_eps)
            inv_ref[rs, :] = jnp.broadcast_to(inverse, (128, 128))
            s.normed[rs, :] = (v * inverse * gain).astype(bf16)

        dst_t[...] = jnp.transpose(s.normed[...])

    def norm_back(src, inv_ref, row, extra):
        gain = vectors[row : row + 1, :]

        @pl.loop(0, SEQ // 128)
        def _(i):
            rs = tile(i, 128)
            up = s.inner[rs, :]
            inverse = inv_ref[rs, 0:1]
            scaled = src[rs, :] * inverse
            inner = up * gain
            mean = jnp.sum(inner * scaled, axis=-1, keepdims=True) / D
            result = inverse * (inner - scaled * mean)
            s.grad[rs, :] = result if extra is None else result + extra[rs, :]
            s.vec_acc[row : row + 1, :] += jnp.sum(up * scaled, axis=0, keepdims=True)

    s.vec_acc[...] = jnp.zeros_like(s.vec_acc)
    norm(s.stream, s.inv_a, vectors[0:1, :], s.na_t)
    mixed = mm(s.normed[...], s.w_qkv[...])
    for part, dst in ((0, s.qs), (1, s.ks), (2, s.vs)):
        for c in range(3):
            piece = mixed[:, part * D + c * 128 : part * D + (c + 1) * 128]
            if part < 2:
                piece = turn(piece, s.sin_t[...])
            dst[:, c * 128 : (c + 1) * 128] = piece.astype(bf16)

    @pl.loop(0, HEADS // 2)
    def _(p):
        ps = tile(p, 128)
        qp, kp = s.qs[:, ps], s.ks[:, ps]
        vt = jnp.transpose(s.vs[:, ps])
        outs = []
        for hh in range(2):
            mine = low_head if hh == 0 else jnp.logical_not(low_head)
            qm = jnp.where(mine, qp.astype(f32) * HEAD_DIM**-0.5, 0.0).astype(bf16)
            b0 = bias[2 * p + hh]
            b1 = bias[HEADS + 2 * p + hh]
            parts = []
            for c in range(1):
                cs = slice(c * 512, (c + 1) * 512)
                code = s.code_t[:, cs]
                score = mm_nt(kp, qm[cs, :])
                score = jnp.where(code > 0.5, score + jnp.where(code > 1.5, b0, b1), -1e30)
                raised = jnp.exp(score - jnp.max(score, axis=0, keepdims=True))
                prob = raised * (1.0 / jnp.sum(raised, axis=0, keepdims=True))
                s.probs[2 * p + hh, :, cs] = prob
                parts.append(mm(vt[hh * 64 : (hh + 1) * 64, :], prob.astype(bf16)))
            outs.append(jnp.concatenate(parts, axis=1))
        out_t = jnp.concatenate(outs, axis=0).astype(bf16)
        s.merged_t[ps, :] = out_t
        s.merged[:, ps] = jnp.transpose(out_t)

    s.middle[...] = s.stream[...] + mm(s.merged[...], s.w_out[...])
    norm(s.middle, s.inv_b, vectors[1:2, :], s.nb_t)

    @pl.loop(0, FF // 1024)
    def _(j):
        js = tile(j, 1024)
        opening = mm(s.normed[...], s.w_gu[:, js])
        up = mm(s.normed[...], s.w_gu[:, tile(j + FF // 1024, 1024)])
        sigma = 1.0 / (1.0 + jnp.exp(-opening))
        silu = opening * sigma
        s.silu[:, js] = silu
        s.slope[:, js] = up * sigma * (1.0 + opening * (1.0 - sigma))
        s.hidden[:, js] = (silu * up).astype(bf16)

    s.last[...] = s.middle[...] + mm(s.hidden[...], s.w_down[...])
    norm(s.last, s.inv_f, vectors[2:3, :], s.nf_t)


    wide = [mm(s.w_head[:, g * GROUP : (g + 1) * GROUP], order[...]) for g in range(4)]
    for kind in range(3):
        pieces = swap_quarters([w[:, kind * 128 : (kind + 1) * 128] for w in wide])
        for k, piece in enumerate(pieces):
            at = (4 * kind + k) * 128
            s.w_headp[:, at : at + 128] = piece.astype(bf16)

    @pl.loop(0, HEADCOLS // 512)
    def _(j):
        js = tile(j, 512)
        s.params[:, js] = mm(s.normed[...], s.w_headp[:, js])

    inv_n = 1.0 / value_count
    s.loss_acc[...] = jnp.zeros_like(s.loss_acc)

    @pl.loop(0, SEQ // 32)
    def _(i):
        rs = tile(i, 32)
        y = s.row_patches[rs, :].astype(f32)
        weight = s.weight[rs, :]
        logits, means, raws = [
            [s.params[rs, (4 * kind + k) * 128 : (4 * kind + k + 1) * 128] for k in range(COMPS)] for kind in range(3)
        ]
        top = jnp.maximum(jnp.maximum(logits[0], logits[1]), jnp.maximum(logits[2], logits[3]))
        shifted = [v - top for v in logits]
        raised = [jnp.exp(v) for v in shifted]
        total = raised[0] + raised[1] + raised[2] + raised[3]
        log_total = jnp.log(total)
        inv_total = 1.0 / total
        terms, zs, inv_widths = [], [], []
        for k in range(COMPS):
            width = jnp.maximum(raws[k], 0.0) + jnp.log1p(jnp.exp(-jnp.abs(raws[k]))) + scale_floor
            inv_width = 1.0 / width
            z = (y - means[k]) * inv_width
            terms.append((shifted[k] - log_total) - 0.5 * z * z - jnp.log(width) - half_log_tau)
            zs.append(z)
            inv_widths.append(inv_width)
        best = jnp.maximum(jnp.maximum(terms[0], terms[1]), jnp.maximum(terms[2], terms[3]))
        lifted = [jnp.exp(t - best) for t in terms]
        lift_total = lifted[0] + lifted[1] + lifted[2] + lifted[3]
        inv_lift = 1.0 / lift_total
        s.loss_acc[...] += jnp.where(weight > 0.0, -(best + jnp.log(lift_total)), 0.0)
        scale = -(weight * inv_n)
        for k in range(COMPS):
            share = lifted[k] * inv_lift
            d_term = scale * share
            ratio = zs[k] * inv_widths[k]
            d_logit = scale * (share - raised[k] * inv_total)
            d_width = d_term * (zs[k] * ratio - inv_widths[k])
            sigma = 1.0 / (1.0 + jnp.exp(-raws[k]))
            for kind, value in ((0, d_logit), (1, d_term * ratio), (2, d_width * sigma)):
                at = (4 * kind + k) * 128
                s.gparams[rs, at : at + 128] = value.astype(bf16)

    for kind in range(3):
        ks = slice(kind * 512, (kind + 1) * 512)
        wide = mm(s.nf_t[...], s.gparams[:, ks])
        pieces = swap_quarters([wide[:, k * 128 : (k + 1) * 128] for k in range(4)])
        for g in range(4):
            s.w_head[:, (3 * g + kind) * 128 : (3 * g + kind + 1) * 128] = pieces[g].astype(bf16)
    for g in range(4):
        gs = slice(g * GROUP, (g + 1) * GROUP)
        keep(M_HEAD, 0, 3 * g, mm_nt(s.w_head[:, gs], order[...]))
    s.inner[...] = mm_nt(s.gparams[...], s.w_headp[...])
    norm_back(s.last, s.inv_f, 2, None)

    s.normed[...] = s.grad[...].astype(bf16)

    @pl.loop(0, FF // 1024)
    def _(j):
        js = tile(j, 1024)
        keep(M_DOWN, 8 * j, 0, mm_tn(s.hidden[:, js], s.normed[...]))
        up_grad = mm_nt(s.normed[...], s.w_down[js, :])
        s.ggu[:, js] = (up_grad * s.slope[:, js]).astype(bf16)
        s.ggu[:, tile(j + FF // 1024, 1024)] = (up_grad * s.silu[:, js]).astype(bf16)

    @pl.loop(0, 2 * FF // 512)
    def _(j):
        keep(M_GU, 0, 4 * j, mm(s.nb_t[...], s.ggu[:, tile(j, 512)]))

    s.inner[...] = mm_nt(s.ggu[...], s.w_gu[...])
    norm_back(s.middle, s.inv_b, 1, s.grad)

    s.normed[...] = s.grad[...].astype(bf16)
    keep(M_OUT, 0, 0, mm(s.merged_t[...], s.normed[...]))
    s.merged[...] = mm_nt(s.normed[...], s.w_out[...]).astype(bf16)
    s.bias_acc[...] = jnp.zeros_like(s.bias_acc)

    @pl.loop(0, HEADS // 2)
    def _(p):
        ps = tile(p, 128)
        qp, kp, vp, dop = s.qs[:, ps], s.ks[:, ps], s.vs[:, ps], s.merged[:, ps]
        kt = jnp.transpose(kp)
        dq, dk, dv = [], [], []
        for hh in range(2):
            mine = low_head if hh == 0 else jnp.logical_not(low_head)
            dom = jnp.where(mine, dop.astype(f32), 0.0).astype(bf16)
            same_sum = jnp.zeros((1, 256), f32)
            all_sum = jnp.zeros((1, 256), f32)
            for c in range(2):
                cs = slice(c * 256, (c + 1) * 256)
                prob = s.probs[2 * p + hh, :, cs]
                d_prob = mm_nt(vp, dom[cs, :])
                d_score = prob * (d_prob - jnp.sum(prob * d_prob, axis=0, keepdims=True))
                same_sum += jnp.sum(jnp.where(s.code_t[:, cs] > 1.5, d_score, 0.0), axis=0, keepdims=True)
                all_sum += jnp.sum(d_score, axis=0, keepdims=True)
                s.ggu[:, hh * SEQ + c * 256 : hh * SEQ + (c + 1) * 256] = (d_score * HEAD_DIM**-0.5).astype(bf16)
            s.bias_acc[pl.ds(2 * p + hh, 1), :] = same_sum[:, :128] + same_sum[:, 128:]
            s.bias_acc[pl.ds(8 + 2 * p + hh, 1), :] = all_sum[:, :128] + all_sum[:, 128:]
            dv.append(mm(s.probs[2 * p + hh].astype(bf16), dop))
            dk.append(mm(s.ggu[:, hh * SEQ : (hh + 1) * SEQ], qp))
            dq.append(mm(kt[hh * 64 : (hh + 1) * 64, :], s.ggu[:, hh * SEQ : (hh + 1) * SEQ]))
        dqs = jnp.transpose(jnp.concatenate(dq, axis=0)).astype(bf16).astype(f32)
        dks = jnp.where(low_head, dk[0], dk[1]).astype(bf16).astype(f32)
        s.gparams[:, ps] = turn(dqs, -s.sin_t[...]).astype(bf16)
        s.gparams[:, tile(p + 3, 128)] = turn(dks, -s.sin_t[...]).astype(bf16)
        s.gparams[:, tile(p + 6, 128)] = jnp.where(low_head, dv[0], dv[1]).astype(bf16)

    keep(M_QKV, 0, 0, mm(s.na_t[...], s.gparams[:, : 3 * D]))
    s.inner[...] = mm_nt(s.gparams[:, : 3 * D], s.w_qkv[...])
    norm_back(s.stream, s.inv_a, 0, s.grad)
    for c in range(3):
        cs = slice(c * 128, (c + 1) * 128)
        hidden_token = s.flag[...] == 1.0
        s.vec_acc[3:4, cs] = jnp.sum(jnp.where(hidden_token, s.grad[:, cs], 0.0), axis=0, keepdims=True)
        s.normed[:, cs] = jnp.where(hidden_token, 0.0, s.grad[:, cs]).astype(bf16)
    keep(M_IN, 0, 0, mm_tn(s.x5[...], s.normed[...]))

    sums = jnp.sum(s.bias_acc[...], axis=1, keepdims=True)
    sums = jnp.concatenate([sums[0:8], sums[8:16] - sums[0:8]], axis=0)
    entry = lax.broadcasted_iota(jnp.int32, (16, D), 0)
    target = jnp.where(entry < HEADS, entry, jnp.where((entry >= 8) & (entry < 8 + HEADS), entry - 8 + HEADS, -1))
    bias_row = jnp.sum(
        jnp.where(target == lax.broadcasted_iota(jnp.int32, (16, D), 1), sums, 0.0), axis=0, keepdims=True
    )
    row = lax.broadcasted_iota(jnp.int32, (8, D), 0)
    small_sum = jnp.where(row == 4, jnp.sum(s.loss_acc[...]), jnp.where(row == 5, bias_row, s.vec_acc[...]))
    for copy in outgoing + cross:
        copy.wait_send()
    send = Pool(send_pool)
    s.blocks[BLOCKS] = jnp.zeros((SIDE, SIDE), bf16)
    toks = dims[0] * dims[1] * dims[2]

    def fill(h):
        @pl.loop(0, toks)
        def _(t):
            for i in range(per):
                at = (h, t // (dims[1] * dims[2]), t // dims[2] % dims[1], t % dims[2], i)
                gathered[at] = s.blocks[holder[(h * toks + t) * per + i]]

    everywhere = (slice(None),) * 3
    parts = cut_parts(REDUCE_PARTS)
    fill(1 - head)
    arriving, outgoing = {}, []

    def start_reduce(p, k):
        axes, a, n = parts[p]
        if k == 0:
            view = everywhere + (slice(None), pl.ds(a, n))
            copies = [remote(gathered.at[(1 - head,) + view], crossed.at[view], send(), recv(), place.partner())]
        else:
            axis, left = axes[k - 1], axes[k:]
            copies = []
            for j in range(1, dims[axis]):
                region = place.region(left, {axis: place.coordinate(axis, j)})
                src = gathered.at[(head,) + region + (slice(None), pl.ds(a, n))]
                copies.append(remote(src, landing[3 * p + k - 1].at[j - 1], send(), recv(), place.peer(axis, j)))
        for copy in copies:
            copy.start()
        arriving[p] = copies
        outgoing.extend(copies)

    def end_reduce(p, k):
        axes, a, n = parts[p]
        left = sorted(axes[k:])
        region = place.region(left)
        for copy in arriving[p]:
            copy.wait_recv()

        def body(*index):
            at = tuple(index[left.index(i)] if i in left else region[i] for i in range(3)) + (slice(None), pl.ds(a, n))
            value = gathered[(head,) + at].astype(f32)
            if k == 0:
                value = value + crossed[at].astype(f32)
            else:
                for j in range(1, dims[axes[k - 1]]):
                    value = value + landing[3 * p + k - 1][(j - 1,) + index].astype(f32)
            if k < 3:
                gathered[(head,) + at] = value.astype(bf16)
            else:
                owned[:, a : a + n, :] = value

        def loops(index):
            if len(index) == len(left):
                body(*index)
            else:
                pl.loop(0, dims[left[len(index)]])(lambda i: loops(index + (i,)))

        loops(())

    for p in range(len(parts)):
        start_reduce(p, 0)
    vec_sum = all_sum(place, small_sum, vec_buf, send, recv)
    vec_total = next(vec_sum)
    fill(head)

    ended = 0
    for step in REDUCE_PLAN:
        if step < 100:
            start_reduce(step // 10, step % 10)
            continue
        end_reduce(step // 10 % 10, step % 10)
        ended += 1
        if vec_total is None and ended in (12, 18):
            vec_total = next(vec_sum)
    while vec_total is None:
        vec_total = next(vec_sum)
    part_square = jnp.zeros((8, 128), f32)
    for i in range(per):
        piece = owned[i]
        part_square = part_square + jnp.sum((piece * piece).reshape(16, 8, 128), axis=0)
    sq_sum = all_sum(place, part_square, sq_buf, send, recv)
    total = next(sq_sum)
    for i in range(per):
        grad = owned[i]
        gram_left[i] = lax.dot_general(grad, grad, (((1,), (1,)), ((), ())), precision=highest, preferred_element_type=f32)
        turned = jnp.transpose(grad)
        gram_right[i] = jnp.dot(turned, grad, precision=highest, preferred_element_type=f32)
    while total is None:
        total = next(sq_sum)

    grads4 = vec_total[0:4]
    bias_total = vec_total[5:6, 0 : 2 * HEADS]
    square = jnp.sum(total) + jnp.sum(grads4 * grads4) + jnp.sum(bias_total * bias_total)
    grad_norm = jnp.sqrt(jnp.broadcast_to(square, (8, 128)))
    factor = jnp.minimum(1.0, clip_limit / grad_norm)
    loss_out[0, 0] = vec_total[4, 0]
    norm_out[0, 0] = jnp.max(grad_norm)
    factor_out[0, 0] = jnp.max(factor)
    small_out[...] = vec_total
    for copy in outgoing:
        copy.wait_send()


def update_kernel(
    factor_ref, small, vectors, vector_first, vector_second, var_bias, bias_first, bias_second, *rest,
):
    sources, rest = rest[:8], rest[8:]
    clipped_out, left_out, right_out, master_out = rest[:4]
    vector_grads, vector_second_new, vector_new, bias_grads, bias_second_new, bias_new = rest[4:10]
    held, made, in_sem, out_sem = rest[10:]
    fetches = [pltpu.make_async_copy(ref, held.at[k], in_sem.at[k]) for k, ref in enumerate(sources)]
    for copy in fetches:
        copy.start()
    owned, left_root, right_root, gram_left, left, gram_right, right, master = (held.at[k] for k in range(8))
    sends = [
        pltpu.make_async_copy(made.at[k], ref, out_sem.at[k])
        for k, ref in enumerate((clipped_out, left_out, right_out, master_out))
    ]
    factor = factor_ref[0, 0]
    per = owned.shape[0]
    fetches[0].wait()
    fetches[1].wait()
    grads = [owned[i] * factor for i in range(per)]
    for i in range(per):
        made[0, i] = grads[i]
    sends[0].start()
    shaped = [jnp.dot(left_root[i], grads[i], precision=highest, preferred_element_type=f32) for i in range(per)]
    fetches[2].wait()
    shaped = [jnp.dot(shaped[i], right_root[i], precision=highest, preferred_element_type=f32) for i in range(per)]
    for copy in fetches[3:]:
        copy.wait()
    for k, (stat, gram) in enumerate(((left, gram_left), (right, gram_right))):
        for i in range(per):
            scaled = jnp.where(factor > 0.0, gram[i] * factor * factor, 0.0)
            made[1 + k, i] = stat_beta * stat[i] + (1.0 - stat_beta) * scaled
        sends[1 + k].start()
    for i in range(per):
        unit = shaped[i] * lax.rsqrt(jnp.sum(shaped[i] * shaped[i]) / (SIDE * SIDE) + root_eps)
        made[3, i] = master[i] - mat_rate * (unit + decay_rate * master[i])
    sends[3].start()

    def adamw(gradient, first, second, old, grad_out, second_out, new_out):
        gradient = gradient * factor
        grad_out[...] = gradient
        first_next = beta_one * first[...] + (1.0 - beta_one) * gradient
        second_next = beta_two * second[...] + (1.0 - beta_two) * gradient * gradient
        ratio = first_next / (1.0 - beta_one**STEP) / (jnp.sqrt(second_next / (1.0 - beta_two**STEP)) + adam_eps)
        second_out[...] = second_next
        new_out[...] = old[...] - vec_rate * (ratio + decay_rate * old[...])

    adamw(small[0:4], vector_first, vector_second, vectors, vector_grads, vector_second_new, vector_new)
    adamw(small[5:6, 0 : 2 * HEADS], bias_first, bias_second, var_bias, bias_grads, bias_second_new, bias_new)
    for copy in sends:
        copy.wait()


def update_call(factor, small, owned, gram_left, gram_right, master, left, right, left_root, right_root, *rest):
    vmem, hbm = pl.BlockSpec(memory_space=pltpu.VMEM), pl.BlockSpec(memory_space=pl.ANY)
    sources = (owned, left_root, right_root, gram_left, left, gram_right, right, master)
    vectors, var_bias = rest[0], rest[3]
    outs = [master] * 4 + [vectors] * 3 + [var_bias] * 3
    return pl.pallas_call(
        update_kernel,
        out_shape=tuple(jax.ShapeDtypeStruct(a.shape, f32) for a in outs),
        in_specs=[pl.BlockSpec(memory_space=pltpu.SMEM)] + [vmem] * (1 + len(rest)) + [hbm] * 8,
        out_specs=(hbm,) * 4 + (vmem,) * 6,
        scratch_shapes=[
            pltpu.VMEM((8,) + master.shape, f32),
            pltpu.VMEM((4,) + master.shape, f32),
            pltpu.SemaphoreType.DMA((8,)),
            pltpu.SemaphoreType.DMA((4,)),
        ],
        compiler_params=pltpu.CompilerParams(vmem_limit_bytes=60 * 2**20),
        name="update",
    )(factor, small, *rest, *sources)


def step_call(dims, slots, holder, lengths, bias, master, patches, sizes, times, predict, variates, vectors):
    freq = (10000.0 ** (-np.arange(HEAD_DIM // 2) / (HEAD_DIM // 2))).astype(np.float32)
    freq = jnp.asarray(np.tile(freq[None], (8, 4)))
    per = master.shape[0]
    places = np.stack(np.unravel_index(np.arange(2 * math.prod(dims) * per), (2, *dims, per))).astype(np.int32)
    half = patches.shape[2]
    received, sent = semaphores(dims)
    smem = pl.BlockSpec(memory_space=pltpu.SMEM)
    vmem = pl.BlockSpec(memory_space=pltpu.VMEM)
    sems = pltpu.SemaphoreType.DMA
    landing = []
    for axes, _, n in cut_parts(REDUCE_PARTS):
        for k in range(3):
            wide = [dims[i] for i in sorted(axes[k + 1 :])]
            landing.append(pltpu.VMEM((max(dims[axes[k]] - 1, 1), *wide, per, n, SIDE), bf16))
    return pl.pallas_call(
        functools.partial(step_kernel, dims),
        out_shape=tuple(
            jax.ShapeDtypeStruct(shape, f32)
            for shape in [(1, 1)] * 4 + [(8, D)] + [(per, SIDE, SIDE)] * 3
        ),
        in_specs=[smem] * 5 + [vmem] * 9,
        out_specs=(smem,) * 4 + (vmem,) * 4,
        scratch_shapes=[pltpu.VMEM(shape, dtype) for shape, dtype in SCRATCH.values()]
        + [
            pltpu.VMEM((per, SIDE, SIDE), bf16),
            pltpu.VMEM((2,) + dims + (per, SIDE, SIDE), bf16),
            pltpu.VMEM(dims + (per, SIDE, SIDE), bf16),
            pltpu.VMEM((half, PMAX), bf16),
            pltpu.VMEM((3, 2, half), jnp.int32),
            pltpu.VMEM((3, 2, half), jnp.int32),
            sum_shape(dims, (8, 128)),
            sum_shape(dims, (8, D)),
            sum_shape(dims, (8, 128)),
            sems,
            sems((sent,)),
            sems((received,)),
            *landing,
        ],
        compiler_params=pltpu.CompilerParams(
            collective_id=0, has_side_effects=True, vmem_limit_bytes=63 * 2**20
        ),
        name="step",
    )(slots, jnp.asarray(places), holder, lengths, bias, master, patches, sizes, times, predict, variates, vectors, freq,
      jnp.asarray(group_order(), bf16))


def shards(
    dims,
    patches, patch_sizes, sample_lengths, variate_ids, time_ids, predict_mask, block_owner_slot,
    master_blocks, left_stats, right_stats, left_roots, right_roots,
    vectors, vector_first, vector_second, var_bias, bias_first, bias_second,
):
    slot_count = master_blocks.shape[0] * lax.axis_size("head") * lax.axis_size("tok")
    match = block_owner_slot[None, :] == jnp.arange(slot_count)[:, None]
    holder = BLOCKS + jnp.sum(jnp.where(match, jnp.arange(BLOCKS)[None, :] - BLOCKS, 0), axis=1)
    loss_sum, count, grad_norm, factor, small, owned, gram_left, gram_right = step_call(
        dims, block_owner_slot, holder, sample_lengths, var_bias[0], master_blocks, patches, patch_sizes, time_ids,
        predict_mask, variate_ids, vectors,
    )
    outs = update_call(
        factor, small, owned, gram_left, gram_right, master_blocks, left_stats, right_stats, left_roots, right_roots,
        vectors, vector_first, vector_second, var_bias, bias_first, bias_second,
    )
    return (loss_sum.reshape(()), count.reshape(()), grad_norm.reshape(())) + tuple(outs)


def solution(mesh):
    rep = P()
    dims = tok_dims(mesh.shape["tok"])
    slot = P(("head", "tok"), None, None)
    return jax.shard_map(
        functools.partial(shards, dims),
        mesh=mesh,
        in_specs=(
            P(None, "tok", "head", None), P(None, "tok", "head"), P(None, "tok", None), P(None, "tok", None),
            P(None, "tok", "head"), P(None, "tok", "head"), rep, slot, slot, slot, slot, slot,
            rep, rep, rep, rep, rep, rep,
        ),
        out_specs=(rep, rep, rep, slot, slot, slot, slot, rep, rep, rep, rep, rep, rep),
        check_vma=False,
    )
```

```python
import functools
import itertools
import math

import jax
import jax.numpy as jnp
import numpy as np
from jax import lax
from jax.experimental import pallas as pl
from jax.experimental.pallas import tpu as pltpu
from jax.sharding import PartitionSpec as P

D = 384
FF = 1024
HEADS = 6
HEAD_DIM = 64
PSIZES = 5
PMAX = 128
COMPS = 4
SEQ = 512
SIDE = 128
STEP = 10
HEADCOLS = 3 * COMPS * PMAX
BLOCKS = 159

norm_eps = 1e-06
scale_floor = 0.05
half_log_tau = 0.9189385332046727
clip_limit = 0.02
mat_rate = 0.01
vec_rate = 0.3
decay_rate = 0.01
beta_one = 0.9
beta_two = 0.95
stat_beta = 0.99
root_eps = 1e-06
adam_eps = 1e-08
highest = lax.Precision.HIGHEST
f32 = jnp.float32
bf16 = jnp.bfloat16

GRIDS = ((5, 3), (3, 12), (3, 9), (3, 3), (3, 16), (8, 3))
FIRSTS = (0, 15, 51, 78, 87, 135)
M_IN, M_HEAD, M_QKV, M_OUT, M_GU, M_DOWN = range(6)


def mm(a, b):
    return jnp.dot(a, b, preferred_element_type=f32)


def mm_nt(a, b):
    return lax.dot_general(a, b, (((1,), (1,)), ((), ())), preferred_element_type=f32)


def mm_tn(a, b):
    return lax.dot_general(a, b, (((0,), (0,)), ((), ())), preferred_element_type=f32)


GROUP = 384


def group_order():
    order = np.zeros((GROUP, GROUP), np.float32)
    for col in range(GROUP):
        order[col, (col % 12) * 32 + col // 12] = 1.0
    return order


def swap_quarters(parts):
    lane = lax.broadcasted_iota(jnp.int32, (1, 128), 1)
    low, even = lane < 64, lane % 64 < 32
    a, b, c, d = parts
    a, c = jnp.where(low, a, pltpu.roll(c, 64, 1)), jnp.where(low, pltpu.roll(a, 64, 1), c)
    b, d = jnp.where(low, b, pltpu.roll(d, 64, 1)), jnp.where(low, pltpu.roll(b, 64, 1), d)
    a, b = jnp.where(even, a, pltpu.roll(b, 32, 1)), jnp.where(even, pltpu.roll(a, 96, 1), b)
    c, d = jnp.where(even, c, pltpu.roll(d, 32, 1)), jnp.where(even, pltpu.roll(c, 96, 1), d)
    return a, b, c, d


SCRATCH = dict(
    w_in=((640, D), bf16), w_head=((D, HEADCOLS), bf16), w_qkv=((D, 3 * D), bf16), w_out=((D, D), bf16),
    w_gu=((D, 2 * FF), bf16), w_down=((FF, D), bf16), w_headp=((D, HEADCOLS), bf16),
    blocks=((BLOCKS + 1, SIDE, SIDE), bf16),
    x5=((SEQ, 640), bf16), weight=((SEQ, PMAX), f32), flag=((SEQ, 128), f32),
    cos_t=((SEQ, 128), f32), sin_t=((SEQ, 128), f32),
    code_t=((SEQ, SEQ), f32), probs=((HEADS, SEQ, SEQ), f32),
    stream=((SEQ, D), f32), middle=((SEQ, D), f32), last=((SEQ, D), f32), grad=((SEQ, D), f32), inner=((SEQ, D), f32),
    inv_a=((SEQ, 128), f32), inv_b=((SEQ, 128), f32), inv_f=((SEQ, 128), f32),
    normed=((SEQ, D), bf16), na_t=((D, SEQ), bf16), nb_t=((D, SEQ), bf16), nf_t=((D, SEQ), bf16),
    qs=((SEQ, D), bf16), ks=((SEQ, D), bf16), vs=((SEQ, D), bf16), merged=((SEQ, D), bf16), merged_t=((D, SEQ), bf16),
    silu=((SEQ, FF), f32), slope=((SEQ, FF), f32), hidden=((SEQ, FF), bf16),
    params=((SEQ, HEADCOLS), f32), gparams=((SEQ, HEADCOLS), bf16), ggu=((SEQ, 2 * FF), bf16),
    loss_acc=((32, 128), f32), bias_acc=((16, 128), f32), vec_acc=((8, D), f32),
    meta=((8, SEQ), jnp.int32), row_patches=((SEQ, PMAX), bf16),
)


def tile(i, size):
    return pl.ds(pl.multiple_of(i * size, size), size)


MESH = pl.DeviceIdType.MESH


def tok_dims(count):
    return {16: (4, 2, 2), 128: (4, 4, 8)}.get(count, (count, 1, 1))


class Place:
    def __init__(self, dims):
        self.dims = dims
        self.head = lax.axis_index("head")
        tok = lax.axis_index("tok")
        self.tok = tok
        self.strides = (dims[1] * dims[2], dims[2], 1)
        self.at = [lax.rem(lax.div(tok, s), n) for s, n in zip(self.strides, dims)]

    def coordinate(self, axis, step):
        return lax.rem(self.at[axis] + step, self.dims[axis])

    def peer(self, axis, step):
        return (self.head, self.tok + (self.coordinate(axis, step) - self.at[axis]) * self.strides[axis])

    def partner(self):
        return (1 - self.head, self.tok)

    def groups(self):
        result, size = [[None]], 2
        for axis in (1, 2, 0):
            if self.dims[axis] == 1:
                continue
            if size * self.dims[axis] > 8:
                result.append([])
                size = 1
            result[-1].append(axis)
            size *= self.dims[axis]
        return result

    def members(self, group):
        sizes = [2 if axis is None else self.dims[axis] for axis in group]
        mine = 0
        for axis, n in zip(group, sizes):
            mine = mine * n + (self.head if axis is None else self.at[axis])
        others = []
        for steps in itertools.product(*[range(n) for n in sizes]):
            head, tok = self.head, self.tok
            for axis, step in zip(group, steps):
                if axis is None:
                    head = lax.rem(head + step, 2)
                else:
                    tok = tok + (self.coordinate(axis, step) - self.at[axis]) * self.strides[axis]
            if any(steps):
                others.append((head, tok))
        return mine, math.prod(sizes), others

    def greet(self, meanwhile):
        barrier = pltpu.get_barrier_semaphore()
        groups = self.groups()
        others = [other for group in groups for other in self.members(group)[2]]
        joint = [group for group in groups if len(group) > 1]
        singles = {group[0] for group in groups if len(group) == 1} | {a for group in joint for a in group}
        others += [self.peer(a, j) for a in range(3) if a not in singles for j in range(1, self.dims[a])]
        for other in others:
            pl.semaphore_signal(barrier, inc=1, device_id=other, device_id_type=MESH)
        meanwhile()
        pl.semaphore_wait(barrier, len(others))

    def region(self, whole, fixed=None):
        fixed = fixed or {}
        return tuple(slice(None) if a in whole else fixed.get(a, self.at[a]) for a in range(3))


def remote(src, dst, send, recv, device):
    return pltpu.make_async_remote_copy(
        src_ref=src, dst_ref=dst, send_sem=send, recv_sem=recv, device_id=device, device_id_type=MESH
    )


def split_rows(rows, shares):
    units = rows // 16
    edges = [round(units * sum(shares[:i]) / sum(shares)) * 16 for i in range(len(shares) + 1)]
    return [(a, b - a) for a, b in zip(edges, edges[1:])]


class Pool:
    def __init__(self, ref):
        self.ref, self.used = ref, 0

    def __call__(self):
        self.used += 1
        return self.ref.at[self.used - 1]


def all_sum(place, values, buf, send, recv):
    total = values
    for k, group in enumerate(place.groups()):
        mine, size, others = place.members(group)
        buf[k, mine] = total
        copies = [remote(buf.at[k, mine], buf.at[k, mine], send(), recv(), other) for other in others]
        for copy in copies:
            copy.start()
        yield None
        for copy in copies:
            copy.wait()
        total = buf[k, 0]
        for i in range(1, size):
            total = total + buf[k, i]
    yield total


def sum_sizes(dims):
    place = Place.__new__(Place)
    place.dims = dims
    return [math.prod(2 if a is None else dims[a] for a in group) for group in place.groups()]


def sum_shape(dims, shape):
    sizes = sum_sizes(dims)
    return pltpu.VMEM((len(sizes), max(sizes)) + shape, f32)


GATHER_PARTS = (
    ((1, 2, 0), 1), ((0, 1, 2), 1), ((0, 2, 1), 1), ((0, 1, 2), 1), ((0, 1, 2), 1), ((0, 2, 1), 1), ((1, 0, 2), 1), ((2, 0, 1), 1),
)
PREPARE_AFTER = 2
GATHER_PLAN = (
    0, 10, 20, 60, 100, 1, 30, 70, 110, 11, 50, 120, 21, 130, 31, 40, 111, 12, 160, 61, 150, 51, 170, 71,
    121, 22, 140, 41, 131, 32, 141, 42, 151, 52, 101, 2, 122, 171, 72, 112, 161, 62, 172, 132, 142, 102, 152, 162,
)
REDUCE_PARTS = (
    ((2, 0, 1), 1), ((0, 1, 2), 1), ((2, 1, 0), 1), ((1, 2, 0), 1), ((2, 1, 0), 1), ((1, 0, 2), 1), ((1, 2, 0), 1), ((2, 1, 0), 1),
)
REDUCE_PLAN = (
    100, 1, 110, 11, 120, 21, 130, 31, 140, 41, 150, 51, 101, 2, 111, 12, 131, 32, 160, 61, 121, 22, 170, 71,
    151, 52, 112, 13, 122, 23, 141, 42, 161, 62, 132, 33, 152, 53, 171, 72, 102, 3, 142, 43, 162, 63, 133, 172,
    73, 143, 163, 153, 113, 123, 103, 173,
)


def cut_parts(table):
    return [(order, a, n) for (order, _), (a, n) in zip(table, split_rows(SIDE, [s for _, s in table]))]


def semaphores(dims):
    steps = sum(n - 1 for n in dims)
    sums = sum(n - 1 for n in sum_sizes(dims))
    gather = sum(steps + 1 + sum(dims[a] - 1 for a in order[1:]) for order, _ in GATHER_PARTS) + 2 + sums
    reduce = len(REDUCE_PARTS) * (steps + 1) + 2 * sums
    return gather + reduce, max(gather, reduce)


def step_kernel(
    dims, slots, places, lengths, bias, *rest,
):
    sources, rest = rest[:9], rest[9:]
    loss_out, count_out, norm_out, factor_out, small_out = rest[:5]
    results, rest = rest[5:8], rest[8:]
    (master, patches, sizes, times_in, predict_in, variates_in, vectors, freq, order), rest = rest[:9], rest[9:]
    (owned, gram_left, gram_right), rest = rest[:3], rest[3:]
    (fetch_sem, result_sem, holder_row, holder, holder_sem), rest = rest[:5], rest[5:]
    held = (master, patches, sizes, times_in, predict_in, variates_in, vectors, freq, order)
    fetches = [pltpu.make_async_copy(a, b, fetch_sem.at[k]) for k, (a, b) in enumerate(zip(sources, held))]
    for copy in fetches:
        copy.start()
    stores = [
        pltpu.make_async_copy(a, b, result_sem.at[k]) for k, (a, b) in enumerate(zip((owned, gram_left, gram_right), results))
    ]
    names = list(SCRATCH)
    s = type("S", (), dict(zip(names, rest)))
    rest = rest[len(names) :]
    mine, gathered, crossed, land_patch, land_ints, own_ints = rest[:6]
    cnt_buf, vec_buf, sq_buf, own_sem, send_pool, recv_pool = rest[6:12]
    send, recv = Pool(send_pool), Pool(recv_pool)
    landing = rest[12:]
    place = Place(dims)
    per = mine.shape[0]
    head = place.head
    lane = lax.broadcasted_iota(jnp.int32, (1, 128), 1)
    first_half = lane % HEAD_DIM < HEAD_DIM // 2
    low_head = lane < HEAD_DIM
    weights = (s.w_in, s.w_head, s.w_qkv, s.w_out, s.w_gu, s.w_down)

    def keep(m, r0, c0, value):
        value = value.astype(bf16)
        cols = GRIDS[m][1]
        for r in range(value.shape[0] // SIDE):
            for c in range(value.shape[1] // SIDE):
                piece = value[r * SIDE : (r + 1) * SIDE, c * SIDE : (c + 1) * SIDE]
                s.blocks[FIRSTS[m] + (r0 + r) * cols + c0 + c] = piece

    half = SEQ // 2
    s.meta[4:8, :] = jnp.zeros((4, SEQ), jnp.int32)

    def local_work():
        for copy in fetches[:6]:
            copy.wait()
        mine[...] = master[...].astype(bf16)
        for k, ref in enumerate((sizes, times_in, predict_in)):
            own_ints[k, :, :] = ref[:, 0, :]
        for h in range(2):

            @pl.when(head == h)
            def _():
                here = slice(h * half, (h + 1) * half)
                s.row_patches[here, :] = patches[h, 0]
                for k, ref in enumerate((sizes, times_in, predict_in)):
                    s.meta[k : k + 1, here] = ref[h]
                s.meta[3:4, :] = variates_in[h]

    place.greet(local_work)
    swaps = [
        remote(patches.at[1 - head, 0], land_patch, send(), recv(), place.partner()),
        remote(own_ints, land_ints, send(), recv(), place.partner()),
    ]
    for copy in swaps:
        copy.start()
    parts = cut_parts(GATHER_PARTS)

    def block(head_index, whole, fixed, a, n):
        return gathered.at[(head_index,) + place.region(whole, fixed) + (slice(None), pl.ds(a, n))]

    arriving, outgoing, cross = {}, list(swaps), []
    own = pltpu.make_async_copy(mine, gathered.at[(head,) + place.region(())], own_sem)
    own.start()

    def start_gather(p, k):
        axes, a, n = parts[p]
        axis, whole = axes[k], axes[:k]
        arriving[p] = []
        for j in range(1, dims[axis]):
            src = mine.at[:, pl.ds(a, n)] if k == 0 else block(head, whole, None, a, n)
            copy = remote(src, block(head, whole, None, a, n), send(), recv(), place.peer(axis, j))
            copy.start()
            arriving[p].append(copy)
        outgoing.extend(arriving[p])

    def end_gather(p, k):
        axes, a, n = parts[p]
        for copy in arriving[p]:
            copy.wait_recv()
        axis, whole = axes[k], axes[:k]
        if k == 0:
            views = [block(head, axes[:1], None, a, n)]
        else:
            views = [
                block(head, whole, {axis: place.coordinate(axis, dims[axis] - j)}, a, n) for j in range(1, dims[axis])
            ]
        for view in views:
            copy = remote(view, view, send(), recv(), place.partner())
            copy.start()
            cross.append(copy)

    first = next(i for i, step in enumerate(GATHER_PLAN) if step >= 100)
    for step in GATHER_PLAN[:first]:
        start_gather(step // 10, step % 10)
    wide_size = jnp.zeros_like(own_ints[0])
    for c in range(PSIZES):
        wide_size = wide_size + jnp.where(own_ints[0] == c, PMAX * 2**c // 2 ** (PSIZES - 1), 0)
    partial = (wide_size * own_ints[2]).astype(f32)
    partial = jnp.sum(partial[:, :128] + partial[:, 128:], axis=0, keepdims=True)
    counting = all_sum(place, jnp.concatenate([partial, jnp.zeros((7, 128), f32)], axis=0), cnt_buf, send, recv)
    counted = next(counting)
    own.wait()
    for copy in swaps:
        copy.wait_recv()
    for h in range(2):

        @pl.when(head == h)
        def _():
            there = slice((1 - h) * half, (2 - h) * half)
            s.row_patches[there, :] = land_patch[...]
            for k in range(3):
                s.meta[k : k + 1, there] = land_ints[k, h : h + 1, :]

    def prepare_holder():
        position = lax.broadcasted_iota(jnp.int32, holder_row.shape, 1)

        def body(b, row):
            return jnp.where(position == slots[b], b, row)

        holder_row[...] = lax.fori_loop(0, BLOCKS, body, jnp.full(holder_row.shape, BLOCKS, jnp.int32), unroll=3)
        copy = pltpu.make_async_copy(holder_row, holder, holder_sem)
        copy.start()
        copy.wait()

    def prepare_tokens():
        for copy in fetches[6:]:
            copy.wait()
        metaf = s.meta[...].astype(f32)
        columns = jnp.transpose(metaf)
        codes, times, flag = columns[:, 0:1], columns[:, 1:2], columns[:, 2:3]
        position = lax.broadcasted_iota(jnp.int32, (1, SEQ), 1)
        ids = jnp.zeros((1, SEQ), f32)
        end = jnp.int32(0)
        for j in range(lengths.shape[2]):
            end = end + lengths[head, 0, j]
            ids = ids + jnp.where(position >= end, 1.0, 0.0)
        variates = metaf[3:4]
        id_columns = jnp.transpose(jnp.concatenate([ids] * 8, axis=0))[:, 0:1]
        var_columns = columns[:, 3:4]
        for c in range(4):
            cs = slice(c * 128, (c + 1) * 128)
            same_sample = id_columns == ids[:, cs]
            same_var = var_columns == variates[:, cs]
            s.code_t[:, cs] = jnp.where(same_sample, jnp.where(same_var, 2.0, 1.0), 0.0)
        s.flag[...] = jnp.broadcast_to(flag, (SEQ, 128))
        angle = times * freq[0:1, :]
        s.cos_t[...] = jnp.cos(angle)
        s.sin_t[...] = jnp.where(first_half, -1.0, 1.0) * jnp.sin(angle)

        wide = s.row_patches[...].astype(f32)
        weight = jnp.zeros((SEQ, PMAX), f32)
        for c in range(PSIZES):
            keep = (codes == float(c)) & (lane < PMAX * 2**c // 2 ** (PSIZES - 1))
            s.x5[:, c * 128 : (c + 1) * 128] = jnp.where(keep, wide, 0.0).astype(bf16)
            weight = jnp.where(keep, 1.0, weight)
        s.weight[...] = jnp.where(flag == 1.0, weight, 0.0)
    ended = 0
    for step in GATHER_PLAN[first:]:
        if step < 100:
            start_gather(step // 10, step % 10)
            continue
        end_gather(step // 10 % 10, step % 10)
        ended += 1
        if counted is None and ended in (4, 8):
            counted = next(counting)
        if ended == PREPARE_AFTER:
            prepare_tokens()
        if ended == PREPARE_AFTER + 3:
            prepare_holder()
    while counted is None:
        counted = next(counting)
    value_count = jnp.sum(counted)
    count_out[0, 0] = value_count
    for copy in cross:
        copy.wait_recv()

    def load(m):
        n_rows, cols = GRIDS[m]

        @pl.loop(0, n_rows)
        def _(r):
            for c in range(cols):
                slot = slots[FIRSTS[m] + r * cols + c]
                where = tuple(places[k, slot] for k in range(5))
                weights[m][tile(r, SIDE), c * SIDE : (c + 1) * SIDE] = gathered[where]

    for m in range(6):
        load(m)

    def turn(v, sine):
        swapped = jnp.where(first_half, pltpu.roll(v, 96, 1), pltpu.roll(v, 32, 1))
        return v * s.cos_t[...] + swapped * sine

    embedded = mm(s.x5[...], s.w_in[...])
    for c in range(3):
        cs = slice(c * 128, (c + 1) * 128)
        s.stream[:, cs] = jnp.where(s.flag[...] == 1.0, vectors[3:4, cs], embedded[:, cs])

    def norm(src, inv_ref, gain, dst_t):
        @pl.loop(0, SEQ // 128)
        def _(i):
            rs = tile(i, 128)
            v = src[rs, :]
            inverse = lax.rsqrt(jnp.sum(v * v, axis=-1, keepdims=True) / D + norm_eps)
            inv_ref[rs, :] = jnp.broadcast_to(inverse, (128, 128))
            s.normed[rs, :] = (v * inverse * gain).astype(bf16)

        dst_t[...] = jnp.transpose(s.normed[...])

    def norm_back(src, inv_ref, row, extra):
        gain = vectors[row : row + 1, :]

        @pl.loop(0, SEQ // 128)
        def _(i):
            rs = tile(i, 128)
            up = s.inner[rs, :]
            inverse = inv_ref[rs, 0:1]
            scaled = src[rs, :] * inverse
            inner = up * gain
            mean = jnp.sum(inner * scaled, axis=-1, keepdims=True) / D
            result = inverse * (inner - scaled * mean)
            s.grad[rs, :] = result if extra is None else result + extra[rs, :]
            s.vec_acc[row : row + 1, :] += jnp.sum(up * scaled, axis=0, keepdims=True)

    s.vec_acc[...] = jnp.zeros_like(s.vec_acc)
    norm(s.stream, s.inv_a, vectors[0:1, :], s.na_t)
    mixed = mm(s.normed[...], s.w_qkv[...])
    for part, dst in ((0, s.qs), (1, s.ks), (2, s.vs)):
        for c in range(3):
            piece = mixed[:, part * D + c * 128 : part * D + (c + 1) * 128]
            if part < 2:
                piece = turn(piece, s.sin_t[...])
            dst[:, c * 128 : (c + 1) * 128] = piece.astype(bf16)

    @pl.loop(0, HEADS // 2)
    def _(p):
        ps = tile(p, 128)
        qp, kp = s.qs[:, ps], s.ks[:, ps]
        vt = jnp.transpose(s.vs[:, ps])
        outs = []
        for hh in range(2):
            mine = low_head if hh == 0 else jnp.logical_not(low_head)
            qm = jnp.where(mine, qp.astype(f32) * HEAD_DIM**-0.5, 0.0).astype(bf16)
            b0 = bias[2 * p + hh]
            b1 = bias[HEADS + 2 * p + hh]
            parts = []
            for c in range(1):
                cs = slice(c * 512, (c + 1) * 512)
                code = s.code_t[:, cs]
                score = mm_nt(kp, qm[cs, :])
                score = jnp.where(code > 0.5, score + jnp.where(code > 1.5, b0, b1), -1e30)
                raised = jnp.exp(score - jnp.max(score, axis=0, keepdims=True))
                prob = raised * (1.0 / jnp.sum(raised, axis=0, keepdims=True))
                s.probs[2 * p + hh, :, cs] = prob
                parts.append(mm(vt[hh * 64 : (hh + 1) * 64, :], prob.astype(bf16)))
            outs.append(jnp.concatenate(parts, axis=1))
        out_t = jnp.concatenate(outs, axis=0).astype(bf16)
        s.merged_t[ps, :] = out_t
        s.merged[:, ps] = jnp.transpose(out_t)

    s.middle[...] = s.stream[...] + mm(s.merged[...], s.w_out[...])
    norm(s.middle, s.inv_b, vectors[1:2, :], s.nb_t)

    @pl.loop(0, FF // 1024)
    def _(j):
        js = tile(j, 1024)
        opening = mm(s.normed[...], s.w_gu[:, js])
        up = mm(s.normed[...], s.w_gu[:, tile(j + FF // 1024, 1024)])
        sigma = 1.0 / (1.0 + jnp.exp(-opening))
        silu = opening * sigma
        s.silu[:, js] = silu
        s.slope[:, js] = up * sigma * (1.0 + opening * (1.0 - sigma))
        s.hidden[:, js] = (silu * up).astype(bf16)

    s.last[...] = s.middle[...] + mm(s.hidden[...], s.w_down[...])
    norm(s.last, s.inv_f, vectors[2:3, :], s.nf_t)


    wide = [mm(s.w_head[:, g * GROUP : (g + 1) * GROUP], order[...]) for g in range(4)]
    for kind in range(3):
        pieces = swap_quarters([w[:, kind * 128 : (kind + 1) * 128] for w in wide])
        for k, piece in enumerate(pieces):
            at = (4 * kind + k) * 128
            s.w_headp[:, at : at + 128] = piece.astype(bf16)

    @pl.loop(0, HEADCOLS // 512)
    def _(j):
        js = tile(j, 512)
        s.params[:, js] = mm(s.normed[...], s.w_headp[:, js])

    inv_n = 1.0 / value_count
    s.loss_acc[...] = jnp.zeros_like(s.loss_acc)

    @pl.loop(0, SEQ // 32)
    def _(i):
        rs = tile(i, 32)
        y = s.row_patches[rs, :].astype(f32)
        weight = s.weight[rs, :]
        logits, means, raws = [
            [s.params[rs, (4 * kind + k) * 128 : (4 * kind + k + 1) * 128] for k in range(COMPS)] for kind in range(3)
        ]
        top = jnp.maximum(jnp.maximum(logits[0], logits[1]), jnp.maximum(logits[2], logits[3]))
        shifted = [v - top for v in logits]
        raised = [jnp.exp(v) for v in shifted]
        total = raised[0] + raised[1] + raised[2] + raised[3]
        log_total = jnp.log(total)
        inv_total = 1.0 / total
        terms, zs, inv_widths = [], [], []
        for k in range(COMPS):
            width = jnp.maximum(raws[k], 0.0) + jnp.log1p(jnp.exp(-jnp.abs(raws[k]))) + scale_floor
            inv_width = 1.0 / width
            z = (y - means[k]) * inv_width
            terms.append((shifted[k] - log_total) - 0.5 * z * z - jnp.log(width) - half_log_tau)
            zs.append(z)
            inv_widths.append(inv_width)
        best = jnp.maximum(jnp.maximum(terms[0], terms[1]), jnp.maximum(terms[2], terms[3]))
        lifted = [jnp.exp(t - best) for t in terms]
        lift_total = lifted[0] + lifted[1] + lifted[2] + lifted[3]
        inv_lift = 1.0 / lift_total
        s.loss_acc[...] += jnp.where(weight > 0.0, -(best + jnp.log(lift_total)), 0.0)
        scale = -(weight * inv_n)
        for k in range(COMPS):
            share = lifted[k] * inv_lift
            d_term = scale * share
            ratio = zs[k] * inv_widths[k]
            d_logit = scale * (share - raised[k] * inv_total)
            d_width = d_term * (zs[k] * ratio - inv_widths[k])
            sigma = 1.0 / (1.0 + jnp.exp(-raws[k]))
            for kind, value in ((0, d_logit), (1, d_term * ratio), (2, d_width * sigma)):
                at = (4 * kind + k) * 128
                s.gparams[rs, at : at + 128] = value.astype(bf16)

    for kind in range(3):
        ks = slice(kind * 512, (kind + 1) * 512)
        wide = mm(s.nf_t[...], s.gparams[:, ks])
        pieces = swap_quarters([wide[:, k * 128 : (k + 1) * 128] for k in range(4)])
        for g in range(4):
            s.w_head[:, (3 * g + kind) * 128 : (3 * g + kind + 1) * 128] = pieces[g].astype(bf16)
    for g in range(4):
        gs = slice(g * GROUP, (g + 1) * GROUP)
        keep(M_HEAD, 0, 3 * g, mm_nt(s.w_head[:, gs], order[...]))
    s.inner[...] = mm_nt(s.gparams[...], s.w_headp[...])
    norm_back(s.last, s.inv_f, 2, None)

    s.normed[...] = s.grad[...].astype(bf16)

    @pl.loop(0, FF // 1024)
    def _(j):
        js = tile(j, 1024)
        keep(M_DOWN, 8 * j, 0, mm_tn(s.hidden[:, js], s.normed[...]))
        up_grad = mm_nt(s.normed[...], s.w_down[js, :])
        s.ggu[:, js] = (up_grad * s.slope[:, js]).astype(bf16)
        s.ggu[:, tile(j + FF // 1024, 1024)] = (up_grad * s.silu[:, js]).astype(bf16)

    @pl.loop(0, 2 * FF // 512)
    def _(j):
        keep(M_GU, 0, 4 * j, mm(s.nb_t[...], s.ggu[:, tile(j, 512)]))

    s.inner[...] = mm_nt(s.ggu[...], s.w_gu[...])
    norm_back(s.middle, s.inv_b, 1, s.grad)

    s.normed[...] = s.grad[...].astype(bf16)
    keep(M_OUT, 0, 0, mm(s.merged_t[...], s.normed[...]))
    s.merged[...] = mm_nt(s.normed[...], s.w_out[...]).astype(bf16)
    s.bias_acc[...] = jnp.zeros_like(s.bias_acc)

    @pl.loop(0, HEADS // 2)
    def _(p):
        ps = tile(p, 128)
        qp, kp, vp, dop = s.qs[:, ps], s.ks[:, ps], s.vs[:, ps], s.merged[:, ps]
        kt = jnp.transpose(kp)
        dq, dk, dv = [], [], []
        for hh in range(2):
            mine = low_head if hh == 0 else jnp.logical_not(low_head)
            dom = jnp.where(mine, dop.astype(f32), 0.0).astype(bf16)
            same_sum = jnp.zeros((1, 256), f32)
            all_sum = jnp.zeros((1, 256), f32)
            for c in range(2):
                cs = slice(c * 256, (c + 1) * 256)
                prob = s.probs[2 * p + hh, :, cs]
                d_prob = mm_nt(vp, dom[cs, :])
                d_score = prob * (d_prob - jnp.sum(prob * d_prob, axis=0, keepdims=True))
                same_sum += jnp.sum(jnp.where(s.code_t[:, cs] > 1.5, d_score, 0.0), axis=0, keepdims=True)
                all_sum += jnp.sum(d_score, axis=0, keepdims=True)
                s.ggu[:, hh * SEQ + c * 256 : hh * SEQ + (c + 1) * 256] = (d_score * HEAD_DIM**-0.5).astype(bf16)
            s.bias_acc[pl.ds(2 * p + hh, 1), :] = same_sum[:, :128] + same_sum[:, 128:]
            s.bias_acc[pl.ds(8 + 2 * p + hh, 1), :] = all_sum[:, :128] + all_sum[:, 128:]
            dv.append(mm(s.probs[2 * p + hh].astype(bf16), dop))
            dk.append(mm(s.ggu[:, hh * SEQ : (hh + 1) * SEQ], qp))
            dq.append(mm(kt[hh * 64 : (hh + 1) * 64, :], s.ggu[:, hh * SEQ : (hh + 1) * SEQ]))
        dqs = jnp.transpose(jnp.concatenate(dq, axis=0)).astype(bf16).astype(f32)
        dks = jnp.where(low_head, dk[0], dk[1]).astype(bf16).astype(f32)
        s.gparams[:, ps] = turn(dqs, -s.sin_t[...]).astype(bf16)
        s.gparams[:, tile(p + 3, 128)] = turn(dks, -s.sin_t[...]).astype(bf16)
        s.gparams[:, tile(p + 6, 128)] = jnp.where(low_head, dv[0], dv[1]).astype(bf16)

    keep(M_QKV, 0, 0, mm(s.na_t[...], s.gparams[:, : 3 * D]))
    s.inner[...] = mm_nt(s.gparams[:, : 3 * D], s.w_qkv[...])
    norm_back(s.stream, s.inv_a, 0, s.grad)
    for c in range(3):
        cs = slice(c * 128, (c + 1) * 128)
        hidden_token = s.flag[...] == 1.0
        s.vec_acc[3:4, cs] = jnp.sum(jnp.where(hidden_token, s.grad[:, cs], 0.0), axis=0, keepdims=True)
        s.normed[:, cs] = jnp.where(hidden_token, 0.0, s.grad[:, cs]).astype(bf16)
    keep(M_IN, 0, 0, mm_tn(s.x5[...], s.normed[...]))

    sums = jnp.sum(s.bias_acc[...], axis=1, keepdims=True)
    sums = jnp.concatenate([sums[0:8], sums[8:16] - sums[0:8]], axis=0)
    entry = lax.broadcasted_iota(jnp.int32, (16, D), 0)
    target = jnp.where(entry < HEADS, entry, jnp.where((entry >= 8) & (entry < 8 + HEADS), entry - 8 + HEADS, -1))
    bias_row = jnp.sum(
        jnp.where(target == lax.broadcasted_iota(jnp.int32, (16, D), 1), sums, 0.0), axis=0, keepdims=True
    )
    row = lax.broadcasted_iota(jnp.int32, (8, D), 0)
    small_sum = jnp.where(row == 4, jnp.sum(s.loss_acc[...]), jnp.where(row == 5, bias_row, s.vec_acc[...]))
    for copy in outgoing + cross:
        copy.wait_send()
    send = Pool(send_pool)
    s.blocks[BLOCKS] = jnp.zeros((SIDE, SIDE), bf16)
    toks = dims[0] * dims[1] * dims[2]

    def fill(h):
        @pl.loop(0, toks)
        def _(t):
            for i in range(per):
                at = (h, t // (dims[1] * dims[2]), t // dims[2] % dims[1], t % dims[2], i)
                gathered[at] = s.blocks[holder[0, (h * toks + t) * per + i]]

    everywhere = (slice(None),) * 3
    parts = cut_parts(REDUCE_PARTS)
    fill(1 - head)
    arriving, outgoing = {}, []

    def start_reduce(p, k):
        axes, a, n = parts[p]
        if k == 0:
            view = everywhere + (slice(None), pl.ds(a, n))
            copies = [remote(gathered.at[(1 - head,) + view], crossed.at[view], send(), recv(), place.partner())]
        else:
            axis, left = axes[k - 1], axes[k:]
            copies = []
            for j in range(1, dims[axis]):
                region = place.region(left, {axis: place.coordinate(axis, j)})
                src = gathered.at[(head,) + region + (slice(None), pl.ds(a, n))]
                copies.append(remote(src, landing[3 * p + k - 1].at[j - 1], send(), recv(), place.peer(axis, j)))
        for copy in copies:
            copy.start()
        arriving[p] = copies
        outgoing.extend(copies)

    def end_reduce(p, k):
        axes, a, n = parts[p]
        left = sorted(axes[k:])
        region = place.region(left)
        for copy in arriving[p]:
            copy.wait_recv()

        def body(*index):
            at = tuple(index[left.index(i)] if i in left else region[i] for i in range(3)) + (slice(None), pl.ds(a, n))
            value = gathered[(head,) + at].astype(f32)
            if k == 0:
                value = value + crossed[at].astype(f32)
            else:
                for j in range(1, dims[axes[k - 1]]):
                    value = value + landing[3 * p + k - 1][(j - 1,) + index].astype(f32)
            if k < 3:
                gathered[(head,) + at] = value.astype(bf16)
            else:
                owned[:, a : a + n, :] = value

        def loops(index):
            if len(index) == len(left):
                body(*index)
            else:
                pl.loop(0, dims[left[len(index)]])(lambda i: loops(index + (i,)))

        loops(())

    for p in range(len(parts)):
        start_reduce(p, 0)
    vec_sum = all_sum(place, small_sum, vec_buf, send, recv)
    vec_total = next(vec_sum)
    fill(head)

    ended = 0
    for step in REDUCE_PLAN:
        if step < 100:
            start_reduce(step // 10, step % 10)
            continue
        end_reduce(step // 10 % 10, step % 10)
        ended += 1
        if vec_total is None and ended in (12, 18):
            vec_total = next(vec_sum)
    while vec_total is None:
        vec_total = next(vec_sum)
    part_square = jnp.zeros((8, 128), f32)
    for i in range(per):
        piece = owned[i]
        part_square = part_square + jnp.sum((piece * piece).reshape(16, 8, 128), axis=0)
    sq_sum = all_sum(place, part_square, sq_buf, send, recv)
    total = next(sq_sum)
    stores[0].start()
    for i in range(per):
        grad = owned[i]
        gram_left[i] = lax.dot_general(grad, grad, (((1,), (1,)), ((), ())), precision=highest, preferred_element_type=f32)
        turned = jnp.transpose(grad)
        gram_right[i] = jnp.dot(turned, grad, precision=highest, preferred_element_type=f32)
    stores[1].start()
    stores[2].start()
    while total is None:
        total = next(sq_sum)

    grads4 = vec_total[0:4]
    bias_total = vec_total[5:6, 0 : 2 * HEADS]
    square = jnp.sum(total) + jnp.sum(grads4 * grads4) + jnp.sum(bias_total * bias_total)
    grad_norm = jnp.sqrt(jnp.broadcast_to(square, (8, 128)))
    factor = jnp.minimum(1.0, clip_limit / grad_norm)
    loss_out[0, 0] = vec_total[4, 0]
    norm_out[0, 0] = jnp.max(grad_norm)
    factor_out[0, 0] = jnp.max(factor)
    small_out[...] = vec_total
    for copy in stores:
        copy.wait()
    for copy in outgoing:
        copy.wait_send()


def update_kernel(
    factor_ref, small, vectors, vector_first, vector_second, var_bias, bias_first, bias_second, *rest,
):
    sources, rest = rest[:8], rest[8:]
    clipped_out, left_out, right_out, master_out = rest[:4]
    vector_grads, vector_second_new, vector_new, bias_grads, bias_second_new, bias_new = rest[4:10]
    held, made, in_sem, out_sem = rest[10:]
    fetches = [pltpu.make_async_copy(ref, held.at[k], in_sem.at[k]) for k, ref in enumerate(sources)]
    for copy in fetches:
        copy.start()
    owned, left_root, right_root, gram_left, left, gram_right, right, master = (held.at[k] for k in range(8))
    sends = [
        pltpu.make_async_copy(made.at[k], ref, out_sem.at[k])
        for k, ref in enumerate((clipped_out, left_out, right_out, master_out))
    ]
    factor = factor_ref[0, 0]
    per = owned.shape[0]
    fetches[0].wait()
    fetches[1].wait()
    grads = [owned[i] * factor for i in range(per)]
    for i in range(per):
        made[0, i] = grads[i]
    sends[0].start()
    shaped = [jnp.dot(left_root[i], grads[i], precision=highest, preferred_element_type=f32) for i in range(per)]
    fetches[2].wait()
    shaped = [jnp.dot(shaped[i], right_root[i], precision=highest, preferred_element_type=f32) for i in range(per)]
    for copy in fetches[3:]:
        copy.wait()
    for k, (stat, gram) in enumerate(((left, gram_left), (right, gram_right))):
        for i in range(per):
            scaled = jnp.where(factor > 0.0, gram[i] * factor * factor, 0.0)
            made[1 + k, i] = stat_beta * stat[i] + (1.0 - stat_beta) * scaled
        sends[1 + k].start()
    for i in range(per):
        unit = shaped[i] * lax.rsqrt(jnp.sum(shaped[i] * shaped[i]) / (SIDE * SIDE) + root_eps)
        made[3, i] = master[i] - mat_rate * (unit + decay_rate * master[i])
    sends[3].start()

    def adamw(gradient, first, second, old, grad_out, second_out, new_out):
        gradient = gradient * factor
        grad_out[...] = gradient
        first_next = beta_one * first[...] + (1.0 - beta_one) * gradient
        second_next = beta_two * second[...] + (1.0 - beta_two) * gradient * gradient
        ratio = first_next / (1.0 - beta_one**STEP) / (jnp.sqrt(second_next / (1.0 - beta_two**STEP)) + adam_eps)
        second_out[...] = second_next
        new_out[...] = old[...] - vec_rate * (ratio + decay_rate * old[...])

    adamw(small[0:4], vector_first, vector_second, vectors, vector_grads, vector_second_new, vector_new)
    adamw(small[5:6, 0 : 2 * HEADS], bias_first, bias_second, var_bias, bias_grads, bias_second_new, bias_new)
    for copy in sends:
        copy.wait()


def update_call(factor, small, owned, gram_left, gram_right, master, left, right, left_root, right_root, *rest):
    vmem, hbm = pl.BlockSpec(memory_space=pltpu.VMEM), pl.BlockSpec(memory_space=pl.ANY)
    sources = (owned, left_root, right_root, gram_left, left, gram_right, right, master)
    vectors, var_bias = rest[0], rest[3]
    outs = [master] * 4 + [vectors] * 3 + [var_bias] * 3
    return pl.pallas_call(
        update_kernel,
        out_shape=tuple(jax.ShapeDtypeStruct(a.shape, f32) for a in outs),
        in_specs=[pl.BlockSpec(memory_space=pltpu.SMEM)] + [vmem] * (1 + len(rest)) + [hbm] * 8,
        out_specs=(hbm,) * 4 + (vmem,) * 6,
        scratch_shapes=[
            pltpu.VMEM((8,) + master.shape, f32),
            pltpu.VMEM((4,) + master.shape, f32),
            pltpu.SemaphoreType.DMA((8,)),
            pltpu.SemaphoreType.DMA((4,)),
        ],
        compiler_params=pltpu.CompilerParams(vmem_limit_bytes=60 * 2**20),
        name="update",
    )(factor, small, *rest, *sources)


def step_call(dims, slots, lengths, bias, master, patches, sizes, times, predict, variates, vectors):
    freq = (10000.0 ** (-np.arange(HEAD_DIM // 2) / (HEAD_DIM // 2))).astype(np.float32)
    freq = jnp.asarray(np.tile(freq[None], (8, 4)))
    per = master.shape[0]
    places = np.stack(np.unravel_index(np.arange(2 * math.prod(dims) * per), (2, *dims, per))).astype(np.int32)
    half = patches.shape[2]
    received, sent = semaphores(dims)
    lanes = -(-2 * math.prod(dims) * per // 128) * 128
    smem = pl.BlockSpec(memory_space=pltpu.SMEM)
    vmem = pl.BlockSpec(memory_space=pltpu.VMEM)
    sems = pltpu.SemaphoreType.DMA
    landing = []
    for axes, _, n in cut_parts(REDUCE_PARTS):
        for k in range(3):
            wide = [dims[i] for i in sorted(axes[k + 1 :])]
            landing.append(pltpu.VMEM((max(dims[axes[k]] - 1, 1), *wide, per, n, SIDE), bf16))
    hbm = pl.BlockSpec(memory_space=pl.ANY)
    sources = (master, patches, sizes, times, predict, variates, vectors, freq, jnp.asarray(group_order(), bf16))
    return pl.pallas_call(
        functools.partial(step_kernel, dims),
        out_shape=tuple(
            jax.ShapeDtypeStruct(shape, f32)
            for shape in [(1, 1)] * 4 + [(8, D)] + [(per, SIDE, SIDE)] * 3
        ),
        in_specs=[smem] * 4 + [hbm] * 9,
        out_specs=(smem,) * 4 + (vmem,) + (hbm,) * 3,
        scratch_shapes=[pltpu.VMEM(a.shape, a.dtype) for a in sources]
        + [pltpu.VMEM((per, SIDE, SIDE), f32)] * 3
        + [sems((len(sources),)), sems((3,))]
        + [pltpu.VMEM((1, lanes), jnp.int32), pltpu.SMEM((1, lanes), jnp.int32), sems]
        + [pltpu.VMEM(shape, dtype) for shape, dtype in SCRATCH.values()]
        + [
            pltpu.VMEM((per, SIDE, SIDE), bf16),
            pltpu.VMEM((2,) + dims + (per, SIDE, SIDE), bf16),
            pltpu.VMEM(dims + (per, SIDE, SIDE), bf16),
            pltpu.VMEM((half, PMAX), bf16),
            pltpu.VMEM((3, 2, half), jnp.int32),
            pltpu.VMEM((3, 2, half), jnp.int32),
            sum_shape(dims, (8, 128)),
            sum_shape(dims, (8, D)),
            sum_shape(dims, (8, 128)),
            sems,
            sems((sent,)),
            sems((received,)),
            *landing,
        ],
        compiler_params=pltpu.CompilerParams(
            collective_id=0, has_side_effects=True, vmem_limit_bytes=63 * 2**20
        ),
        name="step",
    )(slots, jnp.asarray(places), lengths, bias, *sources)


def shards(
    dims,
    patches, patch_sizes, sample_lengths, variate_ids, time_ids, predict_mask, block_owner_slot,
    master_blocks, left_stats, right_stats, left_roots, right_roots,
    vectors, vector_first, vector_second, var_bias, bias_first, bias_second,
):
    loss_sum, count, grad_norm, factor, small, owned, gram_left, gram_right = step_call(
        dims, block_owner_slot, sample_lengths, var_bias[0], master_blocks, patches, patch_sizes, time_ids,
        predict_mask, variate_ids, vectors,
    )
    outs = update_call(
        factor, small, owned, gram_left, gram_right, master_blocks, left_stats, right_stats, left_roots, right_roots,
        vectors, vector_first, vector_second, var_bias, bias_first, bias_second,
    )
    return (loss_sum.reshape(()), count.reshape(()), grad_norm.reshape(())) + tuple(outs)


def solution(mesh):
    rep = P()
    dims = tok_dims(mesh.shape["tok"])
    slot = P(("head", "tok"), None, None)
    return jax.shard_map(
        functools.partial(shards, dims),
        mesh=mesh,
        in_specs=(
            P(None, "tok", "head", None), P(None, "tok", "head"), P(None, "tok", None), P(None, "tok", None),
            P(None, "tok", "head"), P(None, "tok", "head"), rep, slot, slot, slot, slot, slot,
            rep, rep, rep, rep, rep, rep,
        ),
        out_specs=(rep, rep, rep, slot, slot, slot, slot, rep, rep, rep, rep, rep, rep),
        check_vma=False,
    )
```

```python
import functools
import itertools
import math

import jax
import jax.numpy as jnp
import numpy as np
from jax import lax
from jax.experimental import pallas as pl
from jax.experimental.pallas import tpu as pltpu
from jax.sharding import PartitionSpec as P

D = 384
FF = 1024
HEADS = 6
HEAD_DIM = 64
PSIZES = 5
PMAX = 128
COMPS = 4
SEQ = 512
SIDE = 128
STEP = 10
HEADCOLS = 3 * COMPS * PMAX
BLOCKS = 159

norm_eps = 1e-06
scale_floor = 0.05
half_log_tau = 0.9189385332046727
clip_limit = 0.02
mat_rate = 0.01
vec_rate = 0.3
decay_rate = 0.01
beta_one = 0.9
beta_two = 0.95
stat_beta = 0.99
root_eps = 1e-06
adam_eps = 1e-08
highest = lax.Precision.HIGHEST
f32 = jnp.float32
bf16 = jnp.bfloat16

GRIDS = ((5, 3), (3, 12), (3, 9), (3, 3), (3, 16), (8, 3))
FIRSTS = (0, 15, 51, 78, 87, 135)
M_IN, M_HEAD, M_QKV, M_OUT, M_GU, M_DOWN = range(6)


def mm(a, b):
    return jnp.dot(a, b, preferred_element_type=f32)


def mm_nt(a, b):
    return lax.dot_general(a, b, (((1,), (1,)), ((), ())), preferred_element_type=f32)


def mm_tn(a, b):
    return lax.dot_general(a, b, (((0,), (0,)), ((), ())), preferred_element_type=f32)


GROUP = 384


def group_order():
    order = np.zeros((GROUP, GROUP), np.float32)
    for col in range(GROUP):
        order[col, (col % 12) * 32 + col // 12] = 1.0
    return order


def swap_quarters(parts):
    lane = lax.broadcasted_iota(jnp.int32, (1, 128), 1)
    low, even = lane < 64, lane % 64 < 32
    a, b, c, d = parts
    a, c = jnp.where(low, a, pltpu.roll(c, 64, 1)), jnp.where(low, pltpu.roll(a, 64, 1), c)
    b, d = jnp.where(low, b, pltpu.roll(d, 64, 1)), jnp.where(low, pltpu.roll(b, 64, 1), d)
    a, b = jnp.where(even, a, pltpu.roll(b, 32, 1)), jnp.where(even, pltpu.roll(a, 96, 1), b)
    c, d = jnp.where(even, c, pltpu.roll(d, 32, 1)), jnp.where(even, pltpu.roll(c, 96, 1), d)
    return a, b, c, d


SCRATCH = dict(
    w_in=((640, D), bf16), w_head=((D, HEADCOLS), bf16), w_qkv=((D, 3 * D), bf16), w_out=((D, D), bf16),
    w_gu=((D, 2 * FF), bf16), w_down=((FF, D), bf16), w_headp=((D, HEADCOLS), bf16),
    blocks=((BLOCKS + 1, SIDE, SIDE), bf16),
    x5=((SEQ, 640), bf16), weight=((SEQ, PMAX), f32), flag=((SEQ, 128), f32),
    cos_t=((SEQ, 128), f32), sin_t=((SEQ, 128), f32),
    code_t=((SEQ, SEQ), f32), probs=((HEADS, SEQ, SEQ), f32),
    stream=((SEQ, D), f32), middle=((SEQ, D), f32), last=((SEQ, D), f32), grad=((SEQ, D), f32), inner=((SEQ, D), f32),
    inv_a=((SEQ, 128), f32), inv_b=((SEQ, 128), f32), inv_f=((SEQ, 128), f32),
    normed=((SEQ, D), bf16), na_t=((D, SEQ), bf16), nb_t=((D, SEQ), bf16), nf_t=((D, SEQ), bf16),
    qs=((SEQ, D), bf16), ks=((SEQ, D), bf16), vs=((SEQ, D), bf16), merged=((SEQ, D), bf16), merged_t=((D, SEQ), bf16),
    silu=((SEQ, FF), f32), slope=((SEQ, FF), f32), hidden=((SEQ, FF), bf16),
    params=((SEQ, HEADCOLS), f32), gparams=((SEQ, HEADCOLS), bf16), ggu=((SEQ, 2 * FF), bf16),
    loss_acc=((32, 128), f32), bias_acc=((16, 128), f32), vec_acc=((8, D), f32),
    meta=((8, SEQ), jnp.int32), row_patches=((SEQ, PMAX), bf16),
)


def tile(i, size):
    return pl.ds(pl.multiple_of(i * size, size), size)


MESH = pl.DeviceIdType.MESH


def tok_dims(count):
    return {16: (4, 2, 2), 128: (4, 4, 8)}.get(count, (count, 1, 1))


class Place:
    def __init__(self, dims):
        self.dims = dims
        self.head = lax.axis_index("head")
        tok = lax.axis_index("tok")
        self.tok = tok
        self.strides = (dims[1] * dims[2], dims[2], 1)
        self.at = [lax.rem(lax.div(tok, s), n) for s, n in zip(self.strides, dims)]

    def coordinate(self, axis, step):
        return lax.rem(self.at[axis] + step, self.dims[axis])

    def peer(self, axis, step):
        return (self.head, self.tok + (self.coordinate(axis, step) - self.at[axis]) * self.strides[axis])

    def partner(self):
        return (1 - self.head, self.tok)

    def groups(self):
        result, size = [[None]], 2
        for axis in (1, 2, 0):
            if self.dims[axis] == 1:
                continue
            if size * self.dims[axis] > 8:
                result.append([])
                size = 1
            result[-1].append(axis)
            size *= self.dims[axis]
        return result

    def members(self, group):
        sizes = [2 if axis is None else self.dims[axis] for axis in group]
        mine = 0
        for axis, n in zip(group, sizes):
            mine = mine * n + (self.head if axis is None else self.at[axis])
        others = []
        for steps in itertools.product(*[range(n) for n in sizes]):
            head, tok = self.head, self.tok
            for axis, step in zip(group, steps):
                if axis is None:
                    head = lax.rem(head + step, 2)
                else:
                    tok = tok + (self.coordinate(axis, step) - self.at[axis]) * self.strides[axis]
            if any(steps):
                others.append((head, tok))
        return mine, math.prod(sizes), others

    def greet(self, meanwhile):
        barrier = pltpu.get_barrier_semaphore()
        groups = self.groups()
        others = [other for group in groups for other in self.members(group)[2]]
        joint = [group for group in groups if len(group) > 1]
        singles = {group[0] for group in groups if len(group) == 1} | {a for group in joint for a in group}
        others += [self.peer(a, j) for a in range(3) if a not in singles for j in range(1, self.dims[a])]
        for other in others:
            pl.semaphore_signal(barrier, inc=1, device_id=other, device_id_type=MESH)
        meanwhile()
        pl.semaphore_wait(barrier, len(others))

    def region(self, whole, fixed=None):
        fixed = fixed or {}
        return tuple(slice(None) if a in whole else fixed.get(a, self.at[a]) for a in range(3))


def remote(src, dst, send, recv, device):
    return pltpu.make_async_remote_copy(
        src_ref=src, dst_ref=dst, send_sem=send, recv_sem=recv, device_id=device, device_id_type=MESH
    )


def split_rows(rows, shares):
    units = rows // 16
    edges = [round(units * sum(shares[:i]) / sum(shares)) * 16 for i in range(len(shares) + 1)]
    return [(a, b - a) for a, b in zip(edges, edges[1:])]


class Pool:
    def __init__(self, ref):
        self.ref, self.used = ref, 0

    def __call__(self):
        self.used += 1
        return self.ref.at[self.used - 1]


def all_sum(place, values, buf, send, recv):
    total = values
    for k, group in enumerate(place.groups()):
        mine, size, others = place.members(group)
        buf[k, mine] = total
        copies = [remote(buf.at[k, mine], buf.at[k, mine], send(), recv(), other) for other in others]
        for copy in copies:
            copy.start()
        yield None
        for copy in copies:
            copy.wait()
        total = buf[k, 0]
        for i in range(1, size):
            total = total + buf[k, i]
    yield total


def sum_sizes(dims):
    place = Place.__new__(Place)
    place.dims = dims
    return [math.prod(2 if a is None else dims[a] for a in group) for group in place.groups()]


def sum_shape(dims, shape):
    sizes = sum_sizes(dims)
    return pltpu.VMEM((len(sizes), max(sizes)) + shape, f32)


GATHER_PARTS = (
    ((1, 2, 0), 1), ((0, 1, 2), 1), ((0, 2, 1), 1), ((0, 1, 2), 1), ((0, 1, 2), 1), ((0, 2, 1), 1), ((1, 0, 2), 1), ((2, 0, 1), 1),
)
PREPARE_AFTER = 4
GATHER_PLAN = (
    0, 10, 20, 60, 100, 1, 30, 70, 110, 11, 50, 120, 21, 130, 31, 40, 111, 12, 160, 61, 150, 51, 170, 71,
    121, 22, 140, 41, 131, 32, 141, 42, 151, 52, 101, 2, 122, 171, 72, 112, 161, 62, 172, 132, 142, 102, 152, 162,
)
REDUCE_PARTS = (
    ((2, 0, 1), 1), ((0, 1, 2), 1), ((2, 1, 0), 1), ((1, 2, 0), 1), ((2, 1, 0), 1), ((1, 0, 2), 1), ((1, 2, 0), 1), ((2, 1, 0), 1),
)
REDUCE_PLAN = (
    100, 1, 110, 11, 120, 21, 130, 31, 140, 41, 150, 51, 101, 2, 111, 12, 131, 32, 160, 61, 121, 22, 170, 71,
    151, 52, 112, 13, 122, 23, 141, 42, 161, 62, 132, 33, 152, 53, 171, 72, 102, 3, 142, 43, 162, 63, 133, 172,
    73, 143, 163, 153, 113, 123, 103, 173,
)


def cut_parts(table):
    return [(order, a, n) for (order, _), (a, n) in zip(table, split_rows(SIDE, [s for _, s in table]))]


def semaphores(dims):
    steps = sum(n - 1 for n in dims)
    sums = sum(n - 1 for n in sum_sizes(dims))
    gather = sum(steps + 1 + sum(dims[a] - 1 for a in order[1:]) for order, _ in GATHER_PARTS) + 2 + sums
    reduce = len(REDUCE_PARTS) * (steps + 1) + 2 * sums
    return gather + reduce, max(gather, reduce)


def step_kernel(
    dims, *rest,
):
    sources, rest = rest[:13], rest[13:]
    loss_out, count_out, norm_out, small_out = rest[:4]
    results, rest = rest[4:7], rest[7:]
    held, rest = rest[:13], rest[13:]
    master, patches, sizes, times_in, predict_in, variates_in, vectors, freq, order, slots, places, lengths, bias = held
    (owned, gram_left, gram_right), rest = rest[:3], rest[3:]
    (fetch_sem, result_sem, holder_row, holder, holder_sem), rest = rest[:5], rest[5:]
    fetches = [pltpu.make_async_copy(a, b, fetch_sem.at[k]) for k, (a, b) in enumerate(zip(sources, held))]
    for copy in fetches:
        copy.start()
    stores = [
        pltpu.make_async_copy(a, b, result_sem.at[k]) for k, (a, b) in enumerate(zip((owned, gram_left, gram_right), results))
    ]
    names = list(SCRATCH)
    s = type("S", (), dict(zip(names, rest)))
    rest = rest[len(names) :]
    mine, gathered, crossed, land_patch, land_ints, own_ints = rest[:6]
    cnt_buf, vec_buf, sq_buf, own_sem, send_pool, recv_pool = rest[6:12]
    send, recv = Pool(send_pool), Pool(recv_pool)
    landing = rest[12:]
    place = Place(dims)
    per = mine.shape[0]
    head = place.head
    lane = lax.broadcasted_iota(jnp.int32, (1, 128), 1)
    first_half = lane % HEAD_DIM < HEAD_DIM // 2
    low_head = lane < HEAD_DIM
    weights = (s.w_in, s.w_head, s.w_qkv, s.w_out, s.w_gu, s.w_down)

    def keep(m, r0, c0, value):
        value = value.astype(bf16)
        cols = GRIDS[m][1]
        for r in range(value.shape[0] // SIDE):
            for c in range(value.shape[1] // SIDE):
                piece = value[r * SIDE : (r + 1) * SIDE, c * SIDE : (c + 1) * SIDE]
                s.blocks[FIRSTS[m] + (r0 + r) * cols + c0 + c] = piece

    half = SEQ // 2
    s.meta[4:8, :] = jnp.zeros((4, SEQ), jnp.int32)

    def local_work():
        for copy in fetches[:6]:
            copy.wait()
        mine[...] = master[...].astype(bf16)
        for k, ref in enumerate((sizes, times_in, predict_in)):
            own_ints[k, :, :] = ref[:, 0, :]
        for h in range(2):

            @pl.when(head == h)
            def _():
                here = slice(h * half, (h + 1) * half)
                s.row_patches[here, :] = patches[h, 0]
                for k, ref in enumerate((sizes, times_in, predict_in)):
                    s.meta[k : k + 1, here] = ref[h]
                s.meta[3:4, :] = variates_in[h]

    place.greet(local_work)
    swaps = [
        remote(patches.at[1 - head, 0], land_patch, send(), recv(), place.partner()),
        remote(own_ints, land_ints, send(), recv(), place.partner()),
    ]
    for copy in swaps:
        copy.start()
    parts = cut_parts(GATHER_PARTS)

    def block(head_index, whole, fixed, a, n):
        return gathered.at[(head_index,) + place.region(whole, fixed) + (slice(None), pl.ds(a, n))]

    arriving, outgoing, cross = {}, list(swaps), []
    own = pltpu.make_async_copy(mine, gathered.at[(head,) + place.region(())], own_sem)
    own.start()

    def start_gather(p, k):
        axes, a, n = parts[p]
        axis, whole = axes[k], axes[:k]
        arriving[p] = []
        for j in range(1, dims[axis]):
            src = mine.at[:, pl.ds(a, n)] if k == 0 else block(head, whole, None, a, n)
            copy = remote(src, block(head, whole, None, a, n), send(), recv(), place.peer(axis, j))
            copy.start()
            arriving[p].append(copy)
        outgoing.extend(arriving[p])

    def end_gather(p, k):
        axes, a, n = parts[p]
        for copy in arriving[p]:
            copy.wait_recv()
        axis, whole = axes[k], axes[:k]
        if k == 0:
            views = [block(head, axes[:1], None, a, n)]
        else:
            views = [
                block(head, whole, {axis: place.coordinate(axis, dims[axis] - j)}, a, n) for j in range(1, dims[axis])
            ]
        for view in views:
            copy = remote(view, view, send(), recv(), place.partner())
            copy.start()
            cross.append(copy)

    first = next(i for i, step in enumerate(GATHER_PLAN) if step >= 100)
    for step in GATHER_PLAN[:first]:
        start_gather(step // 10, step % 10)
    wide_size = jnp.zeros_like(own_ints[0])
    for c in range(PSIZES):
        wide_size = wide_size + jnp.where(own_ints[0] == c, PMAX * 2**c // 2 ** (PSIZES - 1), 0)
    partial = (wide_size * own_ints[2]).astype(f32)
    partial = jnp.sum(partial[:, :128] + partial[:, 128:], axis=0, keepdims=True)
    counting = all_sum(place, jnp.concatenate([partial, jnp.zeros((7, 128), f32)], axis=0), cnt_buf, send, recv)
    counted = next(counting)
    own.wait()
    for copy in swaps:
        copy.wait_recv()
    for h in range(2):

        @pl.when(head == h)
        def _():
            there = slice((1 - h) * half, (2 - h) * half)
            s.row_patches[there, :] = land_patch[...]
            for k in range(3):
                s.meta[k : k + 1, there] = land_ints[k, h : h + 1, :]

    def prepare_holder():
        position = lax.broadcasted_iota(jnp.int32, holder_row.shape, 1)

        def body(b, row):
            return jnp.where(position == slots[b], b, row)

        holder_row[...] = lax.fori_loop(0, BLOCKS, body, jnp.full(holder_row.shape, BLOCKS, jnp.int32), unroll=3)
        copy = pltpu.make_async_copy(holder_row, holder, holder_sem)
        copy.start()
        copy.wait()

    def prepare_tokens():
        for copy in fetches[6:]:
            copy.wait()
        metaf = s.meta[...].astype(f32)
        columns = jnp.transpose(metaf)
        codes, times, flag = columns[:, 0:1], columns[:, 1:2], columns[:, 2:3]
        position = lax.broadcasted_iota(jnp.int32, (1, SEQ), 1)
        ids = jnp.zeros((1, SEQ), f32)
        end = jnp.int32(0)
        for j in range(lengths.shape[2]):
            end = end + lengths[head, 0, j]
            ids = ids + jnp.where(position >= end, 1.0, 0.0)
        variates = metaf[3:4]
        id_columns = jnp.transpose(jnp.concatenate([ids] * 8, axis=0))[:, 0:1]
        var_columns = columns[:, 3:4]
        for c in range(4):
            cs = slice(c * 128, (c + 1) * 128)
            same_sample = id_columns == ids[:, cs]
            same_var = var_columns == variates[:, cs]
            s.code_t[:, cs] = jnp.where(same_sample, jnp.where(same_var, 2.0, 1.0), 0.0)
        s.flag[...] = jnp.broadcast_to(flag, (SEQ, 128))
        angle = times * freq[0:1, :]
        s.cos_t[...] = jnp.cos(angle)
        s.sin_t[...] = jnp.where(first_half, -1.0, 1.0) * jnp.sin(angle)

        wide = s.row_patches[...].astype(f32)
        weight = jnp.zeros((SEQ, PMAX), f32)
        for c in range(PSIZES):
            keep = (codes == float(c)) & (lane < PMAX * 2**c // 2 ** (PSIZES - 1))
            s.x5[:, c * 128 : (c + 1) * 128] = jnp.where(keep, wide, 0.0).astype(bf16)
            weight = jnp.where(keep, 1.0, weight)
        s.weight[...] = jnp.where(flag == 1.0, weight, 0.0)
    ended = 0
    for step in GATHER_PLAN[first:]:
        if step < 100:
            start_gather(step // 10, step % 10)
            continue
        end_gather(step // 10 % 10, step % 10)
        ended += 1
        if counted is None and ended in (4, 8):
            counted = next(counting)
        if ended == PREPARE_AFTER:
            prepare_tokens()
        if ended == PREPARE_AFTER + 3:
            prepare_holder()
    while counted is None:
        counted = next(counting)
    value_count = jnp.sum(counted)
    count_out[0, 0] = value_count
    for copy in cross:
        copy.wait_recv()

    def load(m):
        n_rows, cols = GRIDS[m]

        @pl.loop(0, n_rows)
        def _(r):
            for c in range(cols):
                slot = slots[FIRSTS[m] + r * cols + c]
                where = tuple(places[k, slot] for k in range(5))
                weights[m][tile(r, SIDE), c * SIDE : (c + 1) * SIDE] = gathered[where]

    for m in range(6):
        load(m)

    def turn(v, sine):
        swapped = jnp.where(first_half, pltpu.roll(v, 96, 1), pltpu.roll(v, 32, 1))
        return v * s.cos_t[...] + swapped * sine

    embedded = mm(s.x5[...], s.w_in[...])
    for c in range(3):
        cs = slice(c * 128, (c + 1) * 128)
        s.stream[:, cs] = jnp.where(s.flag[...] == 1.0, vectors[3:4, cs], embedded[:, cs])

    def norm(src, inv_ref, gain, dst_t):
        @pl.loop(0, SEQ // 128)
        def _(i):
            rs = tile(i, 128)
            v = src[rs, :]
            inverse = lax.rsqrt(jnp.sum(v * v, axis=-1, keepdims=True) / D + norm_eps)
            inv_ref[rs, :] = jnp.broadcast_to(inverse, (128, 128))
            s.normed[rs, :] = (v * inverse * gain).astype(bf16)

        dst_t[...] = jnp.transpose(s.normed[...])

    def norm_back(src, inv_ref, row, extra):
        gain = vectors[row : row + 1, :]

        @pl.loop(0, SEQ // 128)
        def _(i):
            rs = tile(i, 128)
            up = s.inner[rs, :]
            inverse = inv_ref[rs, 0:1]
            scaled = src[rs, :] * inverse
            inner = up * gain
            mean = jnp.sum(inner * scaled, axis=-1, keepdims=True) / D
            result = inverse * (inner - scaled * mean)
            s.grad[rs, :] = result if extra is None else result + extra[rs, :]
            s.vec_acc[row : row + 1, :] += jnp.sum(up * scaled, axis=0, keepdims=True)

    s.vec_acc[...] = jnp.zeros_like(s.vec_acc)
    norm(s.stream, s.inv_a, vectors[0:1, :], s.na_t)
    mixed = mm(s.normed[...], s.w_qkv[...])
    for part, dst in ((0, s.qs), (1, s.ks), (2, s.vs)):
        for c in range(3):
            piece = mixed[:, part * D + c * 128 : part * D + (c + 1) * 128]
            if part < 2:
                piece = turn(piece, s.sin_t[...])
            dst[:, c * 128 : (c + 1) * 128] = piece.astype(bf16)

    @pl.loop(0, HEADS // 2)
    def _(p):
        ps = tile(p, 128)
        qp, kp = s.qs[:, ps], s.ks[:, ps]
        vt = jnp.transpose(s.vs[:, ps])
        outs = []
        for hh in range(2):
            mine = low_head if hh == 0 else jnp.logical_not(low_head)
            qm = jnp.where(mine, qp.astype(f32) * HEAD_DIM**-0.5, 0.0).astype(bf16)
            b0 = bias[2 * p + hh]
            b1 = bias[HEADS + 2 * p + hh]
            parts = []
            for c in range(1):
                cs = slice(c * 512, (c + 1) * 512)
                code = s.code_t[:, cs]
                score = mm_nt(kp, qm[cs, :])
                score = jnp.where(code > 0.5, score + jnp.where(code > 1.5, b0, b1), -1e30)
                raised = jnp.exp(score - jnp.max(score, axis=0, keepdims=True))
                prob = raised * (1.0 / jnp.sum(raised, axis=0, keepdims=True))
                s.probs[2 * p + hh, :, cs] = prob
                parts.append(mm(vt[hh * 64 : (hh + 1) * 64, :], prob.astype(bf16)))
            outs.append(jnp.concatenate(parts, axis=1))
        out_t = jnp.concatenate(outs, axis=0).astype(bf16)
        s.merged_t[ps, :] = out_t
        s.merged[:, ps] = jnp.transpose(out_t)

    s.middle[...] = s.stream[...] + mm(s.merged[...], s.w_out[...])
    norm(s.middle, s.inv_b, vectors[1:2, :], s.nb_t)

    @pl.loop(0, FF // 1024)
    def _(j):
        js = tile(j, 1024)
        opening = mm(s.normed[...], s.w_gu[:, js])
        up = mm(s.normed[...], s.w_gu[:, tile(j + FF // 1024, 1024)])
        sigma = 1.0 / (1.0 + jnp.exp(-opening))
        silu = opening * sigma
        s.silu[:, js] = silu
        s.slope[:, js] = up * sigma * (1.0 + opening * (1.0 - sigma))
        s.hidden[:, js] = (silu * up).astype(bf16)

    s.last[...] = s.middle[...] + mm(s.hidden[...], s.w_down[...])
    norm(s.last, s.inv_f, vectors[2:3, :], s.nf_t)


    wide = [mm(s.w_head[:, g * GROUP : (g + 1) * GROUP], order[...]) for g in range(4)]
    for kind in range(3):
        pieces = swap_quarters([w[:, kind * 128 : (kind + 1) * 128] for w in wide])
        for k, piece in enumerate(pieces):
            at = (4 * kind + k) * 128
            s.w_headp[:, at : at + 128] = piece.astype(bf16)

    @pl.loop(0, HEADCOLS // 512)
    def _(j):
        js = tile(j, 512)
        s.params[:, js] = mm(s.normed[...], s.w_headp[:, js])

    inv_n = 1.0 / value_count
    s.loss_acc[...] = jnp.zeros_like(s.loss_acc)

    @pl.loop(0, SEQ // 32)
    def _(i):
        rs = tile(i, 32)
        y = s.row_patches[rs, :].astype(f32)
        weight = s.weight[rs, :]
        logits, means, raws = [
            [s.params[rs, (4 * kind + k) * 128 : (4 * kind + k + 1) * 128] for k in range(COMPS)] for kind in range(3)
        ]
        top = jnp.maximum(jnp.maximum(logits[0], logits[1]), jnp.maximum(logits[2], logits[3]))
        shifted = [v - top for v in logits]
        raised = [jnp.exp(v) for v in shifted]
        total = raised[0] + raised[1] + raised[2] + raised[3]
        log_total = jnp.log(total)
        inv_total = 1.0 / total
        terms, zs, inv_widths = [], [], []
        for k in range(COMPS):
            width = jnp.maximum(raws[k], 0.0) + jnp.log1p(jnp.exp(-jnp.abs(raws[k]))) + scale_floor
            inv_width = 1.0 / width
            z = (y - means[k]) * inv_width
            terms.append((shifted[k] - log_total) - 0.5 * z * z - jnp.log(width) - half_log_tau)
            zs.append(z)
            inv_widths.append(inv_width)
        best = jnp.maximum(jnp.maximum(terms[0], terms[1]), jnp.maximum(terms[2], terms[3]))
        lifted = [jnp.exp(t - best) for t in terms]
        lift_total = lifted[0] + lifted[1] + lifted[2] + lifted[3]
        inv_lift = 1.0 / lift_total
        s.loss_acc[...] += jnp.where(weight > 0.0, -(best + jnp.log(lift_total)), 0.0)
        scale = -(weight * inv_n)
        for k in range(COMPS):
            share = lifted[k] * inv_lift
            d_term = scale * share
            ratio = zs[k] * inv_widths[k]
            d_logit = scale * (share - raised[k] * inv_total)
            d_width = d_term * (zs[k] * ratio - inv_widths[k])
            sigma = 1.0 / (1.0 + jnp.exp(-raws[k]))
            for kind, value in ((0, d_logit), (1, d_term * ratio), (2, d_width * sigma)):
                at = (4 * kind + k) * 128
                s.gparams[rs, at : at + 128] = value.astype(bf16)

    for kind in range(3):
        ks = slice(kind * 512, (kind + 1) * 512)
        wide = mm(s.nf_t[...], s.gparams[:, ks])
        pieces = swap_quarters([wide[:, k * 128 : (k + 1) * 128] for k in range(4)])
        for g in range(4):
            s.w_head[:, (3 * g + kind) * 128 : (3 * g + kind + 1) * 128] = pieces[g].astype(bf16)
    for g in range(4):
        gs = slice(g * GROUP, (g + 1) * GROUP)
        keep(M_HEAD, 0, 3 * g, mm_nt(s.w_head[:, gs], order[...]))
    s.inner[...] = mm_nt(s.gparams[...], s.w_headp[...])
    norm_back(s.last, s.inv_f, 2, None)

    s.normed[...] = s.grad[...].astype(bf16)

    @pl.loop(0, FF // 1024)
    def _(j):
        js = tile(j, 1024)
        keep(M_DOWN, 8 * j, 0, mm_tn(s.hidden[:, js], s.normed[...]))
        up_grad = mm_nt(s.normed[...], s.w_down[js, :])
        s.ggu[:, js] = (up_grad * s.slope[:, js]).astype(bf16)
        s.ggu[:, tile(j + FF // 1024, 1024)] = (up_grad * s.silu[:, js]).astype(bf16)

    @pl.loop(0, 2 * FF // 512)
    def _(j):
        keep(M_GU, 0, 4 * j, mm(s.nb_t[...], s.ggu[:, tile(j, 512)]))

    s.inner[...] = mm_nt(s.ggu[...], s.w_gu[...])
    norm_back(s.middle, s.inv_b, 1, s.grad)

    s.normed[...] = s.grad[...].astype(bf16)
    keep(M_OUT, 0, 0, mm(s.merged_t[...], s.normed[...]))
    s.merged[...] = mm_nt(s.normed[...], s.w_out[...]).astype(bf16)
    s.bias_acc[...] = jnp.zeros_like(s.bias_acc)

    @pl.loop(0, HEADS // 2)
    def _(p):
        ps = tile(p, 128)
        qp, kp, vp, dop = s.qs[:, ps], s.ks[:, ps], s.vs[:, ps], s.merged[:, ps]
        kt = jnp.transpose(kp)
        dq, dk, dv = [], [], []
        for hh in range(2):
            mine = low_head if hh == 0 else jnp.logical_not(low_head)
            dom = jnp.where(mine, dop.astype(f32), 0.0).astype(bf16)
            same_sum = jnp.zeros((1, 256), f32)
            all_sum = jnp.zeros((1, 256), f32)
            for c in range(2):
                cs = slice(c * 256, (c + 1) * 256)
                prob = s.probs[2 * p + hh, :, cs]
                d_prob = mm_nt(vp, dom[cs, :])
                d_score = prob * (d_prob - jnp.sum(prob * d_prob, axis=0, keepdims=True))
                same_sum += jnp.sum(jnp.where(s.code_t[:, cs] > 1.5, d_score, 0.0), axis=0, keepdims=True)
                all_sum += jnp.sum(d_score, axis=0, keepdims=True)
                s.ggu[:, hh * SEQ + c * 256 : hh * SEQ + (c + 1) * 256] = (d_score * HEAD_DIM**-0.5).astype(bf16)
            s.bias_acc[pl.ds(2 * p + hh, 1), :] = same_sum[:, :128] + same_sum[:, 128:]
            s.bias_acc[pl.ds(8 + 2 * p + hh, 1), :] = all_sum[:, :128] + all_sum[:, 128:]
            dv.append(mm(s.probs[2 * p + hh].astype(bf16), dop))
            dk.append(mm(s.ggu[:, hh * SEQ : (hh + 1) * SEQ], qp))
            dq.append(mm(kt[hh * 64 : (hh + 1) * 64, :], s.ggu[:, hh * SEQ : (hh + 1) * SEQ]))
        dqs = jnp.transpose(jnp.concatenate(dq, axis=0)).astype(bf16).astype(f32)
        dks = jnp.where(low_head, dk[0], dk[1]).astype(bf16).astype(f32)
        s.gparams[:, ps] = turn(dqs, -s.sin_t[...]).astype(bf16)
        s.gparams[:, tile(p + 3, 128)] = turn(dks, -s.sin_t[...]).astype(bf16)
        s.gparams[:, tile(p + 6, 128)] = jnp.where(low_head, dv[0], dv[1]).astype(bf16)

    keep(M_QKV, 0, 0, mm(s.na_t[...], s.gparams[:, : 3 * D]))
    s.inner[...] = mm_nt(s.gparams[:, : 3 * D], s.w_qkv[...])
    norm_back(s.stream, s.inv_a, 0, s.grad)
    for c in range(3):
        cs = slice(c * 128, (c + 1) * 128)
        hidden_token = s.flag[...] == 1.0
        s.vec_acc[3:4, cs] = jnp.sum(jnp.where(hidden_token, s.grad[:, cs], 0.0), axis=0, keepdims=True)
        s.normed[:, cs] = jnp.where(hidden_token, 0.0, s.grad[:, cs]).astype(bf16)
    keep(M_IN, 0, 0, mm_tn(s.x5[...], s.normed[...]))

    sums = jnp.sum(s.bias_acc[...], axis=1, keepdims=True)
    sums = jnp.concatenate([sums[0:8], sums[8:16] - sums[0:8]], axis=0)
    entry = lax.broadcasted_iota(jnp.int32, (16, D), 0)
    target = jnp.where(entry < HEADS, entry, jnp.where((entry >= 8) & (entry < 8 + HEADS), entry - 8 + HEADS, -1))
    bias_row = jnp.sum(
        jnp.where(target == lax.broadcasted_iota(jnp.int32, (16, D), 1), sums, 0.0), axis=0, keepdims=True
    )
    row = lax.broadcasted_iota(jnp.int32, (8, D), 0)
    small_sum = jnp.where(row == 4, jnp.sum(s.loss_acc[...]), jnp.where(row == 5, bias_row, s.vec_acc[...]))
    for copy in outgoing + cross:
        copy.wait_send()
    send = Pool(send_pool)
    s.blocks[BLOCKS] = jnp.zeros((SIDE, SIDE), bf16)
    toks = dims[0] * dims[1] * dims[2]

    def fill(h):
        @pl.loop(0, toks)
        def _(t):
            for i in range(per):
                at = (h, t // (dims[1] * dims[2]), t // dims[2] % dims[1], t % dims[2], i)
                gathered[at] = s.blocks[holder[0, (h * toks + t) * per + i]]

    everywhere = (slice(None),) * 3
    parts = cut_parts(REDUCE_PARTS)
    fill(1 - head)
    arriving, outgoing = {}, []

    def start_reduce(p, k):
        axes, a, n = parts[p]
        if k == 0:
            view = everywhere + (slice(None), pl.ds(a, n))
            copies = [remote(gathered.at[(1 - head,) + view], crossed.at[view], send(), recv(), place.partner())]
        else:
            axis, left = axes[k - 1], axes[k:]
            copies = []
            for j in range(1, dims[axis]):
                region = place.region(left, {axis: place.coordinate(axis, j)})
                src = gathered.at[(head,) + region + (slice(None), pl.ds(a, n))]
                copies.append(remote(src, landing[3 * p + k - 1].at[j - 1], send(), recv(), place.peer(axis, j)))
        for copy in copies:
            copy.start()
        arriving[p] = copies
        outgoing.extend(copies)

    def end_reduce(p, k):
        axes, a, n = parts[p]
        left = sorted(axes[k:])
        region = place.region(left)
        for copy in arriving[p]:
            copy.wait_recv()

        def body(*index):
            at = tuple(index[left.index(i)] if i in left else region[i] for i in range(3)) + (slice(None), pl.ds(a, n))
            value = gathered[(head,) + at].astype(f32)
            if k == 0:
                value = value + crossed[at].astype(f32)
            else:
                for j in range(1, dims[axes[k - 1]]):
                    value = value + landing[3 * p + k - 1][(j - 1,) + index].astype(f32)
            if k < 3:
                gathered[(head,) + at] = value.astype(bf16)
            else:
                owned[:, a : a + n, :] = value

        def loops(index):
            if len(index) == len(left):
                body(*index)
            else:
                pl.loop(0, dims[left[len(index)]])(lambda i: loops(index + (i,)))

        loops(())

    for p in range(len(parts)):
        start_reduce(p, 0)
    vec_sum = all_sum(place, small_sum, vec_buf, send, recv)
    vec_total = next(vec_sum)
    fill(head)

    ended = 0
    for step in REDUCE_PLAN:
        if step < 100:
            start_reduce(step // 10, step % 10)
            continue
        end_reduce(step // 10 % 10, step % 10)
        ended += 1
        if vec_total is None and ended in (12, 18):
            vec_total = next(vec_sum)
    while vec_total is None:
        vec_total = next(vec_sum)
    part_square = jnp.zeros((8, 128), f32)
    for i in range(per):
        piece = owned[i]
        part_square = part_square + jnp.sum((piece * piece).reshape(16, 8, 128), axis=0)
    sq_sum = all_sum(place, part_square, sq_buf, send, recv)
    total = next(sq_sum)
    stores[0].start()
    for i in range(per):
        grad = owned[i]
        gram_left[i] = lax.dot_general(grad, grad, (((1,), (1,)), ((), ())), precision=highest, preferred_element_type=f32)
        turned = jnp.transpose(grad)
        gram_right[i] = jnp.dot(turned, grad, precision=highest, preferred_element_type=f32)
    stores[1].start()
    stores[2].start()
    while total is None:
        total = next(sq_sum)

    grads4 = vec_total[0:4]
    bias_total = vec_total[5:6, 0 : 2 * HEADS]
    square = jnp.sum(total) + jnp.sum(grads4 * grads4) + jnp.sum(bias_total * bias_total)
    grad_norm = jnp.sqrt(jnp.broadcast_to(square, (8, 128)))
    factor = jnp.minimum(1.0, clip_limit / grad_norm)
    loss_out[0, 0] = vec_total[4, 0]
    norm_out[0, 0] = jnp.max(grad_norm)
    small_out[...] = jnp.where(lax.broadcasted_iota(jnp.int32, (8, D), 0) == 6, jnp.max(factor), vec_total)
    for copy in stores:
        copy.wait()
    for copy in outgoing:
        copy.wait_send()


def update_kernel(*refs):
    sources, results, held, made = refs[:15], refs[15:25], refs[25:40], refs[40:50]
    in_sem, out_sem = refs[50:]
    fetches = [pltpu.make_async_copy(a, b, in_sem.at[k]) for k, (a, b) in enumerate(zip(sources, held))]
    for copy in fetches:
        copy.start()
    small, vectors, vector_first, vector_second, var_bias, bias_first, bias_second = held[8:]
    owned, left_root, right_root, gram_left, left, gram_right, right, master = held[:8]
    sends = [pltpu.make_async_copy(a, b, out_sem.at[k]) for k, (a, b) in enumerate(zip(made, results))]
    fetches[8].wait()
    factor = jnp.max(small[6:7, :])
    per = owned.shape[0]
    fetches[0].wait()
    fetches[1].wait()
    grads = [owned[i] * factor for i in range(per)]
    for i in range(per):
        made[0][i] = grads[i]
    sends[0].start()
    shaped = [jnp.dot(left_root[i], grads[i], precision=highest, preferred_element_type=f32) for i in range(per)]
    fetches[2].wait()
    shaped = [jnp.dot(shaped[i], right_root[i], precision=highest, preferred_element_type=f32) for i in range(per)]
    for copy in fetches[3:8]:
        copy.wait()
    for k, (stat, gram) in enumerate(((left, gram_left), (right, gram_right))):
        for i in range(per):
            scaled = jnp.where(factor > 0.0, gram[i] * factor * factor, 0.0)
            made[1 + k][i] = stat_beta * stat[i] + (1.0 - stat_beta) * scaled
        sends[1 + k].start()
    for i in range(per):
        unit = shaped[i] * lax.rsqrt(jnp.sum(shaped[i] * shaped[i]) / (SIDE * SIDE) + root_eps)
        made[3][i] = master[i] - mat_rate * (unit + decay_rate * master[i])
    sends[3].start()

    def adamw(gradient, first, second, old, grad_out, second_out, new_out):
        gradient = gradient * factor
        grad_out[...] = gradient
        first_next = beta_one * first[...] + (1.0 - beta_one) * gradient
        second_next = beta_two * second[...] + (1.0 - beta_two) * gradient * gradient
        ratio = first_next / (1.0 - beta_one**STEP) / (jnp.sqrt(second_next / (1.0 - beta_two**STEP)) + adam_eps)
        second_out[...] = second_next
        new_out[...] = old[...] - vec_rate * (ratio + decay_rate * old[...])

    for copy in fetches[9:]:
        copy.wait()
    adamw(small[0:4], vector_first, vector_second, vectors, *made[4:7])
    adamw(small[5:6, 0 : 2 * HEADS], bias_first, bias_second, var_bias, *made[7:10])
    for copy in sends[4:]:
        copy.start()
    for copy in sends:
        copy.wait()


def update_call(small, owned, gram_left, gram_right, master, left, right, left_root, right_root, *rest):
    hbm = pl.BlockSpec(memory_space=pl.ANY)
    sources = (owned, left_root, right_root, gram_left, left, gram_right, right, master, small, *rest)
    outs = [master] * 4 + [rest[0]] * 3 + [rest[3]] * 3
    return pl.pallas_call(
        update_kernel,
        out_shape=tuple(jax.ShapeDtypeStruct(a.shape, f32) for a in outs),
        in_specs=[hbm] * len(sources),
        out_specs=(hbm,) * len(outs),
        scratch_shapes=[pltpu.VMEM(a.shape, f32) for a in sources]
        + [pltpu.VMEM(a.shape, f32) for a in outs]
        + [pltpu.SemaphoreType.DMA((len(sources),)), pltpu.SemaphoreType.DMA((len(outs),))],
        compiler_params=pltpu.CompilerParams(vmem_limit_bytes=60 * 2**20),
        name="update",
    )(*sources)


def step_call(dims, slots, lengths, bias, master, patches, sizes, times, predict, variates, vectors):
    freq = (10000.0 ** (-np.arange(HEAD_DIM // 2) / (HEAD_DIM // 2))).astype(np.float32)
    freq = jnp.asarray(np.tile(freq[None], (8, 4)))
    per = master.shape[0]
    places = np.stack(np.unravel_index(np.arange(2 * math.prod(dims) * per), (2, *dims, per))).astype(np.int32)
    half = patches.shape[2]
    received, sent = semaphores(dims)
    lanes = -(-2 * math.prod(dims) * per // 128) * 128
    smem = pl.BlockSpec(memory_space=pltpu.SMEM)
    vmem = pl.BlockSpec(memory_space=pltpu.VMEM)
    sems = pltpu.SemaphoreType.DMA
    landing = []
    for axes, _, n in cut_parts(REDUCE_PARTS):
        for k in range(3):
            wide = [dims[i] for i in sorted(axes[k + 1 :])]
            landing.append(pltpu.VMEM((max(dims[axes[k]] - 1, 1), *wide, per, n, SIDE), bf16))
    hbm = pl.BlockSpec(memory_space=pl.ANY)
    sources = (master, patches, sizes, times, predict, variates, vectors, freq, jnp.asarray(group_order(), bf16))
    sources += (slots, jnp.asarray(places), lengths, bias)
    return pl.pallas_call(
        functools.partial(step_kernel, dims),
        out_shape=tuple(
            jax.ShapeDtypeStruct(shape, f32)
            for shape in [(1, 1)] * 3 + [(8, D)] + [(per, SIDE, SIDE)] * 3
        ),
        in_specs=[hbm] * len(sources),
        out_specs=(smem,) * 3 + (vmem,) + (hbm,) * 3,
        scratch_shapes=[pltpu.VMEM(a.shape, a.dtype) for a in sources[:9]]
        + [pltpu.SMEM(a.shape, a.dtype) for a in sources[9:]]
        + [pltpu.VMEM((per, SIDE, SIDE), f32)] * 3
        + [sems((len(sources),)), sems((3,))]
        + [pltpu.VMEM((1, lanes), jnp.int32), pltpu.SMEM((1, lanes), jnp.int32), sems]
        + [pltpu.VMEM(shape, dtype) for shape, dtype in SCRATCH.values()]
        + [
            pltpu.VMEM((per, SIDE, SIDE), bf16),
            pltpu.VMEM((2,) + dims + (per, SIDE, SIDE), bf16),
            pltpu.VMEM(dims + (per, SIDE, SIDE), bf16),
            pltpu.VMEM((half, PMAX), bf16),
            pltpu.VMEM((3, 2, half), jnp.int32),
            pltpu.VMEM((3, 2, half), jnp.int32),
            sum_shape(dims, (8, 128)),
            sum_shape(dims, (8, D)),
            sum_shape(dims, (8, 128)),
            sems,
            sems((sent,)),
            sems((received,)),
            *landing,
        ],
        compiler_params=pltpu.CompilerParams(
            collective_id=0, has_side_effects=True, vmem_limit_bytes=63 * 2**20
        ),
        name="step",
    )(*sources)


def shards(
    dims,
    patches, patch_sizes, sample_lengths, variate_ids, time_ids, predict_mask, block_owner_slot,
    master_blocks, left_stats, right_stats, left_roots, right_roots,
    vectors, vector_first, vector_second, var_bias, bias_first, bias_second,
):
    loss_sum, count, grad_norm, small, owned, gram_left, gram_right = step_call(
        dims, block_owner_slot, sample_lengths, var_bias[0], master_blocks, patches, patch_sizes, time_ids,
        predict_mask, variate_ids, vectors,
    )
    outs = update_call(
        small, owned, gram_left, gram_right, master_blocks, left_stats, right_stats, left_roots, right_roots,
        vectors, vector_first, vector_second, var_bias, bias_first, bias_second,
    )
    return (loss_sum.reshape(()), count.reshape(()), grad_norm.reshape(())) + tuple(outs)


def solution(mesh):
    rep = P()
    dims = tok_dims(mesh.shape["tok"])
    slot = P(("head", "tok"), None, None)
    return jax.shard_map(
        functools.partial(shards, dims),
        mesh=mesh,
        in_specs=(
            P(None, "tok", "head", None), P(None, "tok", "head"), P(None, "tok", None), P(None, "tok", None),
            P(None, "tok", "head"), P(None, "tok", "head"), rep, slot, slot, slot, slot, slot,
            rep, rep, rep, rep, rep, rep,
        ),
        out_specs=(rep, rep, rep, slot, slot, slot, slot, rep, rep, rep, rep, rep, rep),
        check_vma=False,
    )
```

```python
import functools
import itertools
import math

import jax
import jax.numpy as jnp
import numpy as np
from jax import lax
from jax.experimental import pallas as pl
from jax.experimental.pallas import tpu as pltpu
from jax.sharding import PartitionSpec as P

D = 384
FF = 1024
HEADS = 6
HEAD_DIM = 64
PSIZES = 5
PMAX = 128
COMPS = 4
SEQ = 512
SIDE = 128
STEP = 10
HEADCOLS = 3 * COMPS * PMAX
BLOCKS = 159

norm_eps = 1e-06
scale_floor = 0.05
half_log_tau = 0.9189385332046727
clip_limit = 0.02
mat_rate = 0.01
vec_rate = 0.3
decay_rate = 0.01
beta_one = 0.9
beta_two = 0.95
stat_beta = 0.99
root_eps = 1e-06
adam_eps = 1e-08
highest = lax.Precision.HIGHEST
f32 = jnp.float32
bf16 = jnp.bfloat16

GRIDS = ((5, 3), (3, 12), (3, 9), (3, 3), (3, 16), (8, 3))
FIRSTS = (0, 15, 51, 78, 87, 135)
M_IN, M_HEAD, M_QKV, M_OUT, M_GU, M_DOWN = range(6)


def mm(a, b):
    return jnp.dot(a, b, preferred_element_type=f32)


def mm_nt(a, b):
    return lax.dot_general(a, b, (((1,), (1,)), ((), ())), preferred_element_type=f32)


def mm_tn(a, b):
    return lax.dot_general(a, b, (((0,), (0,)), ((), ())), preferred_element_type=f32)


GROUP = 384


def shuffle(pieces, source, lane):
    rows = pieces[0].shape[0]
    source, lane = (jnp.broadcast_to(v, (rows, 128)) for v in (source, lane))
    a, b, c = (jnp.take_along_axis(piece, lane, axis=1) for piece in pieces)
    return jnp.where(source == 0, a, jnp.where(source == 1, b, c))


def sort_columns(pieces):
    lane = lax.broadcasted_iota(jnp.int32, (1, 128), 1)
    result = []
    for kind in range(3):
        column = lane % 32 * 12 + kind * 4 + lane // 32
        result.append(shuffle(pieces, column // 128, column % 128))
    return result


def unsort_columns(pieces):
    result = []
    for piece in range(3):
        column = lax.broadcasted_iota(jnp.int32, (1, 128), 1) + 128 * piece
        entry = column % 12
        result.append(shuffle(pieces, entry // 4, entry % 4 * 32 + column // 12))
    return result


def swap_quarters(parts):
    lane = lax.broadcasted_iota(jnp.int32, (1, 128), 1)
    low, even = lane < 64, lane % 64 < 32
    a, b, c, d = parts
    a, c = jnp.where(low, a, pltpu.roll(c, 64, 1)), jnp.where(low, pltpu.roll(a, 64, 1), c)
    b, d = jnp.where(low, b, pltpu.roll(d, 64, 1)), jnp.where(low, pltpu.roll(b, 64, 1), d)
    a, b = jnp.where(even, a, pltpu.roll(b, 32, 1)), jnp.where(even, pltpu.roll(a, 96, 1), b)
    c, d = jnp.where(even, c, pltpu.roll(d, 32, 1)), jnp.where(even, pltpu.roll(c, 96, 1), d)
    return a, b, c, d


SCRATCH = dict(
    w_in=((640, D), bf16), w_head=((D, HEADCOLS), bf16), w_qkv=((D, 3 * D), bf16), w_out=((D, D), bf16),
    w_gu=((D, 2 * FF), bf16), w_down=((FF, D), bf16), w_headp=((D, HEADCOLS), bf16),
    blocks=((BLOCKS + 1, SIDE, SIDE), bf16),
    x5=((SEQ, 640), bf16), weight=((SEQ, PMAX), f32), flag=((SEQ, 128), f32),
    cos_t=((SEQ, 128), f32), sin_t=((SEQ, 128), f32),
    code_t=((SEQ, SEQ), f32), probs=((HEADS, SEQ, SEQ), f32),
    stream=((SEQ, D), f32), middle=((SEQ, D), f32), last=((SEQ, D), f32), grad=((SEQ, D), f32), inner=((SEQ, D), f32),
    inv_a=((SEQ, 128), f32), inv_b=((SEQ, 128), f32), inv_f=((SEQ, 128), f32),
    normed=((SEQ, D), bf16), na_t=((D, SEQ), bf16), nb_t=((D, SEQ), bf16), nf_t=((D, SEQ), bf16),
    qs=((SEQ, D), bf16), ks=((SEQ, D), bf16), vs=((SEQ, D), bf16), merged=((SEQ, D), bf16), merged_t=((D, SEQ), bf16),
    silu=((SEQ, FF), f32), slope=((SEQ, FF), f32), hidden=((SEQ, FF), bf16),
    params=((SEQ, HEADCOLS), f32), gparams=((SEQ, HEADCOLS), bf16), ggu=((SEQ, 2 * FF), bf16),
    loss_acc=((32, 128), f32), bias_acc=((16, 128), f32), vec_acc=((8, D), f32),
    meta=((8, SEQ), jnp.int32), row_patches=((SEQ, PMAX), bf16),
)


def tile(i, size):
    return pl.ds(pl.multiple_of(i * size, size), size)


MESH = pl.DeviceIdType.MESH


def tok_dims(count):
    return {16: (4, 2, 2), 128: (4, 4, 8)}.get(count, (count, 1, 1))


class Place:
    def __init__(self, dims):
        self.dims = dims
        self.head = lax.axis_index("head")
        tok = lax.axis_index("tok")
        self.tok = tok
        self.strides = (dims[1] * dims[2], dims[2], 1)
        self.at = [lax.rem(lax.div(tok, s), n) for s, n in zip(self.strides, dims)]

    def coordinate(self, axis, step):
        return lax.rem(self.at[axis] + step, self.dims[axis])

    def peer(self, axis, step):
        return (self.head, self.tok + (self.coordinate(axis, step) - self.at[axis]) * self.strides[axis])

    def partner(self):
        return (1 - self.head, self.tok)

    def groups(self):
        result, size = [[None]], 2
        for axis in (1, 2, 0):
            if self.dims[axis] == 1:
                continue
            if size * self.dims[axis] > 8:
                result.append([])
                size = 1
            result[-1].append(axis)
            size *= self.dims[axis]
        return result

    def members(self, group):
        sizes = [2 if axis is None else self.dims[axis] for axis in group]
        mine = 0
        for axis, n in zip(group, sizes):
            mine = mine * n + (self.head if axis is None else self.at[axis])
        others = []
        for steps in itertools.product(*[range(n) for n in sizes]):
            head, tok = self.head, self.tok
            for axis, step in zip(group, steps):
                if axis is None:
                    head = lax.rem(head + step, 2)
                else:
                    tok = tok + (self.coordinate(axis, step) - self.at[axis]) * self.strides[axis]
            if any(steps):
                others.append((head, tok))
        return mine, math.prod(sizes), others

    def greet(self, meanwhile):
        barrier = pltpu.get_barrier_semaphore()
        groups = self.groups()
        others = [other for group in groups for other in self.members(group)[2]]
        joint = [group for group in groups if len(group) > 1]
        singles = {group[0] for group in groups if len(group) == 1} | {a for group in joint for a in group}
        others += [self.peer(a, j) for a in range(3) if a not in singles for j in range(1, self.dims[a])]
        for other in others:
            pl.semaphore_signal(barrier, inc=1, device_id=other, device_id_type=MESH)
        meanwhile()
        pl.semaphore_wait(barrier, len(others))

    def region(self, whole, fixed=None):
        fixed = fixed or {}
        return tuple(slice(None) if a in whole else fixed.get(a, self.at[a]) for a in range(3))


def remote(src, dst, send, recv, device):
    return pltpu.make_async_remote_copy(
        src_ref=src, dst_ref=dst, send_sem=send, recv_sem=recv, device_id=device, device_id_type=MESH
    )


def split_rows(rows, shares):
    units = rows // 16
    edges = [round(units * sum(shares[:i]) / sum(shares)) * 16 for i in range(len(shares) + 1)]
    return [(a, b - a) for a, b in zip(edges, edges[1:])]


class Pool:
    def __init__(self, ref):
        self.ref, self.used = ref, 0

    def __call__(self):
        self.used += 1
        return self.ref.at[self.used - 1]


def all_sum(place, values, buf, send, recv):
    total = values
    for k, group in enumerate(place.groups()):
        mine, size, others = place.members(group)
        buf[k, mine] = total
        copies = [remote(buf.at[k, mine], buf.at[k, mine], send(), recv(), other) for other in others]
        for copy in copies:
            copy.start()
        yield None
        for copy in copies:
            copy.wait()
        total = buf[k, 0]
        for i in range(1, size):
            total = total + buf[k, i]
    yield total


def sum_sizes(dims):
    place = Place.__new__(Place)
    place.dims = dims
    return [math.prod(2 if a is None else dims[a] for a in group) for group in place.groups()]


def sum_shape(dims, shape):
    sizes = sum_sizes(dims)
    return pltpu.VMEM((len(sizes), max(sizes)) + shape, f32)


GATHER_PARTS = (
    ((1, 2, 0), 1), ((0, 1, 2), 1), ((0, 2, 1), 1), ((0, 1, 2), 1), ((0, 1, 2), 1), ((0, 2, 1), 1), ((1, 0, 2), 1), ((2, 0, 1), 1),
)
PREPARE_AFTER = 4
GATHER_PLAN = (
    0, 10, 20, 60, 100, 1, 30, 70, 110, 11, 50, 120, 21, 130, 31, 40, 111, 12, 160, 61, 150, 51, 170, 71,
    121, 22, 140, 41, 131, 32, 141, 42, 151, 52, 101, 2, 122, 171, 72, 112, 161, 62, 172, 132, 142, 102, 152, 162,
)
REDUCE_PARTS = (
    ((0, 1, 2), 1), ((2, 1, 0), 1), ((1, 2, 0), 1), ((2, 1, 0), 1), ((1, 2, 0), 1), ((2, 1, 0), 1), ((0, 2, 1), 1), ((1, 2, 0), 1),
)
REDUCE_PLAN = (
    100, 1, 110, 11, 120, 21, 140, 41, 130, 31, 170, 71, 150, 51, 111, 12, 160, 61, 121, 22, 101, 2, 151, 52,
    112, 13, 122, 23, 102, 3, 141, 42, 131, 32, 161, 62, 171, 72, 152, 53, 132, 33, 142, 43, 113, 153, 162, 63,
    172, 73, 123, 133, 103, 143, 163, 173,
)


def cut_parts(table):
    return [(order, a, n) for (order, _), (a, n) in zip(table, split_rows(SIDE, [s for _, s in table]))]


def semaphores(dims):
    steps = sum(n - 1 for n in dims)
    sums = sum(n - 1 for n in sum_sizes(dims))
    gather = sum(steps + 1 + sum(dims[a] - 1 for a in order[1:]) for order, _ in GATHER_PARTS) + 2 + sums
    reduce = len(REDUCE_PARTS) * (steps + 1) + 2 * sums
    return gather + reduce, max(gather, reduce)


def step_kernel(
    dims, *rest,
):
    sources, rest = rest[:12], rest[12:]
    loss_out, count_out, norm_out, small_out = rest[:4]
    results, rest = rest[4:7], rest[7:]
    held, rest = rest[:12], rest[12:]
    master, patches, sizes, times_in, predict_in, variates_in, vectors, freq, slots, places, lengths, bias = held
    (owned, gram_left, gram_right), rest = rest[:3], rest[3:]
    (fetch_sem, result_sem, holder_row, holder, holder_sem), rest = rest[:5], rest[5:]
    fetches = [pltpu.make_async_copy(a, b, fetch_sem.at[k]) for k, (a, b) in enumerate(zip(sources, held))]
    for copy in fetches:
        copy.start()
    stores = [
        pltpu.make_async_copy(a, b, result_sem.at[k]) for k, (a, b) in enumerate(zip((owned, gram_left, gram_right), results))
    ]
    names = list(SCRATCH)
    s = type("S", (), dict(zip(names, rest)))
    rest = rest[len(names) :]
    mine, gathered, crossed, land_patch, land_ints, own_ints = rest[:6]
    cnt_buf, vec_buf, sq_buf, own_sem, send_pool, recv_pool = rest[6:12]
    send, recv = Pool(send_pool), Pool(recv_pool)
    landing = rest[12:]
    place = Place(dims)
    per = mine.shape[0]
    head = place.head
    lane = lax.broadcasted_iota(jnp.int32, (1, 128), 1)
    first_half = lane % HEAD_DIM < HEAD_DIM // 2
    low_head = lane < HEAD_DIM
    weights = (s.w_in, s.w_head, s.w_qkv, s.w_out, s.w_gu, s.w_down)

    def keep(m, r0, c0, value):
        value = value.astype(bf16)
        cols = GRIDS[m][1]
        for r in range(value.shape[0] // SIDE):
            for c in range(value.shape[1] // SIDE):
                piece = value[r * SIDE : (r + 1) * SIDE, c * SIDE : (c + 1) * SIDE]
                s.blocks[FIRSTS[m] + (r0 + r) * cols + c0 + c] = piece

    half = SEQ // 2
    s.meta[4:8, :] = jnp.zeros((4, SEQ), jnp.int32)

    def local_work():
        for copy in fetches[:6]:
            copy.wait()
        mine[...] = master[...].astype(bf16)
        for k, ref in enumerate((sizes, times_in, predict_in)):
            own_ints[k, :, :] = ref[:, 0, :]
        for h in range(2):

            @pl.when(head == h)
            def _():
                here = slice(h * half, (h + 1) * half)
                s.row_patches[here, :] = patches[h, 0]
                for k, ref in enumerate((sizes, times_in, predict_in)):
                    s.meta[k : k + 1, here] = ref[h]
                s.meta[3:4, :] = variates_in[h]

    place.greet(local_work)
    swaps = [
        remote(patches.at[1 - head, 0], land_patch, send(), recv(), place.partner()),
        remote(own_ints, land_ints, send(), recv(), place.partner()),
    ]
    for copy in swaps:
        copy.start()
    parts = cut_parts(GATHER_PARTS)

    def block(head_index, whole, fixed, a, n):
        return gathered.at[(head_index,) + place.region(whole, fixed) + (slice(None), pl.ds(a, n))]

    arriving, outgoing, cross = {}, list(swaps), []
    own = pltpu.make_async_copy(mine, gathered.at[(head,) + place.region(())], own_sem)
    own.start()

    def start_gather(p, k):
        axes, a, n = parts[p]
        axis, whole = axes[k], axes[:k]
        arriving[p] = []
        for j in range(1, dims[axis]):
            src = mine.at[:, pl.ds(a, n)] if k == 0 else block(head, whole, None, a, n)
            copy = remote(src, block(head, whole, None, a, n), send(), recv(), place.peer(axis, j))
            copy.start()
            arriving[p].append(copy)
        outgoing.extend(arriving[p])

    def end_gather(p, k):
        axes, a, n = parts[p]
        for copy in arriving[p]:
            copy.wait_recv()
        axis, whole = axes[k], axes[:k]
        if k == 0:
            views = [block(head, axes[:1], None, a, n)]
        else:
            views = [
                block(head, whole, {axis: place.coordinate(axis, dims[axis] - j)}, a, n) for j in range(1, dims[axis])
            ]
        for view in views:
            copy = remote(view, view, send(), recv(), place.partner())
            copy.start()
            cross.append(copy)

    first = next(i for i, step in enumerate(GATHER_PLAN) if step >= 100)
    for step in GATHER_PLAN[:first]:
        start_gather(step // 10, step % 10)
    wide_size = jnp.zeros_like(own_ints[0])
    for c in range(PSIZES):
        wide_size = wide_size + jnp.where(own_ints[0] == c, PMAX * 2**c // 2 ** (PSIZES - 1), 0)
    partial = (wide_size * own_ints[2]).astype(f32)
    partial = jnp.sum(partial[:, :128] + partial[:, 128:], axis=0, keepdims=True)
    counting = all_sum(place, jnp.concatenate([partial, jnp.zeros((7, 128), f32)], axis=0), cnt_buf, send, recv)
    counted = next(counting)
    own.wait()
    for copy in swaps:
        copy.wait_recv()
    for h in range(2):

        @pl.when(head == h)
        def _():
            there = slice((1 - h) * half, (2 - h) * half)
            s.row_patches[there, :] = land_patch[...]
            for k in range(3):
                s.meta[k : k + 1, there] = land_ints[k, h : h + 1, :]

    def prepare_holder():
        position = lax.broadcasted_iota(jnp.int32, holder_row.shape, 1)

        def body(b, row):
            return jnp.where(position == slots[b], b, row)

        holder_row[...] = lax.fori_loop(0, BLOCKS, body, jnp.full(holder_row.shape, BLOCKS, jnp.int32), unroll=3)
        copy = pltpu.make_async_copy(holder_row, holder, holder_sem)
        copy.start()
        copy.wait()

    def prepare_tokens():
        for copy in fetches[6:]:
            copy.wait()
        metaf = s.meta[...].astype(f32)
        columns = jnp.transpose(metaf)
        codes, times, flag = columns[:, 0:1], columns[:, 1:2], columns[:, 2:3]
        position = lax.broadcasted_iota(jnp.int32, (1, SEQ), 1)
        ids = jnp.zeros((1, SEQ), f32)
        end = jnp.int32(0)
        for j in range(lengths.shape[2]):
            end = end + lengths[head, 0, j]
            ids = ids + jnp.where(position >= end, 1.0, 0.0)
        variates = metaf[3:4]
        id_columns = jnp.transpose(jnp.concatenate([ids] * 8, axis=0))[:, 0:1]
        var_columns = columns[:, 3:4]
        for c in range(4):
            cs = slice(c * 128, (c + 1) * 128)
            same_sample = id_columns == ids[:, cs]
            same_var = var_columns == variates[:, cs]
            s.code_t[:, cs] = jnp.where(same_sample, jnp.where(same_var, 2.0, 1.0), 0.0)
        s.flag[...] = jnp.broadcast_to(flag, (SEQ, 128))
        angle = times * freq[0:1, :]
        s.cos_t[...] = jnp.cos(angle)
        s.sin_t[...] = jnp.where(first_half, -1.0, 1.0) * jnp.sin(angle)

        wide = s.row_patches[...].astype(f32)
        weight = jnp.zeros((SEQ, PMAX), f32)
        for c in range(PSIZES):
            keep = (codes == float(c)) & (lane < PMAX * 2**c // 2 ** (PSIZES - 1))
            s.x5[:, c * 128 : (c + 1) * 128] = jnp.where(keep, wide, 0.0).astype(bf16)
            weight = jnp.where(keep, 1.0, weight)
        s.weight[...] = jnp.where(flag == 1.0, weight, 0.0)
    ended = 0
    for step in GATHER_PLAN[first:]:
        if step < 100:
            start_gather(step // 10, step % 10)
            continue
        end_gather(step // 10 % 10, step % 10)
        ended += 1
        if counted is None and ended in (4, 8):
            counted = next(counting)
        if ended == PREPARE_AFTER:
            prepare_tokens()
        if ended == PREPARE_AFTER + 3:
            prepare_holder()
    while counted is None:
        counted = next(counting)
    value_count = jnp.sum(counted)
    count_out[0, 0] = value_count
    for copy in cross:
        copy.wait_recv()

    def load(m):
        n_rows, cols = GRIDS[m]

        @pl.loop(0, n_rows)
        def _(r):
            for c in range(cols):
                slot = slots[FIRSTS[m] + r * cols + c]
                where = tuple(places[k, slot] for k in range(5))
                weights[m][tile(r, SIDE), c * SIDE : (c + 1) * SIDE] = gathered[where]

    for m in range(6):
        load(m)

    def turn(v, sine):
        swapped = jnp.where(first_half, pltpu.roll(v, 96, 1), pltpu.roll(v, 32, 1))
        return v * s.cos_t[...] + swapped * sine

    embedded = mm(s.x5[...], s.w_in[...])
    for c in range(3):
        cs = slice(c * 128, (c + 1) * 128)
        s.stream[:, cs] = jnp.where(s.flag[...] == 1.0, vectors[3:4, cs], embedded[:, cs])

    def norm(src, inv_ref, gain, dst_t):
        @pl.loop(0, SEQ // 128)
        def _(i):
            rs = tile(i, 128)
            v = src[rs, :]
            inverse = lax.rsqrt(jnp.sum(v * v, axis=-1, keepdims=True) / D + norm_eps)
            inv_ref[rs, :] = jnp.broadcast_to(inverse, (128, 128))
            s.normed[rs, :] = (v * inverse * gain).astype(bf16)

        dst_t[...] = jnp.transpose(s.normed[...])

    def norm_back(src, inv_ref, row, extra):
        gain = vectors[row : row + 1, :]

        @pl.loop(0, SEQ // 128)
        def _(i):
            rs = tile(i, 128)
            up = s.inner[rs, :]
            inverse = inv_ref[rs, 0:1]
            scaled = src[rs, :] * inverse
            inner = up * gain
            mean = jnp.sum(inner * scaled, axis=-1, keepdims=True) / D
            result = inverse * (inner - scaled * mean)
            s.grad[rs, :] = result if extra is None else result + extra[rs, :]
            s.vec_acc[row : row + 1, :] += jnp.sum(up * scaled, axis=0, keepdims=True)

    s.vec_acc[...] = jnp.zeros_like(s.vec_acc)
    norm(s.stream, s.inv_a, vectors[0:1, :], s.na_t)
    mixed = mm(s.normed[...], s.w_qkv[...])
    for part, dst in ((0, s.qs), (1, s.ks), (2, s.vs)):
        for c in range(3):
            piece = mixed[:, part * D + c * 128 : part * D + (c + 1) * 128]
            if part < 2:
                piece = turn(piece, s.sin_t[...])
            dst[:, c * 128 : (c + 1) * 128] = piece.astype(bf16)

    @pl.loop(0, HEADS // 2)
    def _(p):
        ps = tile(p, 128)
        qp, kp = s.qs[:, ps], s.ks[:, ps]
        vt = jnp.transpose(s.vs[:, ps])
        outs = []
        for hh in range(2):
            mine = low_head if hh == 0 else jnp.logical_not(low_head)
            qm = jnp.where(mine, qp.astype(f32) * HEAD_DIM**-0.5, 0.0).astype(bf16)
            b0 = bias[2 * p + hh]
            b1 = bias[HEADS + 2 * p + hh]
            parts = []
            for c in range(1):
                cs = slice(c * 512, (c + 1) * 512)
                code = s.code_t[:, cs]
                score = mm_nt(kp, qm[cs, :])
                score = jnp.where(code > 0.5, score + jnp.where(code > 1.5, b0, b1), -1e30)
                raised = jnp.exp(score - jnp.max(score, axis=0, keepdims=True))
                prob = raised * (1.0 / jnp.sum(raised, axis=0, keepdims=True))
                s.probs[2 * p + hh, :, cs] = prob
                parts.append(mm(vt[hh * 64 : (hh + 1) * 64, :], prob.astype(bf16)))
            outs.append(jnp.concatenate(parts, axis=1))
        out_t = jnp.concatenate(outs, axis=0).astype(bf16)
        s.merged_t[ps, :] = out_t
        s.merged[:, ps] = jnp.transpose(out_t)

        rs = tile(p, 128)
        wide = []
        for g in range(4):
            at = [g * GROUP + k * 128 for k in range(3)]
            wide.append(sort_columns([s.w_head[rs, a : a + 128].astype(f32) for a in at]))
        for kind in range(3):
            for k, piece in enumerate(swap_quarters([w[kind] for w in wide])):
                at = (4 * kind + k) * 128
                s.w_headp[rs, at : at + 128] = piece.astype(bf16)

    s.middle[...] = s.stream[...] + mm(s.merged[...], s.w_out[...])
    norm(s.middle, s.inv_b, vectors[1:2, :], s.nb_t)

    @pl.loop(0, FF // 1024)
    def _(j):
        js = tile(j, 1024)
        opening = mm(s.normed[...], s.w_gu[:, js])
        up = mm(s.normed[...], s.w_gu[:, tile(j + FF // 1024, 1024)])
        sigma = 1.0 / (1.0 + jnp.exp(-opening))
        silu = opening * sigma
        s.silu[:, js] = silu
        s.slope[:, js] = up * sigma * (1.0 + opening * (1.0 - sigma))
        s.hidden[:, js] = (silu * up).astype(bf16)

    s.last[...] = s.middle[...] + mm(s.hidden[...], s.w_down[...])
    norm(s.last, s.inv_f, vectors[2:3, :], s.nf_t)


    @pl.loop(0, HEADCOLS // 512)
    def _(j):
        js = tile(j, 512)
        s.params[:, js] = mm(s.normed[...], s.w_headp[:, js])

    inv_n = 1.0 / value_count
    s.loss_acc[...] = jnp.zeros_like(s.loss_acc)

    @pl.loop(0, SEQ // 32)
    def _(i):
        rs = tile(i, 32)
        y = s.row_patches[rs, :].astype(f32)
        weight = s.weight[rs, :]
        logits, means, raws = [
            [s.params[rs, (4 * kind + k) * 128 : (4 * kind + k + 1) * 128] for k in range(COMPS)] for kind in range(3)
        ]
        top = jnp.maximum(jnp.maximum(logits[0], logits[1]), jnp.maximum(logits[2], logits[3]))
        shifted = [v - top for v in logits]
        raised = [jnp.exp(v) for v in shifted]
        total = raised[0] + raised[1] + raised[2] + raised[3]
        log_total = jnp.log(total)
        inv_total = 1.0 / total
        terms, zs, inv_widths = [], [], []
        for k in range(COMPS):
            width = jnp.maximum(raws[k], 0.0) + jnp.log1p(jnp.exp(-jnp.abs(raws[k]))) + scale_floor
            inv_width = 1.0 / width
            z = (y - means[k]) * inv_width
            terms.append((shifted[k] - log_total) - 0.5 * z * z - jnp.log(width) - half_log_tau)
            zs.append(z)
            inv_widths.append(inv_width)
        best = jnp.maximum(jnp.maximum(terms[0], terms[1]), jnp.maximum(terms[2], terms[3]))
        lifted = [jnp.exp(t - best) for t in terms]
        lift_total = lifted[0] + lifted[1] + lifted[2] + lifted[3]
        inv_lift = 1.0 / lift_total
        s.loss_acc[...] += jnp.where(weight > 0.0, -(best + jnp.log(lift_total)), 0.0)
        scale = -(weight * inv_n)
        for k in range(COMPS):
            share = lifted[k] * inv_lift
            d_term = scale * share
            ratio = zs[k] * inv_widths[k]
            d_logit = scale * (share - raised[k] * inv_total)
            d_width = d_term * (zs[k] * ratio - inv_widths[k])
            sigma = 1.0 / (1.0 + jnp.exp(-raws[k]))
            for kind, value in ((0, d_logit), (1, d_term * ratio), (2, d_width * sigma)):
                at = (4 * kind + k) * 128
                s.gparams[rs, at : at + 128] = value.astype(bf16)

    for kind in range(3):
        wide = mm(s.nf_t[...], s.gparams[:, kind * 512 : (kind + 1) * 512])
        pieces = swap_quarters([wide[:, k * 128 : (k + 1) * 128] for k in range(4)])
        for g in range(4):
            s.w_head[:, (3 * g + kind) * 128 : (3 * g + kind + 1) * 128] = pieces[g].astype(bf16)

    s.inner[...] = mm_nt(s.gparams[...], s.w_headp[...])
    norm_back(s.last, s.inv_f, 2, None)

    s.normed[...] = s.grad[...].astype(bf16)

    @pl.loop(0, FF // 1024)
    def _(j):
        js = tile(j, 1024)
        keep(M_DOWN, 8 * j, 0, mm_tn(s.hidden[:, js], s.normed[...]))
        up_grad = mm_nt(s.normed[...], s.w_down[js, :])
        s.ggu[:, js] = (up_grad * s.slope[:, js]).astype(bf16)
        s.ggu[:, tile(j + FF // 1024, 1024)] = (up_grad * s.silu[:, js]).astype(bf16)

    @pl.loop(0, 2 * FF // 1024)
    def _(j):
        keep(M_GU, 0, 8 * j, mm(s.nb_t[...], s.ggu[:, tile(j, 1024)]))

    s.inner[...] = mm_nt(s.ggu[...], s.w_gu[...])
    norm_back(s.middle, s.inv_b, 1, s.grad)

    s.normed[...] = s.grad[...].astype(bf16)
    keep(M_OUT, 0, 0, mm(s.merged_t[...], s.normed[...]))
    s.merged[...] = mm_nt(s.normed[...], s.w_out[...]).astype(bf16)
    s.bias_acc[...] = jnp.zeros_like(s.bias_acc)

    @pl.loop(0, HEADS // 2)
    def _(p):
        ps = tile(p, 128)
        qp, kp, vp, dop = s.qs[:, ps], s.ks[:, ps], s.vs[:, ps], s.merged[:, ps]
        kt = jnp.transpose(kp)
        dq, dk, dv = [], [], []
        for hh in range(2):
            mine = low_head if hh == 0 else jnp.logical_not(low_head)
            dom = jnp.where(mine, dop.astype(f32), 0.0).astype(bf16)
            same_sum = jnp.zeros((1, 256), f32)
            all_sum = jnp.zeros((1, 256), f32)
            for c in range(2):
                cs = slice(c * 256, (c + 1) * 256)
                prob = s.probs[2 * p + hh, :, cs]
                d_prob = mm_nt(vp, dom[cs, :])
                d_score = prob * (d_prob - jnp.sum(prob * d_prob, axis=0, keepdims=True))
                same_sum += jnp.sum(jnp.where(s.code_t[:, cs] > 1.5, d_score, 0.0), axis=0, keepdims=True)
                all_sum += jnp.sum(d_score, axis=0, keepdims=True)
                s.ggu[:, hh * SEQ + c * 256 : hh * SEQ + (c + 1) * 256] = (d_score * HEAD_DIM**-0.5).astype(bf16)
            s.bias_acc[pl.ds(2 * p + hh, 1), :] = same_sum[:, :128] + same_sum[:, 128:]
            s.bias_acc[pl.ds(8 + 2 * p + hh, 1), :] = all_sum[:, :128] + all_sum[:, 128:]
            dv.append(mm(s.probs[2 * p + hh].astype(bf16), dop))
            dk.append(mm(s.ggu[:, hh * SEQ : (hh + 1) * SEQ], qp))
            dq.append(mm(kt[hh * 64 : (hh + 1) * 64, :], s.ggu[:, hh * SEQ : (hh + 1) * SEQ]))
        dqs = jnp.transpose(jnp.concatenate(dq, axis=0)).astype(bf16).astype(f32)
        dks = jnp.where(low_head, dk[0], dk[1]).astype(bf16).astype(f32)
        s.gparams[:, ps] = turn(dqs, -s.sin_t[...]).astype(bf16)
        s.gparams[:, tile(p + 3, 128)] = turn(dks, -s.sin_t[...]).astype(bf16)
        s.gparams[:, tile(p + 6, 128)] = jnp.where(low_head, dv[0], dv[1]).astype(bf16)

        rs = tile(p, 128)
        for g in range(4):
            at = [(3 * g + kind) * 128 for kind in range(3)]
            for k, piece in enumerate(unsort_columns([s.w_head[rs, a : a + 128].astype(f32) for a in at])):
                s.blocks[FIRSTS[M_HEAD] + p * 12 + 3 * g + k] = piece.astype(bf16)

    keep(M_QKV, 0, 0, mm(s.na_t[...], s.gparams[:, : 3 * D]))
    s.inner[...] = mm_nt(s.gparams[:, : 3 * D], s.w_qkv[...])
    norm_back(s.stream, s.inv_a, 0, s.grad)
    for c in range(3):
        cs = slice(c * 128, (c + 1) * 128)
        hidden_token = s.flag[...] == 1.0
        s.vec_acc[3:4, cs] = jnp.sum(jnp.where(hidden_token, s.grad[:, cs], 0.0), axis=0, keepdims=True)
        s.normed[:, cs] = jnp.where(hidden_token, 0.0, s.grad[:, cs]).astype(bf16)
    keep(M_IN, 0, 0, mm_tn(s.x5[...], s.normed[...]))

    sums = jnp.sum(s.bias_acc[...], axis=1, keepdims=True)
    sums = jnp.concatenate([sums[0:8], sums[8:16] - sums[0:8]], axis=0)
    entry = lax.broadcasted_iota(jnp.int32, (16, D), 0)
    target = jnp.where(entry < HEADS, entry, jnp.where((entry >= 8) & (entry < 8 + HEADS), entry - 8 + HEADS, -1))
    bias_row = jnp.sum(
        jnp.where(target == lax.broadcasted_iota(jnp.int32, (16, D), 1), sums, 0.0), axis=0, keepdims=True
    )
    row = lax.broadcasted_iota(jnp.int32, (8, D), 0)
    small_sum = jnp.where(row == 4, jnp.sum(s.loss_acc[...]), jnp.where(row == 5, bias_row, s.vec_acc[...]))
    for copy in outgoing + cross:
        copy.wait_send()
    send = Pool(send_pool)
    s.blocks[BLOCKS] = jnp.zeros((SIDE, SIDE), bf16)
    toks = dims[0] * dims[1] * dims[2]

    def fill(h):
        @pl.loop(0, toks)
        def _(t):
            for i in range(per):
                at = (h, t // (dims[1] * dims[2]), t // dims[2] % dims[1], t % dims[2], i)
                gathered[at] = s.blocks[holder[0, (h * toks + t) * per + i]]

    everywhere = (slice(None),) * 3
    parts = cut_parts(REDUCE_PARTS)
    fill(1 - head)
    arriving, outgoing = {}, []

    def start_reduce(p, k):
        axes, a, n = parts[p]
        if k == 0:
            view = everywhere + (slice(None), pl.ds(a, n))
            copies = [remote(gathered.at[(1 - head,) + view], crossed.at[view], send(), recv(), place.partner())]
        else:
            axis, left = axes[k - 1], axes[k:]
            copies = []
            for j in range(1, dims[axis]):
                region = place.region(left, {axis: place.coordinate(axis, j)})
                src = gathered.at[(head,) + region + (slice(None), pl.ds(a, n))]
                copies.append(remote(src, landing[3 * p + k - 1].at[j - 1], send(), recv(), place.peer(axis, j)))
        for copy in copies:
            copy.start()
        arriving[p] = copies
        outgoing.extend(copies)

    def end_reduce(p, k):
        axes, a, n = parts[p]
        left = sorted(axes[k:])
        region = place.region(left)
        for copy in arriving[p]:
            copy.wait_recv()

        def body(*index):
            at = tuple(index[left.index(i)] if i in left else region[i] for i in range(3)) + (slice(None), pl.ds(a, n))
            value = gathered[(head,) + at].astype(f32)
            if k == 0:
                value = value + crossed[at].astype(f32)
            else:
                for j in range(1, dims[axes[k - 1]]):
                    value = value + landing[3 * p + k - 1][(j - 1,) + index].astype(f32)
            if k < 3:
                gathered[(head,) + at] = value.astype(bf16)
            else:
                owned[:, a : a + n, :] = value

        def loops(index):
            if len(index) == len(left):
                body(*index)
            else:
                pl.loop(0, dims[left[len(index)]])(lambda i: loops(index + (i,)))

        loops(())

    for p in range(len(parts)):
        start_reduce(p, 0)
    vec_sum = all_sum(place, small_sum, vec_buf, send, recv)
    vec_total = next(vec_sum)
    fill(head)

    ended = 0
    for step in REDUCE_PLAN:
        if step < 100:
            start_reduce(step // 10, step % 10)
            continue
        end_reduce(step // 10 % 10, step % 10)
        ended += 1
        if vec_total is None and ended in (12, 18):
            vec_total = next(vec_sum)
    while vec_total is None:
        vec_total = next(vec_sum)
    part_square = jnp.zeros((8, 128), f32)
    for i in range(per):
        piece = owned[i]
        part_square = part_square + jnp.sum((piece * piece).reshape(16, 8, 128), axis=0)
    sq_sum = all_sum(place, part_square, sq_buf, send, recv)
    total = next(sq_sum)
    stores[0].start()
    for i in range(per):
        grad = owned[i]
        gram_left[i] = lax.dot_general(grad, grad, (((1,), (1,)), ((), ())), precision=highest, preferred_element_type=f32)
        turned = jnp.transpose(grad)
        gram_right[i] = jnp.dot(turned, grad, precision=highest, preferred_element_type=f32)
    stores[1].start()
    stores[2].start()
    while total is None:
        total = next(sq_sum)

    grads4 = vec_total[0:4]
    bias_total = vec_total[5:6, 0 : 2 * HEADS]
    square = jnp.sum(total) + jnp.sum(grads4 * grads4) + jnp.sum(bias_total * bias_total)
    grad_norm = jnp.sqrt(jnp.broadcast_to(square, (8, 128)))
    factor = jnp.minimum(1.0, clip_limit / grad_norm)
    loss_out[0, 0] = vec_total[4, 0]
    norm_out[0, 0] = jnp.max(grad_norm)
    small_out[...] = jnp.where(lax.broadcasted_iota(jnp.int32, (8, D), 0) == 6, jnp.max(factor), vec_total)
    for copy in stores:
        copy.wait()
    for copy in outgoing:
        copy.wait_send()


def update_kernel(*refs):
    sources, results, held, made = refs[:15], refs[15:25], refs[25:40], refs[40:50]
    in_sem, out_sem = refs[50:]
    fetches = [pltpu.make_async_copy(a, b, in_sem.at[k]) for k, (a, b) in enumerate(zip(sources, held))]
    for copy in fetches:
        copy.start()
    small, vectors, vector_first, vector_second, var_bias, bias_first, bias_second = held[8:]
    owned, left_root, right_root, gram_left, left, gram_right, right, master = held[:8]
    sends = [pltpu.make_async_copy(a, b, out_sem.at[k]) for k, (a, b) in enumerate(zip(made, results))]
    fetches[8].wait()
    factor = jnp.max(small[6:7, :])
    per = owned.shape[0]
    fetches[0].wait()
    fetches[1].wait()
    grads = [owned[i] * factor for i in range(per)]
    for i in range(per):
        made[0][i] = grads[i]
    sends[0].start()
    shaped = [jnp.dot(left_root[i], grads[i], precision=highest, preferred_element_type=f32) for i in range(per)]
    fetches[2].wait()
    shaped = [jnp.dot(shaped[i], right_root[i], precision=highest, preferred_element_type=f32) for i in range(per)]
    for copy in fetches[3:8]:
        copy.wait()
    for k, (stat, gram) in enumerate(((left, gram_left), (right, gram_right))):
        for i in range(per):
            scaled = jnp.where(factor > 0.0, gram[i] * factor * factor, 0.0)
            made[1 + k][i] = stat_beta * stat[i] + (1.0 - stat_beta) * scaled
        sends[1 + k].start()
    for i in range(per):
        unit = shaped[i] * lax.rsqrt(jnp.sum(shaped[i] * shaped[i]) / (SIDE * SIDE) + root_eps)
        made[3][i] = master[i] - mat_rate * (unit + decay_rate * master[i])
    sends[3].start()

    def adamw(gradient, first, second, old, grad_out, second_out, new_out):
        gradient = gradient * factor
        grad_out[...] = gradient
        first_next = beta_one * first[...] + (1.0 - beta_one) * gradient
        second_next = beta_two * second[...] + (1.0 - beta_two) * gradient * gradient
        ratio = first_next / (1.0 - beta_one**STEP) / (jnp.sqrt(second_next / (1.0 - beta_two**STEP)) + adam_eps)
        second_out[...] = second_next
        new_out[...] = old[...] - vec_rate * (ratio + decay_rate * old[...])

    for copy in fetches[9:]:
        copy.wait()
    adamw(small[0:4], vector_first, vector_second, vectors, *made[4:7])
    adamw(small[5:6, 0 : 2 * HEADS], bias_first, bias_second, var_bias, *made[7:10])
    for copy in sends[4:]:
        copy.start()
    for copy in sends:
        copy.wait()


def update_call(small, owned, gram_left, gram_right, master, left, right, left_root, right_root, *rest):
    hbm = pl.BlockSpec(memory_space=pl.ANY)
    sources = (owned, left_root, right_root, gram_left, left, gram_right, right, master, small, *rest)
    outs = [master] * 4 + [rest[0]] * 3 + [rest[3]] * 3
    return pl.pallas_call(
        update_kernel,
        out_shape=tuple(jax.ShapeDtypeStruct(a.shape, f32) for a in outs),
        in_specs=[hbm] * len(sources),
        out_specs=(hbm,) * len(outs),
        scratch_shapes=[pltpu.VMEM(a.shape, f32) for a in sources]
        + [pltpu.VMEM(a.shape, f32) for a in outs]
        + [pltpu.SemaphoreType.DMA((len(sources),)), pltpu.SemaphoreType.DMA((len(outs),))],
        compiler_params=pltpu.CompilerParams(vmem_limit_bytes=60 * 2**20),
        name="update",
    )(*sources)


def step_call(dims, slots, lengths, bias, master, patches, sizes, times, predict, variates, vectors):
    freq = (10000.0 ** (-np.arange(HEAD_DIM // 2) / (HEAD_DIM // 2))).astype(np.float32)
    freq = jnp.asarray(np.tile(freq[None], (8, 4)))
    per = master.shape[0]
    places = np.stack(np.unravel_index(np.arange(2 * math.prod(dims) * per), (2, *dims, per))).astype(np.int32)
    half = patches.shape[2]
    received, sent = semaphores(dims)
    lanes = -(-2 * math.prod(dims) * per // 128) * 128
    smem = pl.BlockSpec(memory_space=pltpu.SMEM)
    vmem = pl.BlockSpec(memory_space=pltpu.VMEM)
    sems = pltpu.SemaphoreType.DMA
    landing = []
    for axes, _, n in cut_parts(REDUCE_PARTS):
        for k in range(3):
            wide = [dims[i] for i in sorted(axes[k + 1 :])]
            landing.append(pltpu.VMEM((max(dims[axes[k]] - 1, 1), *wide, per, n, SIDE), bf16))
    hbm = pl.BlockSpec(memory_space=pl.ANY)
    sources = (master, patches, sizes, times, predict, variates, vectors, freq)
    sources += (slots, jnp.asarray(places), lengths, bias)
    return pl.pallas_call(
        functools.partial(step_kernel, dims),
        out_shape=tuple(
            jax.ShapeDtypeStruct(shape, f32)
            for shape in [(1, 1)] * 3 + [(8, D)] + [(per, SIDE, SIDE)] * 3
        ),
        in_specs=[hbm] * len(sources),
        out_specs=(smem,) * 3 + (vmem,) + (hbm,) * 3,
        scratch_shapes=[pltpu.VMEM(a.shape, a.dtype) for a in sources[:8]]
        + [pltpu.SMEM(a.shape, a.dtype) for a in sources[8:]]
        + [pltpu.VMEM((per, SIDE, SIDE), f32)] * 3
        + [sems((len(sources),)), sems((3,))]
        + [pltpu.VMEM((1, lanes), jnp.int32), pltpu.SMEM((1, lanes), jnp.int32), sems]
        + [pltpu.VMEM(shape, dtype) for shape, dtype in SCRATCH.values()]
        + [
            pltpu.VMEM((per, SIDE, SIDE), bf16),
            pltpu.VMEM((2,) + dims + (per, SIDE, SIDE), bf16),
            pltpu.VMEM(dims + (per, SIDE, SIDE), bf16),
            pltpu.VMEM((half, PMAX), bf16),
            pltpu.VMEM((3, 2, half), jnp.int32),
            pltpu.VMEM((3, 2, half), jnp.int32),
            sum_shape(dims, (8, 128)),
            sum_shape(dims, (8, D)),
            sum_shape(dims, (8, 128)),
            sems,
            sems((sent,)),
            sems((received,)),
            *landing,
        ],
        compiler_params=pltpu.CompilerParams(
            collective_id=0, has_side_effects=True, vmem_limit_bytes=63 * 2**20
        ),
        name="step",
    )(*sources)


def shards(
    dims,
    patches, patch_sizes, sample_lengths, variate_ids, time_ids, predict_mask, block_owner_slot,
    master_blocks, left_stats, right_stats, left_roots, right_roots,
    vectors, vector_first, vector_second, var_bias, bias_first, bias_second,
):
    loss_sum, count, grad_norm, small, owned, gram_left, gram_right = step_call(
        dims, block_owner_slot, sample_lengths, var_bias[0], master_blocks, patches, patch_sizes, time_ids,
        predict_mask, variate_ids, vectors,
    )
    outs = update_call(
        small, owned, gram_left, gram_right, master_blocks, left_stats, right_stats, left_roots, right_roots,
        vectors, vector_first, vector_second, var_bias, bias_first, bias_second,
    )
    return (loss_sum.reshape(()), count.reshape(()), grad_norm.reshape(())) + tuple(outs)


def solution(mesh):
    rep = P()
    dims = tok_dims(mesh.shape["tok"])
    slot = P(("head", "tok"), None, None)
    return jax.shard_map(
        functools.partial(shards, dims),
        mesh=mesh,
        in_specs=(
            P(None, "tok", "head", None), P(None, "tok", "head"), P(None, "tok", None), P(None, "tok", None),
            P(None, "tok", "head"), P(None, "tok", "head"), rep, slot, slot, slot, slot, slot,
            rep, rep, rep, rep, rep, rep,
        ),
        out_specs=(rep, rep, rep, slot, slot, slot, slot, rep, rep, rep, rep, rep, rep),
        check_vma=False,
    )
```
